32 devices in a mesh: layer: 4 (over x, core), row: 8 (over z, y).
Axes of the slice: x: 2, y: 2, z: 4, core: 2. Of those that a mesh axis runs over, the one named last changes fastest.
Arguments:
- density: bfloat16 [5120, 2048], P('row', 'layer'), may hold values from -1 to 1, as said below
- pattern: int32 [80, 32], P('row', 'layer'), may hold values 0 or 1
Outputs:
- purified: float32 [5120, 2048], P('row', 'layer')
The draws below stay inside these ranges and needn't reach their ends.
Inputs may be any that keep to these rules, and one draw needn't show every extreme that they name: `density`: entry (r, o * 64 + c) is P's entry in row r and column ((r // 64 + o - 16) mod 80) * 64 + c.
All inputs are finite; a program needn't handle non-finite values. No bound on the sum of `pattern` on one device may be relied on, other than what follows from the above.
Results may differ from the reference program's by a relative error of at most 0.0065.
Values may be sent and summed in bfloat16 or wider, within the bound.
No kernel may reach another device: no remote copies, remote signals or barrier semaphores. Data moves between devices by JAX's collectives and lax.ppermute only.
A program may use at most 192 MiB of HBM per device.

```python
import jax
import jax.numpy as jnp
from jax import lax

BS = 64
NOFF = 32
HALF = 16
NB = 80


def draw_density(key, part):
    rows_all = NB * BS
    cols_all = NOFF * BS
    key_noise, key_diag = jax.random.split(key, 2)
    noise = jax.random.truncated_normal(key_noise, -4.0, 4.0, (rows_all, cols_all), jnp.float32) * 0.05
    diagonal = jax.random.uniform(key_diag, (rows_all, 1), jnp.float32, 0.3, 0.7)
    row_ids = jnp.arange(rows_all, dtype=jnp.int32)[:, None]
    col_ids = jnp.arange(cols_all, dtype=jnp.int32)[None, :]
    on_diag = (col_ids // BS == NOFF // 2) & (col_ids % BS == row_ids % BS)
    return jnp.where(on_diag, diagonal, noise).astype(jnp.bfloat16)


def plant(drawn, rng, least, top_value):
    longest = drawn.shape.index(max(drawn.shape))
    spots = []
    for shift in (0, 1):
        where = [jax.random.randint(jax.random.fold_in(rng, axis), (), 0, length) for axis, length in enumerate(drawn.shape)]
        where[longest] = (where[longest] + shift) % drawn.shape[longest]
        spots.append(tuple(where))
    return drawn.at[spots[0]].set(least).at[spots[1]].set(top_value)


def setup_inputs(seed: int = 0) -> dict:
    splits = jax.random.split(jax.random.key(seed), 3)
    return {
        "density": draw_density(jax.random.fold_in(splits[2], 71), 0),
        "pattern": plant((jax.random.randint(splits[1], (NB, NOFF), 0, 5) < 4).astype(jnp.int32), jax.random.fold_in(splits[1], 1), 0, 1),
    }


def multiply(left, right):
    doubled = jnp.concatenate([right, right], axis=0)

    def advance(running, offset_idx):
        column_blocks = lax.dynamic_index_in_dim(left, offset_idx, 2, keepdims=False)
        first_row = jnp.mod(offset_idx - HALF, NB).astype(jnp.int32)
        near_rows = lax.dynamic_slice_in_dim(doubled, first_row, NB, 0)
        product = jnp.einsum('ixy,iybz->ixbz', column_blocks.astype(jnp.float32), near_rows.astype(jnp.float32), precision=lax.Precision.HIGHEST)
        padded = jnp.pad(product, ((0, 0), (0, 0), (NOFF, NOFF), (0, 0)))
        moved = lax.dynamic_slice_in_dim(padded, (NOFF - offset_idx + HALF).astype(jnp.int32), NOFF, 2)
        return running + moved, None

    initial = jnp.zeros((NB, BS, NOFF, BS), jnp.float32)
    running, unused = lax.scan(advance, initial, jnp.arange(NOFF, dtype=jnp.int32))
    return running


def reference(density, pattern):
    keep = pattern.astype(jnp.bfloat16)[:, None, :, None]
    blocks = density.reshape(NB, BS, NOFF, BS) * keep
    pattern_f = pattern.astype(jnp.float32)[:, None, :, None]
    square = (multiply(blocks, blocks) * pattern_f).astype(jnp.bfloat16)
    cubic = multiply(square, blocks) * pattern_f
    purified = 3.0 * square.astype(jnp.float32) - 2.0 * cubic
    return purified.reshape(NB * BS, NOFF * BS)
```

```python
import functools

import jax
import jax.numpy as jnp
from jax import lax
from jax.experimental import pallas as pl
from jax.experimental.pallas import tpu as pltpu
from jax.sharding import PartitionSpec as P

VMEM = pl.BlockSpec(memory_space=pltpu.VMEM)
LIMIT = 48 * 1024 * 1024


class Geometry:
    def __init__(self, rows_dev, slab_cols, block_rows, slab_offsets, layers):
        self.rows, self.slab = block_rows, slab_offsets
        self.size = rows_dev // block_rows
        self.layers = layers
        self.offsets = slab_offsets * layers
        self.half = self.offsets // 2
        self.pair = 2 * slab_offsets
        self.reach_low, self.reach_high = self.half, self.half - 1
        self.span = self.even_up(self.pair + block_rows - 1)
        self.inner = self.reach_low + block_rows + self.reach_high

    @staticmethod
    def even_down(n):
        return n // 2 * 2

    @staticmethod
    def even_up(n):
        return (n + 1) // 2 * 2

    def valid(self, t, side):
        lo, hi = 0, self.pair + self.rows - 1
        shift = t - self.pair * side
        lo, hi = max(lo, shift), min(hi, self.offsets + shift)
        if t < 0:
            lo = max(lo, -t + shift)
        if t >= self.rows:
            hi = min(hi, self.offsets - (t - self.rows + 1) + shift)
        return lo, max(lo, hi)

    def message(self, side, step):
        first = step * self.rows
        rows = [
            t
            for t in range(first, first + self.rows)
            if -self.reach_low <= t < self.rows + self.reach_high
        ]
        spans = [self.valid(t, side) for t in rows]
        spans = [s for s in spans if s[1] > s[0]]
        lo = self.even_down(min(s[0] for s in spans))
        hi = self.even_up(max(s[1] for s in spans))
        return rows, lo, hi


def steps_of(side, name):
    sign = -1 if (name[1] == "wide") == (side == 0) else 1
    return sign * (1 if name[0] == "near" else 2)


NAMES = (("near", "wide"), ("near", "thin"), ("far", "wide"), ("far", "thin"))


def message_shape(g, name):
    found = [g.message(side, steps_of(side, name)) for side in (0, 1)]
    return max(len(f[0]) for f in found), max(f[2] - f[1] for f in found)


def expand_pattern(pattern_ref, slab_cols, size):
    rows, cols = pattern_ref.shape
    block = lax.broadcasted_iota(jnp.int32, (cols, slab_cols), 1) // size
    row = lax.broadcasted_iota(jnp.int32, (cols, slab_cols), 0)
    spread = jnp.where(block == row, 1.0, 0.0).astype(jnp.float32)
    return jnp.dot(
        pattern_ref[...].astype(jnp.float32), spread, preferred_element_type=jnp.float32
    )


def mask_kernel(g, density_ref, pattern_ref, out_ref):
    keep = expand_pattern(pattern_ref, density_ref.shape[1], g.size)
    for t in range(g.rows):
        rows = slice(t * g.size, (t + 1) * g.size)
        out_ref[rows, :] = density_ref[rows, :] * keep[t : t + 1, :].astype(jnp.bfloat16)


def place_row(dst_ref, dst_row, dst_lo, src_ref, src_row, height, lo, hi, shift, size, limit):
    first, last = max(lo, shift), min(hi, limit + shift)
    base = dst_lo - lo
    rows = slice(dst_row, dst_row + height)
    if first >= last:
        dst_ref[rows, dst_lo * size : (hi + base) * size] = jnp.zeros(
            (height, (hi - lo) * size), dst_ref.dtype
        )
        return
    value = src_ref[src_row : src_row + height, (first - shift) * size : (last - shift) * size]
    parts = []
    if first > lo:
        parts.append(jnp.zeros((height, (first - lo) * size), dst_ref.dtype))
    parts.append(value)
    if hi > last:
        parts.append(jnp.zeros((height, (hi - last) * size), dst_ref.dtype))
    if len(parts) > 1:
        value = jnp.concatenate(parts, axis=1)
    dst_ref[rows, dst_lo * size : (hi + base) * size] = value


def pack_kernel(g, names, count, layer_ref, *refs):
    slabs, outs, band = refs[:count], refs[count : count + len(names)], refs[-1]
    layer = layer_ref[0]
    side, core = layer // 2, layer % 2
    half = g.size // 2
    cols = g.slab * g.size
    for q, slab in enumerate(slabs):
        place = (layer ^ q) if count == g.layers else (core ^ q)
        start = pl.multiple_of(place * cols, cols)
        for t in range(g.rows):
            src = pl.multiple_of(t * g.size + half * core, half)
            band[t * half : (t + 1) * half, pl.ds(start, cols)] = slab[pl.ds(src, half), :]

    def write(side_value):
        first_block = 0 if count == g.layers else g.pair * side_value
        limit = g.offsets if count == g.layers else g.pair
        for name, out in zip(names, outs):
            step = steps_of(side_value, name)
            rows, lo, hi = g.message(side_value, step)
            width = out.shape[1] // g.size
            for n, t in enumerate(rows):
                own = t - step * g.rows
                shift = t - g.pair * side_value + first_block
                place_row(
                    out, n * half, 0, band, own * half, half, lo, lo + width, shift, g.size, limit
                )
            for n in range(len(rows), out.shape[0] // half):
                out[n * half : (n + 1) * half, :] = jnp.zeros((half, out.shape[1]), out.dtype)

    for side_value in (0, 1):
        pl.when(side == side_value)(functools.partial(write, side_value))


def fill_band(g, layer, slabs, band):
    cols = g.slab * g.size
    for q, slab in enumerate(slabs):
        band[:, pl.ds(pl.multiple_of((layer ^ q) * cols, cols), cols)] = slab[...]


def group_windows(g):
    size = (g.rows + 1) // 2
    found = []
    for first in range(0, g.rows, size):
        count = min(size, g.rows - first)
        lo = g.even_down(first)
        hi = g.even_up(first + count - 1 + g.slab)
        found.append((first, count, first, g.offsets + count - 1, lo, hi - lo))
    return found


def banded_product(g, core, band, left, inner, finish):
    for first, count, inner_first, inner_count, col, cols in group_windows(g):
        inner_pad = g.even_up(inner_count)
        for n in range(count):
            place_row(
                left, n * g.size, 0, band, (first + n) * g.size, g.size, 0, inner_pad, n, g.size, g.offsets
            )
        start = pl.multiple_of((core * g.slab + col) * g.size, 2 * g.size)
        product = jnp.dot(
            left[: count * g.size, : inner_count * g.size],
            inner[
                inner_first * g.size : (inner_first + inner_count) * g.size,
                pl.ds(start, cols * g.size),
            ],
            preferred_element_type=jnp.float32,
        )
        for n in range(count):
            at = (first + n - col) * g.size
            finish(
                first + n,
                product[n * g.size : (n + 1) * g.size, at : at + g.slab * g.size],
            )


def square_kernel(g, layer_ref, pattern_ref, *refs):
    slabs, refs = refs[: g.layers], refs[g.layers :]
    pieces, refs = refs[: 2 * len(NAMES)], refs[2 * len(NAMES) :]
    square_ref, inner, band, left = refs
    layer = layer_ref[0]
    side, core = layer // 2, layer % 2
    half = g.size // 2
    fill_band(g, layer, slabs, band)

    def gather(side_value):
        for t in range(g.rows):
            row = (t + g.reach_low) * g.size
            place_row(
                inner, row, 0, band, t * g.size, g.size, 0, g.span,
                t - g.pair * side_value, g.size, g.offsets,
            )
        for n, name in enumerate(NAMES):
            rows, lo, hi = g.message(side_value, steps_of(side_value, name))
            width = pieces[2 * n].shape[1] // g.size
            for m, t in enumerate(rows):
                row = (t + g.reach_low) * g.size
                block = slice(row, row + g.size)
                if lo > 0:
                    inner[block, : lo * g.size] = jnp.zeros((g.size, lo * g.size), inner.dtype)
                if lo + width < g.span:
                    inner[block, (lo + width) * g.size :] = jnp.zeros(
                        (g.size, (g.span - lo - width) * g.size), inner.dtype
                    )
                for q in range(2):
                    at = pl.multiple_of(row + half * (core ^ q), half)
                    inner[pl.ds(at, half), lo * g.size : (lo + width) * g.size] = pieces[2 * n + q][
                        m * half : (m + 1) * half, :
                    ]

    for side_value in (0, 1):
        pl.when(side == side_value)(functools.partial(gather, side_value))
    keep = expand_pattern(pattern_ref, square_ref.shape[1], g.size)

    def finish(t, value):
        rows = slice(t * g.size, (t + 1) * g.size)
        square_ref[rows, :] = (value * keep[t : t + 1, :]).astype(square_ref.dtype)

    banded_product(g, core, band, left, inner, finish)


def cubic_kernel(g, layer_ref, pattern_ref, *refs):
    slabs, refs = refs[: g.layers], refs[g.layers :]
    inner, out_ref, band, left = refs
    layer = layer_ref[0]
    core = layer % 2
    fill_band(g, layer, slabs, band)
    keep = expand_pattern(pattern_ref, out_ref.shape[1], g.size)

    def finish(t, value):
        rows = slice(t * g.size, (t + 1) * g.size)
        out_ref[rows, :] = 3.0 * slabs[0][rows, :].astype(jnp.float32) - 2.0 * (
            value * keep[t : t + 1, :]
        )

    banded_product(g, core, band, left, inner, finish)


def call(kernel, out_shape, scratch, smem, *args, flops=0):
    specs = [pl.BlockSpec(memory_space=pltpu.SMEM)] * smem + [VMEM] * (len(args) - smem)
    moved = sum(a.size * a.dtype.itemsize for a in args)
    return pl.pallas_call(
        kernel,
        out_shape=out_shape,
        in_specs=specs,
        out_specs=jax.tree.map(lambda _: VMEM, out_shape),
        scratch_shapes=scratch,
        compiler_params=pltpu.CompilerParams(vmem_limit_bytes=LIMIT),
        cost_estimate=pl.CostEstimate(flops=flops, bytes_accessed=moved, transcendentals=0),
    )(*args)


def body(density, pattern):
    layers, ring = lax.axis_size("layer"), lax.axis_size("row")
    g = Geometry(*density.shape, *pattern.shape, layers)
    rows_dev, cols = density.shape
    half_rows = g.size // 2
    layer = lax.axis_index("layer").astype(jnp.int32)
    layer_arg = layer[None]
    bf16 = functools.partial(jax.ShapeDtypeStruct, dtype=jnp.bfloat16)

    def swap(value, bit):
        return lax.ppermute(value, "layer", [(s, s ^ bit) for s in range(layers)])

    def send(value, name):
        pairs = []
        for r in range(ring):
            for l in range(layers):
                to = (r - steps_of(l // 2, name)) % ring
                pairs.append((l * ring + r, l * ring + to))
        return lax.ppermute(value, ("layer", "row"), pairs)

    def shape_of(name):
        rows, width = message_shape(g, name)
        return bf16((rows * half_rows, width * g.size))

    masked = call(functools.partial(mask_kernel, g), bf16((rows_dev, cols)), [], 0, density, pattern)
    across = swap(masked, 2)
    beside = swap(masked, 1)
    thin = [name for name in NAMES if name[1] == "thin"]
    wide = [name for name in NAMES if name[1] == "wide"]
    got = {}
    packed = call(
        functools.partial(pack_kernel, g, thin, 2),
        [shape_of(name) for name in thin],
        [pltpu.VMEM((rows_dev // 2, 2 * cols), jnp.bfloat16)],
        1, layer_arg, masked, beside,
    )
    for name, value in zip(thin, packed):
        got[name] = send(value, name)
    diagonal = swap(across, 1)
    slabs = (masked, beside, across, diagonal)
    packed = call(
        functools.partial(pack_kernel, g, wide, layers),
        [shape_of(name) for name in wide],
        [pltpu.VMEM((rows_dev // 2, layers * cols), jnp.bfloat16)],
        1, layer_arg, *slabs,
    )
    for name, value in zip(wide, packed):
        got[name] = send(value, name)
    pieces = []
    for name in NAMES:
        pieces += [got[name], swap(got[name], 1)]

    windows = group_windows(g)
    flops = sum(2 * w[1] * w[3] * w[5] * g.size**3 for w in windows)
    left = pltpu.VMEM(
        (max(w[1] for w in windows) * g.size, g.even_up(max(w[3] for w in windows)) * g.size), jnp.bfloat16
    )
    band = pltpu.VMEM((rows_dev, layers * cols), jnp.bfloat16)
    square, inner = call(
        functools.partial(square_kernel, g),
        [bf16((rows_dev, cols)), bf16((g.inner * g.size, g.span * g.size))],
        [band, left],
        1, layer_arg, pattern, *slabs, *pieces, flops=flops,
    )
    square_across, square_beside = swap(square, 2), swap(square, 1)
    square_slabs = (square, square_beside, square_across, swap(square_across, 1))
    return call(
        functools.partial(cubic_kernel, g),
        jax.ShapeDtypeStruct((rows_dev, cols), jnp.float32),
        [band, left],
        1, layer_arg, pattern, *square_slabs, inner, flops=flops,
    )


def solution(mesh):
    placed = (P("row", "layer"), P("row", "layer"))
    return jax.shard_map(
        body, mesh=mesh, in_specs=placed, out_specs=P("row", "layer"), check_vma=False
    )
```

```python
import functools

import jax
import jax.numpy as jnp
from jax import lax
from jax.experimental import pallas as pl
from jax.experimental.pallas import tpu as pltpu
from jax.sharding import PartitionSpec as P

VMEM = pl.BlockSpec(memory_space=pltpu.VMEM)
LIMIT = 12 * 1024 * 1024


class Geometry:
    def __init__(self, rows_dev, slab_cols, block_rows, slab_offsets, layers):
        self.rows, self.slab = block_rows, slab_offsets
        self.size = rows_dev // block_rows
        self.layers = layers
        self.offsets = slab_offsets * layers
        self.half = self.offsets // 2
        self.pair = 2 * slab_offsets
        self.reach_low, self.reach_high = self.half, self.half - 1
        self.columns = self.pair + block_rows - 1
        self.span = even_up(self.columns)
        self.far = even_up(max(len(self.reached(step)) for step in (-2, 2)))

    def needed(self, t, side):
        lo, hi = self.pair * side - t, self.pair * side - t + self.columns
        if t < 0:
            lo = max(lo, -t)
        if t >= self.rows:
            hi = min(hi, self.offsets - (t - self.rows + 1))
        lo, hi = max(lo, 0), min(hi, self.offsets)
        return lo, max(lo, hi)

    def reached(self, step):
        first = step * self.rows
        return [
            t
            for t in range(first, first + self.rows)
            if -self.reach_low <= t < self.rows + self.reach_high
        ]

    def inner_rows(self, side, part):
        if part == "early":
            return sorted(list(range(self.rows)) + self.reached(step_of(side, NEAR_THIN)))
        rows = []
        for name in ([NEAR_WIDE, FAR_WIDE] if part == "late" else [FAR_THIN]):
            reached = self.reached(step_of(side, name))
            rows += reached + [None] * (0 if name[0] == "near" else self.far - len(reached))
        return rows

    def inner_count(self, part):
        return len(self.inner_rows(0, part))

    def group(self, name):
        first = even_up(2 * self.rows // 5)
        count = first if name == "A" else self.rows - first
        return count, even_up(count - 1 + self.slab)

    def first(self, side, name):
        return 0 if (side == 0) == (name == "A") else self.rows - self.group(name)[0]

    def layout(self, side, name):
        step = step_of(side, name)
        found = []
        for t in self.reached(step):
            lo, hi = self.needed(t, side)
            lo, hi = max(lo, self.pair * side), min(hi, self.pair * (side + 1))
            if hi > lo:
                found.append((even_up(hi) - even_down(lo), t, even_down(lo), even_up(hi)))
        found.sort(reverse=True)
        slots = (len(found) + 1) // 2
        used = [0] * slots
        places = {}
        for n, (width, t, lo, hi) in enumerate(found):
            slot = n if n < slots else 2 * slots - 1 - n
            places[t] = (slot, used[slot], lo, hi)
            used[slot] += width
        return places, slots, max(used)


def even_down(n):
    return n // 2 * 2


def even_up(n):
    return (n + 1) // 2 * 2


def step_of(side, name):
    sign = 1 if (name[1] == "thin") == (side == 0) else -1
    return sign * (1 if name[0] == "near" else 2)


NEAR_WIDE, NEAR_THIN = ("near", "wide"), ("near", "thin")
FAR_WIDE, FAR_THIN = ("far", "wide"), ("far", "thin")


def message_shape(g, name):
    layouts = [g.layout(side, name) for side in (0, 1)]
    rows, cols = max(f[1] for f in layouts) * g.size // 2, max(f[2] for f in layouts) * g.size
    if name == FAR_WIDE:
        return rows + g.far * g.size, g.slab * g.size
    return (2 * rows, cols) if name == FAR_THIN else (rows, cols)


def expand_pattern(pattern_ref, slab_cols, size):
    offsets = pattern_ref.shape[0]
    block = lax.broadcasted_iota(jnp.int32, (offsets, slab_cols), 1) // size
    row = lax.broadcasted_iota(jnp.int32, (offsets, slab_cols), 0)
    spread = jnp.where(block == row, 1.0, 0.0).astype(jnp.float32)
    return lax.dot_general(
        pattern_ref[...].astype(jnp.float32), spread, (((0,), (0,)), ((), ())),
        preferred_element_type=jnp.float32,
    )


def cross_rows(g, side):
    rows = [t - step_of(side, FAR_WIDE) * g.rows for t in g.reached(step_of(side, FAR_WIDE))]
    count = g.far
    return min(rows[0], g.rows - count), count


def mask_kernel(g, density_ref, pattern_ref, out_ref):
    keep = expand_pattern(pattern_ref, density_ref.shape[1], g.size)
    for t in range(g.rows):
        rows = slice(t * g.size, (t + 1) * g.size)
        out_ref[rows, :] = density_ref[rows, :] * keep[t : t + 1, :].astype(jnp.bfloat16)


def place_row(dst_ref, dst_row, dst_lo, src_ref, src_row, height, lo, hi, shift, size, limit):
    first, last = max(lo, shift), min(hi, limit + shift)
    base = dst_lo - lo
    rows = slice(dst_row, dst_row + height)
    if first >= last:
        dst_ref[rows, dst_lo * size : (hi + base) * size] = jnp.zeros(
            (height, (hi - lo) * size), dst_ref.dtype
        )
        return
    value = src_ref[src_row : src_row + height, (first - shift) * size : (last - shift) * size]
    parts = []
    if first > lo:
        parts.append(jnp.zeros((height, (first - lo) * size), dst_ref.dtype))
    parts.append(value)
    if hi > last:
        parts.append(jnp.zeros((height, (hi - last) * size), dst_ref.dtype))
    if len(parts) > 1:
        value = jnp.concatenate(parts, axis=1)
    dst_ref[rows, dst_lo * size : (hi + base) * size] = value


def pack(g, side, name, source, row_of, lead, height, out):
    places, slots, _ = g.layout(side, name)
    filled = [0] * slots
    for t, (slot, col, lo, hi) in places.items():
        out[slot * height : (slot + 1) * height, col * g.size : (col + hi - lo) * g.size] = source[
            pl.ds(row_of(t - step_of(side, name) * g.rows), height), (lo - lead) * g.size : (hi - lead) * g.size
        ]
        filled[slot] = max(filled[slot], col + hi - lo)
    for slot, count in enumerate(filled):
        if count * g.size < out.shape[1]:
            out[slot * height : (slot + 1) * height, count * g.size :] = jnp.zeros(
                (height, out.shape[1] - count * g.size), out.dtype
            )
    if slots * height < out.shape[0] and name != FAR_WIDE:
        out[slots * height :, :] = jnp.zeros((out.shape[0] - slots * height, out.shape[1]), out.dtype)


def fill_near(g, core, slabs, near):
    half, cols = g.size // 2, g.slab * g.size
    for q, slab in enumerate(slabs):
        start = pl.multiple_of((core ^ q) * cols, cols)
        for t in range(g.rows):
            src = pl.multiple_of(t * g.size + half * core, half)
            near[t * half : (t + 1) * half, pl.ds(start, cols)] = slab[pl.ds(src, half), :]


def pack_far_kernel(g, layer_ref, own_ref, beside_ref, other_ref, message, near):
    side, core = layer_ref[0] // 2, layer_ref[0] % 2
    half = g.size // 2
    fill_near(g, core, (own_ref, beside_ref), near)

    def fill(side):
        pack(g, side, FAR_WIDE, near, lambda row: row * half, side * g.pair, half, message)
        first, count = cross_rows(g, side)
        message[message.shape[0] - count * g.size :, :] = other_ref[first * g.size : (first + count) * g.size, :]

    for value in (0, 1):
        pl.when(side == value)(functools.partial(fill, value))


def relay_kernel(g, device_ref, own_ref, relayed_ref, after_ref, out_ref):
    side, row = device_ref[0] // 2, device_ref[1]
    pick((row % 2) == side, own_ref, relayed_ref, out_ref)


def pass_kernel(in_ref, *refs):
    refs[-1][...] = in_ref[...]


def pass_far_kernel(g, layer_ref, in_ref, after_ref, out_ref, message):
    out_ref[...] = in_ref[...]

    def fill(side):
        first, count = cross_rows(g, side)
        start = in_ref.shape[0] - (count + first) * g.size
        lead = (1 - side) * (g.offsets - g.slab)
        pack(g, 1 - side, FAR_THIN, in_ref, lambda row: start + row * g.size, lead, g.size, message)

    for value in (0, 1):
        pl.when(layer_ref[0] // 2 == value)(functools.partial(fill, value))


def fill_pair(g, core, slabs, pair):
    cols = g.slab * g.size
    for q, slab in enumerate(slabs):
        pair[:, pl.ds(pl.multiple_of((core ^ q) * cols, cols), cols)] = slab[...]


def place_parts(g, dst, at, height, t, side, parts):
    shift = t - g.pair * side
    values, done = [], 0
    for lo, hi, load in parts:
        lo, hi = max(lo, done - shift), min(hi, g.span - shift)
        if lo >= hi:
            continue
        if lo + shift > done:
            values.append(jnp.zeros((height, (lo + shift - done) * g.size), dst.dtype))
        values.append(load(lo, hi))
        done = hi + shift
    if done < g.span:
        values.append(jnp.zeros((height, (g.span - done) * g.size), dst.dtype))
    dst[pl.ds(at, height), :] = jnp.concatenate(values, axis=1) if len(values) > 1 else values[0]


def left_rows(g, dst, inner_rows, rows, band, band_first, lead, limit):
    runs = []
    for k, t in enumerate(inner_rows):
        offset = None if t is None else t - k
        if runs and runs[-1][0] == offset:
            runs[-1][2] = k + 1
        else:
            runs.append([offset, k, k + 1])
    for n, i in enumerate(rows):
        for offset, lo, hi in runs:
            shift = hi if offset is None else i - g.reach_low - offset + lead
            place_row(
                dst, n * g.size, lo, band, (band_first + n) * g.size, g.size, lo, hi, shift, g.size, limit
            )


def window_of(g, core, inner, col, cols):
    start = pl.multiple_of((core * g.slab + col) * g.size, 2 * g.size)
    return inner[:, pl.ds(start, cols * g.size)]


def dot(left, right):
    return jnp.dot(left, right, preferred_element_type=jnp.float32)


def own_columns(g, product, n):
    return product[n * g.size : (n + 1) * g.size, n * g.size : (n + g.slab) * g.size]


def by_side(side, values):
    return jnp.where(side == 0, values[0], values[1])


def group_first(g, side, name):
    return by_side(side, [g.first(value, name) for value in (0, 1)])


def message_part(g, side, name, t, piece, height):
    places, _, _ = g.layout(side, name)
    if t not in places:
        return []
    slot, col, lo, hi = places[t]
    rows = slice(slot * height, (slot + 1) * height)
    return [(lo, hi, lambda a, b: piece[rows, (col + a - lo) * g.size : (col + b - lo) * g.size])]


def pair_part(g, pair_index, ref, row, height):
    base = g.pair * pair_index
    return (
        base,
        base + g.pair,
        lambda a, b: ref[pl.ds(row, height), (a - base) * g.size : (b - base) * g.size],
    )


def pick(condition, first, second, out):
    pl.when(condition)(lambda: out.__setitem__(..., first[...]))
    pl.when(jnp.logical_not(condition))(lambda: out.__setitem__(..., second[...]))


def group_rows(g, side, name):
    first = g.first(side, name)
    return range(first, first + g.group(name)[0])


def early_kernel(g, layer_ref, own, beside, *refs):
    others, thins = refs[:2], refs[2:4]
    inner, sum_a, sum_b, late_a, late_b, far_b, band, left_a, left_b, pair = refs[4:]
    layer = layer_ref[0]
    side, core = layer // 2, layer % 2
    cols = g.slab * g.size
    for q, slab in enumerate((own, beside, *others)):
        band[:, pl.ds(pl.multiple_of((layer ^ q) * cols, cols), cols)] = slab[...]
    fill_pair(g, core, thins, pair)

    def gather(side):
        near = g.reached(step_of(side, NEAR_THIN))
        early, late, far = (g.inner_rows(side, part) for part in ("early", "late", "far"))
        for k, t in enumerate(early):
            if 0 <= t < g.rows:
                part = (0, g.offsets, lambda a, b, t=t: band[
                    t * g.size : (t + 1) * g.size, a * g.size : b * g.size
                ])
            else:
                part = pair_part(g, side, pair, (t - near[0]) * g.size, g.size)
            place_parts(g, inner, k * g.size, g.size, t, side, [part])
        for name, lefts in (("A", ((left_a, early), (late_a, late))), ("B", ((left_b, early), (late_b, late), (far_b, far)))):
            rows = group_rows(g, side, name)
            for left, inner_rows in lefts:
                left_rows(g, left, inner_rows, rows, band, rows[0], 0, g.offsets)

    for value in (0, 1):
        pl.when(side == value)(functools.partial(gather, value))
    for name, left, out in (("A", left_a, sum_a), ("B", left_b, sum_b)):
        col, (_, cols) = group_first(g, side, name), g.group(name)
        out[...] = dot(left[...], window_of(g, core, inner, col, cols))


def square_of(g, name, side, core, pattern_ref, total, lefts, inners, keep):
    keep[: g.rows, :] = expand_pattern(pattern_ref, keep.shape[1], g.size)
    first, (_, cols) = group_first(g, side, name), g.group(name)
    product = total[...]
    for left, inner in zip(lefts, inners):
        product += dot(left[...], window_of(g, core, inner, first, cols))
    return lambda n: (own_columns(g, product, n) * keep[pl.ds(first + n, 1), :]).astype(jnp.bfloat16)


def late_kernel(g, layer_ref, pattern_ref, *refs):
    crossed, wides, wide_fars = (refs[2 * n : 2 * n + 2] for n in range(3))
    total, left, square, inner, pair, own_pair, far_pair, keep = refs[6:]
    layer = layer_ref[0]
    side, core = layer // 2, layer % 2
    half = g.size // 2
    fill_pair(g, core, crossed, pair)
    fill_pair(g, core, wides, own_pair)
    tail = far_pair.shape[0]
    fill_pair(g, core, [piece.at[piece.shape[0] - tail :, :] for piece in wide_fars], far_pair)

    def gather(side):
        near = g.reached(step_of(side, NEAR_WIDE))
        for k, t in enumerate(g.inner_rows(side, "late")):
            if t is None:
                inner[k * g.size : (k + 1) * g.size, :] = jnp.zeros((g.size, inner.shape[1]), inner.dtype)
            elif t in near:
                row = (t - near[0]) * g.size
                parts = [pair_part(g, value, own_pair if value == side else pair, row, g.size) for value in (0, 1)]
                place_parts(g, inner, k * g.size, g.size, t, side, parts)
            else:
                row = (t - step_of(side, FAR_WIDE) * g.rows - cross_rows(g, side)[0]) * g.size
                for q, piece in enumerate(wide_fars):
                    at = half * (core ^ q)
                    parts = message_part(g, side, FAR_WIDE, t, piece, half)
                    parts.append(pair_part(g, 1 - side, far_pair, pl.multiple_of(row + at, half), half))
                    parts.sort(key=lambda part: part[0])
                    place_parts(g, inner, pl.multiple_of(k * g.size + at, half), half, t, side, parts)

    for value in (0, 1):
        pl.when(side == value)(functools.partial(gather, value))
    row_of = square_of(g, "A", side, core, pattern_ref, total, [left], [inner], keep)
    for n in range(g.group("A")[0]):
        square[n * g.size : (n + 1) * g.size, :] = row_of(n)


def square_kernel(g, layer_ref, pattern_ref, far, total, left, far_left, late, *refs):
    square, inner, keep = refs
    side, core = layer_ref[0] // 2, layer_ref[0] % 2

    def gather(side):
        for k, t in enumerate(g.inner_rows(side, "far")):
            parts = [] if t is None else message_part(g, side, FAR_THIN, t, far, g.size)
            place_parts(g, inner, k * g.size, g.size, t or 0, side, parts)

    for value in (0, 1):
        pl.when(side == value)(functools.partial(gather, value))
    row_of = square_of(g, "B", side, core, pattern_ref, total, [left, far_left], [late, inner], keep)
    for n in range(g.group("B")[0]):
        square[n * g.size : (n + 1) * g.size, :] = row_of(n)


def band_rows(g, side, name):
    return pl.ds(pl.multiple_of(group_first(g, side, name) * g.size, 2 * g.size), g.group(name)[0] * g.size)


def block_rows(g, t):
    return pl.ds(pl.multiple_of(t * g.size, g.size), g.size)


def early_span(g, part):
    spans = []
    for side in (0, 1):
        rows, pair = (range(g.rows), side) if part == "own" else (group_rows(g, 1 - side, part), 1 - side)
        lo = rows[0] - g.reach_low + g.pair * pair
        hi = rows[-1] - g.reach_low + g.pair * (pair + 1)
        met = [k for k, t in enumerate(g.inner_rows(side, "early")) if lo <= t < hi]
        spans.append((even_down(met[0]), met[-1] + 1))
    count = even_up(max(hi - lo for lo, hi in spans))
    total = len(g.inner_rows(0, "early"))
    return [min(lo, total - count) for lo, _ in spans], count


def cubic_left(g, side, part, rows, band, band_first, lefts):
    pair = side if part == "own" else 1 - side
    starts, count = early_span(g, part)
    early = g.inner_rows(side, "early")[starts[side] : starts[side] + count]
    rest = g.inner_rows(side, "late" if part == "own" else "far")
    for dst, inner_rows in zip(lefts, (early, rest)):
        left_rows(g, dst, inner_rows, rows, band, band_first, g.pair * pair, g.pair)


def cubic_right(g, side, part, inners):
    starts, count = early_span(g, part)
    start = pl.multiple_of(by_side(side, starts) * g.size, 2 * g.size)
    return [inners[0].at[pl.ds(start, count * g.size), :], inners[1]]


def left_scratch(g, part, count):
    sizes = [early_span(g, part)[1], g.inner_count("late" if part == "own" else "far")]
    return [pltpu.VMEM((count * g.size, n * g.size), jnp.bfloat16) for n in sizes]


def cubic_kernel(g, layer_ref, pattern_ref, *refs):
    squares, inners, (out, band, own, keep, *lefts) = refs[:4], refs[4:6], refs[6:]
    layer = layer_ref[0]
    side, core = layer // 2, layer % 2
    cols = g.slab * g.size
    for n, name in enumerate("AB"):
        rows = band_rows(g, side, name)
        own[rows, :] = squares[2 * n][...]
        for q in range(2):
            column = pl.ds(pl.multiple_of((core ^ q) * cols, cols), cols)
            band[rows, column] = squares[2 * n + q][...]
    keep[: g.rows, :] = expand_pattern(pattern_ref, cols, g.size)
    rights = cubic_right(g, side, "own", inners)
    size = (g.rows + 1) // 2
    for n, first in enumerate(range(0, g.rows, size)):
        rows = range(first, min(first + size, g.rows))
        col = even_down(first)
        width = even_up(rows[-1] + g.slab) - col
        used = lefts[2 * n : 2 * n + 2]
        for value in (0, 1):
            pl.when(side == value)(functools.partial(cubic_left, g, value, "own", rows, band, first, used))
        product = sum(
            dot(left[: len(rows) * g.size, :], window_of(g, core, right, col, width))
            for left, right in zip(used, rights)
        )
        for k, t in enumerate(rows):
            at = (t - col) * g.size
            here = slice(t * g.size, (t + 1) * g.size)
            out[here, :] = 3.0 * own[here, :].astype(jnp.float32) - 2.0 * (
                product[k * g.size : (k + 1) * g.size, at : at + cols] * keep[t : t + 1, :]
            )


def other_part(g, layer, name, squares, inners, band, lefts):
    side, core = layer // 2, layer % 2
    cols = g.slab * g.size
    _, width = g.group(name)
    for q in range(2):
        band[:, pl.ds(pl.multiple_of((core ^ q) * cols, cols), cols)] = squares[q][...]
    for value in (0, 1):
        rows = group_rows(g, 1 - value, name)
        pl.when(side == value)(functools.partial(cubic_left, g, value, name, rows, band, 0, lefts))
    first = group_first(g, 1 - side, name)
    rights = cubic_right(g, side, name, inners)
    return first, sum(
        dot(left[...], window_of(g, core, right, first, width)) for left, right in zip(lefts, rights)
    )


def other_kernel(g, layer_ref, pattern_ref, *refs):
    squares, inners, (partial, out, band, keep, *lefts) = refs[:2], refs[2:4], refs[4:]
    keep[: g.rows, :] = expand_pattern(pattern_ref, out.shape[1], g.size)
    first, product = other_part(g, layer_ref[0], "A", squares, inners, band, lefts)
    for n in range(g.group("A")[0]):
        out[n * g.size : (n + 1) * g.size, :] = partial[block_rows(g, first + n), :] - 2.0 * (
            own_columns(g, product, n) * keep[pl.ds(first + n, 1), :]
        )


def last_kernel(g, layer_ref, pattern_ref, *refs):
    squares, inners, (partial, done, out, band, keep, *lefts) = refs[:2], refs[2:4], refs[4:]
    keep[: g.rows, :] = expand_pattern(pattern_ref, out.shape[1], g.size)
    out[band_rows(g, 1 - layer_ref[0] // 2, "A"), :] = done[...]
    first, product = other_part(g, layer_ref[0], "B", squares, inners, band, lefts)
    for n in range(g.group("B")[0]):
        rows = block_rows(g, first + n)
        out[rows, :] = partial[rows, :] - 2.0 * (own_columns(g, product, n) * keep[pl.ds(first + n, 1), :])


def call(kernel, out_shape, scratch, smem, *args, flops=0, after=()):
    specs = [pl.BlockSpec(memory_space=pltpu.SMEM)] * smem + [VMEM] * (len(args) - smem)
    specs += [pl.BlockSpec(memory_space=pl.ANY)] * len(after)
    return pl.pallas_call(
        kernel,
        out_shape=out_shape,
        in_specs=specs,
        out_specs=jax.tree.map(lambda _: VMEM, out_shape),
        scratch_shapes=scratch,
        compiler_params=pltpu.CompilerParams(vmem_limit_bytes=LIMIT),
        cost_estimate=pl.CostEstimate(flops=0, bytes_accessed=0, transcendentals=0),
    )(*args, *after)


def body(density, pattern):
    layers, ring = lax.axis_size("layer"), lax.axis_size("row")
    g = Geometry(*density.shape, *pattern.shape, layers)
    pattern = pattern.T
    rows_dev, cols = density.shape
    layer_arg = lax.axis_index("layer").astype(jnp.int32)[None]
    bf16 = functools.partial(jax.ShapeDtypeStruct, dtype=jnp.bfloat16)
    scratch = lambda *shape: pltpu.VMEM(shape, jnp.bfloat16)

    def swap(value, bit):
        return lax.ppermute(value, "layer", [(s, s ^ bit) for s in range(layers)])

    def send(value, name, keep=lambda layer, row: True):
        pairs = []
        for l in range(layers):
            step = step_of(l // 2, name)
            pairs += [
                (l * ring + r, l * ring + (r - step) % ring) for r in range(ring) if keep(l, r)
            ]
        return lax.ppermute(value, ("layer", "row"), pairs)

    half_rows, slab = rows_dev // 2, (rows_dev, cols)
    cross_shape = (g.far * g.size, cols)
    device_arg = jnp.stack([layer_arg[0], lax.axis_index("row").astype(jnp.int32)])

    def put_after(value, *after):
        return call(pass_kernel, bf16(value.shape), [], 0, value, after=after)

    masked = call(functools.partial(mask_kernel, g), bf16(slab), [], 0, density, pattern)
    thin = send(masked, NEAR_THIN)
    other = swap(masked, 2)
    relayed = send(masked, FAR_WIDE, lambda layer, row: row % 2 != layer // 2)
    beside = swap(masked, 1)
    crossed = swap(thin, 2)
    wide = call(functools.partial(relay_kernel, g), bf16(slab), [], 1, device_arg, masked, relayed, after=(thin,))
    wide = lax.ppermute(wide, "row", [(r, r ^ 1) for r in range(ring)])
    far_wide = call(
        functools.partial(pack_far_kernel, g),
        bf16(message_shape(g, FAR_WIDE)), [scratch(half_rows, 2 * cols)],
        1, layer_arg, masked, beside, other,
    )
    far_wide = send(far_wide, FAR_WIDE)

    early, late, far = (g.inner_count(part) * g.size for part in ("early", "late", "far"))
    (high_a, wide_a), (high_b, wide_b) = (tuple(n * g.size for n in g.group(name)) for name in "AB")
    span = g.span * g.size
    f32 = functools.partial(jax.ShapeDtypeStruct, dtype=jnp.float32)
    keep = pltpu.VMEM((even_up(g.rows + 6), cols), jnp.float32)

    inner_early, sum_a, sum_b, late_a, late_b, far_b = call(
        functools.partial(early_kernel, g),
        [
            bf16((early, span)), f32((high_a, wide_a)), f32((high_b, wide_b)), bf16((high_a, late)),
            bf16((high_b, late)), bf16((high_b, far)),
        ],
        [
            scratch(rows_dev, layers * cols), scratch(high_a, early), scratch(high_b, early),
            scratch(rows_dev, 2 * cols),
        ],
        1, layer_arg, masked, beside, other, swap(other, 1), thin, swap(thin, 1),
    )
    crossed, wide = (put_after(value, sum_a) for value in (crossed, wide))
    far_wide, far_thin = call(
        functools.partial(pass_far_kernel, g),
        [bf16(far_wide.shape), bf16(message_shape(g, FAR_THIN))], [], 1, layer_arg, far_wide, after=(sum_a,),
    )
    far_thin = lax.ppermute(far_thin, "layer", [(1, 2), (2, 1)])
    pieces = sum(([value, swap(value, 1)] for value in (crossed, wide, far_wide)), [])
    square_a, inner_late = call(
        functools.partial(late_kernel, g),
        [bf16((high_a, cols)), bf16((late, span))],
        [scratch(rows_dev, 2 * cols), scratch(rows_dev, 2 * cols), scratch(cross_shape[0], 2 * cols), keep],
        1, layer_arg, pattern, *pieces, sum_a, late_a,
    )
    across_a, beside_a = swap(square_a, 2), swap(square_a, 1)
    square_b, inner_far = call(
        functools.partial(square_kernel, g),
        [bf16((high_b, cols)), bf16((far, span))],
        [keep],
        1, layer_arg, pattern, far_thin, sum_b, late_b, far_b, inner_late,
    )
    across_b, beside_b = swap(square_b, 2), swap(square_b, 1)
    partial = call(
        functools.partial(cubic_kernel, g),
        f32(slab),
        [scratch(rows_dev, 2 * cols), scratch(*slab), keep] + 2 * left_scratch(g, "own", (g.rows + 1) // 2),
        1, layer_arg, pattern, square_a, beside_a, square_b, beside_b, inner_early, inner_late,
    )
    done = call(
        functools.partial(other_kernel, g),
        f32((high_a, cols)), [scratch(high_a, 2 * cols), keep] + left_scratch(g, "A", g.group("A")[0]),
        1, layer_arg, pattern, across_a, swap(across_a, 1), inner_early, inner_far, partial,
    )
    across_b = put_after(across_b, done)
    return call(
        functools.partial(last_kernel, g),
        f32(slab), [scratch(high_b, 2 * cols), keep] + left_scratch(g, "B", g.group("B")[0]),
        1, layer_arg, pattern, across_b, swap(across_b, 1), inner_early, inner_far, partial, done,
    )


def solution(mesh):
    placed = (P("row", "layer"), P("row", "layer"))
    return jax.shard_map(
        body, mesh=mesh, in_specs=placed, out_specs=P("row", "layer"), check_vma=False
    )
```

```python
import functools

import jax
import jax.numpy as jnp
from jax import lax
from jax.experimental import pallas as pl
from jax.experimental.pallas import tpu as pltpu
from jax.sharding import PartitionSpec as P

VMEM = pl.BlockSpec(memory_space=pltpu.VMEM)
HBM = pl.BlockSpec(memory_space=pltpu.HBM)
LIMIT = 12 * 1024 * 1024


class Geometry:
    def __init__(self, rows_dev, slab_cols, block_rows, slab_offsets, layers):
        self.rows, self.slab = block_rows, slab_offsets
        self.size = rows_dev // block_rows
        self.layers = layers
        self.offsets = slab_offsets * layers
        self.half = self.offsets // 2
        self.pair = 2 * slab_offsets
        self.reach_low, self.reach_high = self.half, self.half - 1
        self.columns = self.pair + block_rows - 1
        self.span = even_up(self.columns)
        self.far = even_up(max(len(self.reached(step)) for step in (-2, 2)))

    def needed(self, t, side):
        lo, hi = self.pair * side - t, self.pair * side - t + self.columns
        if t < 0:
            lo = max(lo, -t)
        if t >= self.rows:
            hi = min(hi, self.offsets - (t - self.rows + 1))
        lo, hi = max(lo, 0), min(hi, self.offsets)
        return lo, max(lo, hi)

    def reached(self, step):
        first = step * self.rows
        return [
            t
            for t in range(first, first + self.rows)
            if -self.reach_low <= t < self.rows + self.reach_high
        ]

    def inner_rows(self, side, part):
        if part == "early":
            return sorted(list(range(self.rows)) + self.reached(step_of(side, NEAR_THIN)))
        rows = []
        for name in ([NEAR_WIDE, FAR_WIDE] if part == "late" else [FAR_THIN]):
            reached = self.reached(step_of(side, name))
            rows += reached + [None] * (0 if name[0] == "near" else self.far - len(reached))
        return rows

    def inner_count(self, part):
        return len(self.inner_rows(0, part))

    def group(self, name):
        first = even_up(2 * self.rows // 5)
        count = first if name == "A" else self.rows - first
        return count, even_up(count - 1 + self.slab)

    def first(self, side, name):
        return 0 if (side == 0) == (name == "A") else self.rows - self.group(name)[0]

    def layout(self, side, name):
        step = step_of(side, name)
        found = []
        for t in self.reached(step):
            lo, hi = self.needed(t, side)
            lo, hi = max(lo, self.pair * side), min(hi, self.pair * (side + 1))
            if hi > lo:
                found.append((even_up(hi) - even_down(lo), t, even_down(lo), even_up(hi)))
        found.sort(reverse=True)
        slots = (len(found) + 1) // 2
        used = [0] * slots
        places = {}
        for n, (width, t, lo, hi) in enumerate(found):
            slot = n if n < slots else 2 * slots - 1 - n
            places[t] = (slot, used[slot], lo, hi)
            used[slot] += width
        return places, slots, max(used)


def even_down(n):
    return n // 2 * 2


def even_up(n):
    return (n + 1) // 2 * 2


def step_of(side, name):
    sign = 1 if (name[1] == "thin") == (side == 0) else -1
    return sign * (1 if name[0] == "near" else 2)


NEAR_WIDE, NEAR_THIN = ("near", "wide"), ("near", "thin")
FAR_WIDE, FAR_THIN = ("far", "wide"), ("far", "thin")


def message_shape(g, name):
    layouts = [g.layout(side, name) for side in (0, 1)]
    rows, cols = max(f[1] for f in layouts) * g.size // 2, max(f[2] for f in layouts) * g.size
    if name == FAR_WIDE:
        return rows + g.far * g.size, g.slab * g.size
    return (2 * rows, cols) if name == FAR_THIN else (rows, cols)


def layer_index():
    return lax.axis_index("layer").astype(jnp.int32)


def keep_kernel(g, pattern_ref, keep):
    offsets, cols = pattern_ref.shape[0], keep.shape[1]
    block = lax.broadcasted_iota(jnp.int32, (offsets, cols), 1) // g.size
    row = lax.broadcasted_iota(jnp.int32, (offsets, cols), 0)
    spread = jnp.where(block == row, 1.0, 0.0).astype(jnp.float32)
    keep[: g.rows, :] = lax.dot_general(
        pattern_ref[...].astype(jnp.float32), spread, (((0,), (0,)), ((), ())),
        preferred_element_type=jnp.float32,
    )
    keep[g.rows :, :] = jnp.zeros((keep.shape[0] - g.rows, cols), keep.dtype)


def cross_rows(g, side):
    rows = [t - step_of(side, FAR_WIDE) * g.rows for t in g.reached(step_of(side, FAR_WIDE))]
    count = g.far
    return min(rows[0], g.rows - count), count


def mask_kernel(g, density_ref, keep, out_ref):
    for t in range(g.rows):
        rows = slice(t * g.size, (t + 1) * g.size)
        out_ref[rows, :] = density_ref[rows, :] * keep[t : t + 1, :].astype(jnp.bfloat16)


def place_row(dst_ref, dst_row, dst_lo, src_ref, src_row, height, lo, hi, shift, size, limit):
    first, last = max(lo, shift), min(hi, limit + shift)
    base = dst_lo - lo
    rows = slice(dst_row, dst_row + height)
    if first >= last:
        dst_ref[rows, dst_lo * size : (hi + base) * size] = jnp.zeros(
            (height, (hi - lo) * size), dst_ref.dtype
        )
        return
    value = src_ref[src_row : src_row + height, (first - shift) * size : (last - shift) * size]
    parts = []
    if first > lo:
        parts.append(jnp.zeros((height, (first - lo) * size), dst_ref.dtype))
    parts.append(value)
    if hi > last:
        parts.append(jnp.zeros((height, (hi - last) * size), dst_ref.dtype))
    if len(parts) > 1:
        value = jnp.concatenate(parts, axis=1)
    dst_ref[rows, dst_lo * size : (hi + base) * size] = value


def pack(g, side, name, source, row_of, lead, height, out):
    places, slots, _ = g.layout(side, name)
    filled = [0] * slots
    for t, (slot, col, lo, hi) in places.items():
        out[slot * height : (slot + 1) * height, col * g.size : (col + hi - lo) * g.size] = source[
            pl.ds(row_of(t - step_of(side, name) * g.rows), height), (lo - lead) * g.size : (hi - lead) * g.size
        ]
        filled[slot] = max(filled[slot], col + hi - lo)
    for slot, count in enumerate(filled):
        if count * g.size < out.shape[1]:
            out[slot * height : (slot + 1) * height, count * g.size :] = jnp.zeros(
                (height, out.shape[1] - count * g.size), out.dtype
            )
    if slots * height < out.shape[0] and name != FAR_WIDE:
        out[slots * height :, :] = jnp.zeros((out.shape[0] - slots * height, out.shape[1]), out.dtype)


def fill_near(g, core, slabs, near):
    half, cols = g.size // 2, g.slab * g.size
    for q, slab in enumerate(slabs):
        start = pl.multiple_of((core ^ q) * cols, cols)
        for t in range(g.rows):
            src = pl.multiple_of(t * g.size + half * core, half)
            near[t * half : (t + 1) * half, pl.ds(start, cols)] = slab[pl.ds(src, half), :]


def pack_kernel(g, own_ref, beside_ref, wide, far, near):
    side, core = layer_index() // 2, layer_index() % 2
    half = g.size // 2
    fill_near(g, core, (own_ref, beside_ref), near)

    def fill(side):
        for name, out in ((NEAR_WIDE, wide), (FAR_WIDE, far)):
            pack(g, side, name, near, lambda row: row * half, side * g.pair, half, out)

    for value in (0, 1):
        pl.when(side == value)(functools.partial(fill, value))


def relay_kernel(g, own_ref, relayed_ref, far_ref, other_ref, after_ref, out_ref, message):
    side, row = layer_index() // 2, lax.axis_index("row")
    pick((row % 2) == side, own_ref, relayed_ref, out_ref)
    message[: far_ref.shape[0], :] = far_ref[...]

    def fill(side):
        first, count = cross_rows(g, side)
        message[far_ref.shape[0] :, :] = other_ref[first * g.size : (first + count) * g.size, :]

    for value in (0, 1):
        pl.when(side == value)(functools.partial(fill, value))


def pass_kernel(in_ref, *refs):
    refs[-1][...] = in_ref[...]


def pass_far_kernel(g, in_ref, message):
    def fill(side):
        first, count = cross_rows(g, side)
        start = in_ref.shape[0] - (count + first) * g.size
        lead = (1 - side) * (g.offsets - g.slab)
        pack(g, 1 - side, FAR_THIN, in_ref, lambda row: start + row * g.size, lead, g.size, message)

    for value in (0, 1):
        pl.when(layer_index() // 2 == value)(functools.partial(fill, value))


def fill_pair(g, core, slabs, pair):
    cols = g.slab * g.size
    for q, slab in enumerate(slabs):
        pair[:, pl.ds(pl.multiple_of((core ^ q) * cols, cols), cols)] = slab[...]


def place_parts(g, dst, at, height, t, side, parts):
    shift = t - g.pair * side
    values, done = [], 0
    for lo, hi, load in parts:
        lo, hi = max(lo, done - shift), min(hi, g.span - shift)
        if lo >= hi:
            continue
        if lo + shift > done:
            values.append(jnp.zeros((height, (lo + shift - done) * g.size), dst.dtype))
        values.append(load(lo, hi))
        done = hi + shift
    if done < g.span:
        values.append(jnp.zeros((height, (g.span - done) * g.size), dst.dtype))
    dst[pl.ds(at, height), :] = jnp.concatenate(values, axis=1) if len(values) > 1 else values[0]


def left_rows(g, dst, inner_rows, rows, band, band_first, lead, limit):
    runs = []
    for k, t in enumerate(inner_rows):
        offset = None if t is None else t - k
        if runs and runs[-1][0] == offset:
            runs[-1][2] = k + 1
        else:
            runs.append([offset, k, k + 1])
    for n, i in enumerate(rows):
        for offset, lo, hi in runs:
            shift = hi if offset is None else i - g.reach_low - offset + lead
            place_row(
                dst, n * g.size, lo, band, (band_first + n) * g.size, g.size, lo, hi, shift, g.size, limit
            )


def window_of(g, core, inner, col, cols):
    start = pl.multiple_of((core * g.slab + col) * g.size, 2 * g.size)
    return inner[:, pl.ds(start, cols * g.size)]


def dot(left, right):
    return jnp.dot(left, right, preferred_element_type=jnp.float32)


def own_columns(g, product, n):
    return product[n * g.size : (n + 1) * g.size, n * g.size : (n + g.slab) * g.size]


def by_side(side, values):
    return jnp.where(side == 0, values[0], values[1])


def group_first(g, side, name):
    return by_side(side, [g.first(value, name) for value in (0, 1)])


def message_part(g, side, name, t, piece, height):
    places, _, _ = g.layout(side, name)
    if t not in places:
        return []
    slot, col, lo, hi = places[t]
    rows = slice(slot * height, (slot + 1) * height)
    return [(lo, hi, lambda a, b: piece[rows, (col + a - lo) * g.size : (col + b - lo) * g.size])]


def pair_part(g, pair_index, ref, row, height):
    base = g.pair * pair_index
    return (
        base,
        base + g.pair,
        lambda a, b: ref[pl.ds(row, height), (a - base) * g.size : (b - base) * g.size],
    )


def pick(condition, first, second, out):
    pl.when(condition)(lambda: out.__setitem__(..., first[...]))
    pl.when(jnp.logical_not(condition))(lambda: out.__setitem__(..., second[...]))


def group_rows(g, side, name):
    first = g.first(side, name)
    return range(first, first + g.group(name)[0])


def early_kernel(g, own, beside, *refs):
    others, thins = refs[:2], refs[2:4]
    inner, sum_a, left_b, late_a, late_b, far_b, band, left_a, pair = refs[4:]
    layer = layer_index()
    side, core = layer // 2, layer % 2
    cols = g.slab * g.size
    for q, slab in enumerate((own, beside, *others)):
        band[:, pl.ds(pl.multiple_of((layer ^ q) * cols, cols), cols)] = slab[...]
    fill_pair(g, core, thins, pair)

    def gather(side):
        near = g.reached(step_of(side, NEAR_THIN))
        early, late, far = (g.inner_rows(side, part) for part in ("early", "late", "far"))
        for k, t in enumerate(early):
            if 0 <= t < g.rows:
                part = (0, g.offsets, lambda a, b, t=t: band[
                    t * g.size : (t + 1) * g.size, a * g.size : b * g.size
                ])
            else:
                part = pair_part(g, side, pair, (t - near[0]) * g.size, g.size)
            place_parts(g, inner, k * g.size, g.size, t, side, [part])
        for name, lefts in (("A", ((left_a, early), (late_a, late))), ("B", ((left_b, early), (late_b, late), (far_b, far)))):
            rows = group_rows(g, side, name)
            for left, inner_rows in lefts:
                left_rows(g, left, inner_rows, rows, band, rows[0], 0, g.offsets)

    for value in (0, 1):
        pl.when(side == value)(functools.partial(gather, value))
    col, (_, cols) = group_first(g, side, "A"), g.group("A")
    sum_a[...] = dot(left_a[...], window_of(g, core, inner, col, cols))


def square_of(g, name, side, core, keep, lefts, inners, product=0.0):
    first, (_, cols) = group_first(g, side, name), g.group(name)
    for left, inner in zip(lefts, inners):
        product = product + dot(left[...], window_of(g, core, inner, first, cols))
    return lambda n: (own_columns(g, product, n) * keep[pl.ds(first + n, 1), :]).astype(jnp.bfloat16)


def late_kernel(g, keep, *refs):
    crossed, wides, wide_fars = (refs[2 * n : 2 * n + 2] for n in range(3))
    total, left, square, inner, pair, far_pair = refs[6:]
    layer = layer_index()
    side, core = layer // 2, layer % 2
    half = g.size // 2
    fill_pair(g, core, crossed, pair)
    tail = far_pair.shape[0]
    fill_pair(g, core, [piece.at[piece.shape[0] - tail :, :] for piece in wide_fars], far_pair)

    def gather(side):
        near = g.reached(step_of(side, NEAR_WIDE))
        for k, t in enumerate(g.inner_rows(side, "late")):
            if t is None:
                inner[k * g.size : (k + 1) * g.size, :] = jnp.zeros((g.size, inner.shape[1]), inner.dtype)
                continue
            if t in near:
                name, pieces, source, row = NEAR_WIDE, wides, pair, t - near[0]
            else:
                name, pieces, source = FAR_WIDE, wide_fars, far_pair
                row = t - step_of(side, FAR_WIDE) * g.rows - cross_rows(g, side)[0]
            for q, piece in enumerate(pieces):
                at = half * (core ^ q)
                parts = message_part(g, side, name, t, piece, half)
                parts.append(pair_part(g, 1 - side, source, pl.multiple_of(row * g.size + at, half), half))
                parts.sort(key=lambda part: part[0])
                place_parts(g, inner, pl.multiple_of(k * g.size + at, half), half, t, side, parts)

    for value in (0, 1):
        pl.when(side == value)(functools.partial(gather, value))
    row_of = square_of(g, "A", side, core, keep, [left], [inner], total[...])
    for n in range(g.group("A")[0]):
        square[n * g.size : (n + 1) * g.size, :] = row_of(n)


def square_kernel(g, keep, far, early_left, left, far_left, early, late, *refs):
    square, inner = refs
    side, core = layer_index() // 2, layer_index() % 2

    def gather(side):
        for k, t in enumerate(g.inner_rows(side, "far")):
            parts = [] if t is None else message_part(g, side, FAR_THIN, t, far, g.size)
            place_parts(g, inner, k * g.size, g.size, t or 0, side, parts)

    for value in (0, 1):
        pl.when(side == value)(functools.partial(gather, value))
    row_of = square_of(g, "B", side, core, keep, [early_left, left, far_left], [early, late, inner])
    for n in range(g.group("B")[0]):
        square[n * g.size : (n + 1) * g.size, :] = row_of(n)


def band_rows(g, side, name):
    return pl.ds(pl.multiple_of(group_first(g, side, name) * g.size, 2 * g.size), g.group(name)[0] * g.size)


def block_rows(g, t):
    return pl.ds(pl.multiple_of(t * g.size, g.size), g.size)


def early_span(g, part):
    spans = []
    for side in (0, 1):
        rows, pair = (range(g.rows), side) if part == "own" else (group_rows(g, 1 - side, part), 1 - side)
        lo = rows[0] - g.reach_low + g.pair * pair
        hi = rows[-1] - g.reach_low + g.pair * (pair + 1)
        met = [k for k, t in enumerate(g.inner_rows(side, "early")) if lo <= t < hi]
        spans.append((even_down(met[0]), met[-1] + 1))
    count = even_up(max(hi - lo for lo, hi in spans))
    total = len(g.inner_rows(0, "early"))
    return [min(lo, total - count) for lo, _ in spans], count


def far_span(g, part):
    spans = []
    for side in (0, 1):
        rows = group_rows(g, 1 - side, part)
        lo = rows[0] - g.reach_low + g.pair * (1 - side)
        hi = rows[-1] - g.reach_low + g.pair * (2 - side)
        met = [k for k, t in enumerate(g.inner_rows(side, "far")) if t is not None and lo <= t < hi]
        spans.append((even_down(met[0]), met[-1] + 1) if met else (0, 0))
    count = even_up(max(hi - lo for lo, hi in spans))
    return [min(lo, g.inner_count("far") - count) for lo, _ in spans], count


def cubic_left(g, side, part, rows, band, band_first, lefts):
    pair = side if part == "own" else 1 - side
    starts, count = early_span(g, part)
    lists = [g.inner_rows(side, "early")[starts[side] : starts[side] + count]]
    if part == "own":
        lists.append(g.inner_rows(side, "late"))
    else:
        starts, count = far_span(g, part)
        lists.append(g.inner_rows(side, "far")[starts[side] : starts[side] + count])
    for dst, inner_rows in zip(lefts, lists):
        left_rows(g, dst, inner_rows, rows, band, band_first, g.pair * pair, g.pair)


def cubic_right(g, side, part, inners):
    rights = []
    for inner, span in zip(inners, (early_span, far_span)):
        if span == far_span and part == "own":
            rights.append(inner)
            continue
        starts, count = span(g, part)
        start = pl.multiple_of(by_side(side, starts) * g.size, 2 * g.size)
        rights.append(inner.at[pl.ds(start, count * g.size), :])
    return rights


def left_scratch(g, part, count):
    sizes = [early_span(g, part)[1], g.inner_count("late") if part == "own" else far_span(g, part)[1]]
    return [pltpu.VMEM((count * g.size, n * g.size), jnp.bfloat16) for n in sizes]


def cubic_kernel(g, keep, *refs):
    squares, inners, (out, band, own, *lefts) = refs[:4], refs[4:6], refs[6:]
    layer = layer_index()
    side, core = layer // 2, layer % 2
    cols = g.slab * g.size
    for n, name in enumerate("AB"):
        rows = band_rows(g, side, name)
        own[rows, :] = squares[2 * n][...]
        for q in range(2):
            column = pl.ds(pl.multiple_of((core ^ q) * cols, cols), cols)
            band[rows, column] = squares[2 * n + q][...]
    rights = cubic_right(g, side, "own", inners)
    size = (g.rows + 1) // 2
    for n, first in enumerate(range(0, g.rows, size)):
        rows = range(first, min(first + size, g.rows))
        col = even_down(first)
        width = even_up(rows[-1] + g.slab) - col
        used = lefts[2 * n : 2 * n + 2]
        for value in (0, 1):
            pl.when(side == value)(functools.partial(cubic_left, g, value, "own", rows, band, first, used))
        product = sum(
            dot(left[: len(rows) * g.size, :], window_of(g, core, right, col, width))
            for left, right in zip(used, rights)
        )
        for k, t in enumerate(rows):
            at = (t - col) * g.size
            here = slice(t * g.size, (t + 1) * g.size)
            out[here, :] = 3.0 * own[here, :].astype(jnp.float32) - 2.0 * (
                product[k * g.size : (k + 1) * g.size, at : at + cols] * keep[t : t + 1, :]
            )


def other_part(g, layer, name, squares, inners, band, lefts):
    side, core = layer // 2, layer % 2
    cols = g.slab * g.size
    _, width = g.group(name)
    for q in range(2):
        band[:, pl.ds(pl.multiple_of((core ^ q) * cols, cols), cols)] = squares[q][...]
    for value in (0, 1):
        rows = group_rows(g, 1 - value, name)
        pl.when(side == value)(functools.partial(cubic_left, g, value, name, rows, band, 0, lefts))
    first = group_first(g, 1 - side, name)
    rights = cubic_right(g, side, name, inners)
    return first, sum(
        dot(left[...], window_of(g, core, right, first, width)) for left, right in zip(lefts, rights)
    )


def other_kernel(g, keep, *refs):
    squares, inners, (partial, out, band, *lefts) = refs[:2], refs[2:4], refs[4:]
    first, product = other_part(g, layer_index(), "A", squares, inners, band, lefts)
    for n in range(g.group("A")[0]):
        out[n * g.size : (n + 1) * g.size, :] = partial[block_rows(g, first + n), :] - 2.0 * (
            own_columns(g, product, n) * keep[pl.ds(first + n, 1), :]
        )


def last_kernel(g, keep, *refs):
    squares, inners, (partial, done, out, band, rows, sems, *lefts) = refs[:2], refs[2:4], refs[4:]
    side = layer_index() // 2
    copies = [pltpu.make_async_copy(done, out.at[band_rows(g, 1 - side, "A"), :], sems.at[0])]
    copies[0].start()
    first, product = other_part(g, layer_index(), "B", squares, inners, band, lefts)
    count = g.group("B")[0]
    step = count // 2
    for n in range(count):
        rows[n * g.size : (n + 1) * g.size, :] = partial[block_rows(g, first + n), :] - 2.0 * (
            own_columns(g, product, n) * keep[pl.ds(first + n, 1), :]
        )
        if n + 1 in (step, count):
            begin, end = (0 if n + 1 == step else step) * g.size, (n + 1) * g.size
            to = pl.ds(pl.multiple_of(first * g.size + begin, g.size), end - begin)
            copies.append(pltpu.make_async_copy(rows.at[begin:end, :], out.at[to, :], sems.at[len(copies)]))
            copies[-1].start()
    for copy in copies:
        copy.wait()


def call(kernel, out_shape, scratch, *args, after=(), place=VMEM):
    specs = [VMEM] * len(args) + [pl.BlockSpec(memory_space=pl.ANY)] * len(after)
    return pl.pallas_call(
        kernel,
        out_shape=out_shape,
        in_specs=specs,
        out_specs=jax.tree.map(lambda _: place, out_shape),
        scratch_shapes=scratch,
        compiler_params=pltpu.CompilerParams(vmem_limit_bytes=LIMIT),
        cost_estimate=pl.CostEstimate(flops=0, bytes_accessed=0, transcendentals=0),
    )(*args, *after)


def body(density, pattern):
    layers, ring = lax.axis_size("layer"), lax.axis_size("row")
    g = Geometry(*density.shape, *pattern.shape, layers)
    keep = call(
        functools.partial(keep_kernel, g),
        jax.ShapeDtypeStruct(((g.rows + 7) // 8 * 8, density.shape[1]), jnp.float32), [], pattern.T,
    )
    rows_dev, cols = density.shape
    bf16 = functools.partial(jax.ShapeDtypeStruct, dtype=jnp.bfloat16)
    scratch = lambda *shape: pltpu.VMEM(shape, jnp.bfloat16)

    def swap(value, bit):
        return lax.ppermute(value, "layer", [(s, s ^ bit) for s in range(layers)])

    def send(value, name, keep=lambda layer, row: True):
        pairs = []
        for l in range(layers):
            step = step_of(l // 2, name)
            pairs += [
                (l * ring + r, l * ring + (r - step) % ring) for r in range(ring) if keep(l, r)
            ]
        return lax.ppermute(value, ("layer", "row"), pairs)

    half_rows, slab = rows_dev // 2, (rows_dev, cols)
    cross_shape = (g.far * g.size, cols)

    def put_after(value, *after):
        return call(pass_kernel, bf16(value.shape), [], value, after=after)

    masked = call(functools.partial(mask_kernel, g), bf16(slab), [], density, keep)
    thin = send(masked, NEAR_THIN)
    other = swap(masked, 2)
    beside = swap(masked, 1)
    far_shape = message_shape(g, FAR_WIDE)
    head_shape = (far_shape[0] - cross_shape[0], cols)
    wide, far_wide = call(
        functools.partial(pack_kernel, g),
        [bf16(message_shape(g, NEAR_WIDE)), bf16(head_shape)], [scratch(half_rows, 2 * cols)],
        masked, beside,
    )
    relayed = send(wide, FAR_WIDE, lambda layer, row: row % 2 != layer // 2)
    crossed = swap(thin, 2)
    wide, far_wide = call(
        functools.partial(relay_kernel, g),
        [bf16(wide.shape), bf16(far_shape)], [], wide, relayed, far_wide, other, after=(thin,),
    )
    wide = lax.ppermute(wide, "row", [(r, r ^ 1) for r in range(ring)])
    far_wide = send(far_wide, FAR_WIDE)

    early, late, far = (g.inner_count(part) * g.size for part in ("early", "late", "far"))
    (high_a, wide_a), (high_b, wide_b) = (tuple(n * g.size for n in g.group(name)) for name in "AB")
    span = g.span * g.size
    f32 = functools.partial(jax.ShapeDtypeStruct, dtype=jnp.float32)

    inner_early, sum_a, left_b, late_a, late_b, far_b = call(
        functools.partial(early_kernel, g),
        [
            bf16((early, span)), f32((high_a, wide_a)), bf16((high_b, early)), bf16((high_a, late)),
            bf16((high_b, late)), bf16((high_b, far)),
        ],
        [
            scratch(rows_dev, layers * cols), scratch(high_a, early),
            scratch(rows_dev, 2 * cols),
        ],
        masked, beside, other, swap(other, 1), thin, swap(thin, 1),
    )
    far_thin = call(
        functools.partial(pass_far_kernel, g), bf16(message_shape(g, FAR_THIN)), [], far_wide,
    )
    far_thin = lax.ppermute(far_thin, "layer", [(1, 2), (2, 1)])
    pieces = sum(([value, swap(value, 1)] for value in (crossed, wide, far_wide)), [])
    square_a, inner_late = call(
        functools.partial(late_kernel, g),
        [bf16((high_a, cols)), bf16((late, span))],
        [scratch(rows_dev, 2 * cols), scratch(cross_shape[0], 2 * cols)],
        keep, *pieces, sum_a, late_a,
    )
    across_a, beside_a = swap(square_a, 2), swap(square_a, 1)
    square_b, inner_far = call(
        functools.partial(square_kernel, g),
        [bf16((high_b, cols)), bf16((far, span))],
        [],
        keep, far_thin, left_b, late_b, far_b, inner_early, inner_late,
    )
    across_b, beside_b = swap(square_b, 2), swap(square_b, 1)
    partial = call(
        functools.partial(cubic_kernel, g),
        f32(slab),
        [scratch(rows_dev, 2 * cols), scratch(*slab)] + 2 * left_scratch(g, "own", (g.rows + 1) // 2),
        keep, square_a, beside_a, square_b, beside_b, inner_early, inner_late,
    )
    done = call(
        functools.partial(other_kernel, g),
        f32((high_a, cols)), [scratch(high_a, 2 * cols)] + left_scratch(g, "A", g.group("A")[0]),
        keep, across_a, swap(across_a, 1), inner_early, inner_far, partial,
    )
    across_b = put_after(across_b, done)
    return call(
        functools.partial(last_kernel, g),
        f32(slab),
        [
            scratch(high_b, 2 * cols), pltpu.VMEM((high_b, cols), jnp.float32),
            pltpu.SemaphoreType.DMA((3,)),
        ]
        + left_scratch(g, "B", g.group("B")[0]),
        keep, across_b, swap(across_b, 1), inner_early, inner_far, partial, done,
        place=HBM,
    )


def solution(mesh):
    placed = (P("row", "layer"), P("row", "layer"))
    return jax.shard_map(
        body, mesh=mesh, in_specs=placed, out_specs=P("row", "layer"), check_vma=False
    )
```

```python
import functools

import jax
import jax.numpy as jnp
from jax import lax
from jax.experimental import pallas as pl
from jax.experimental.pallas import tpu as pltpu
from jax.sharding import PartitionSpec as P

VMEM = pl.BlockSpec(memory_space=pltpu.VMEM)
HBM = pl.BlockSpec(memory_space=pltpu.HBM)
LIMIT = 12 * 1024 * 1024


class Geometry:
    def __init__(self, rows_dev, slab_cols, block_rows, slab_offsets, layers):
        self.rows, self.slab = block_rows, slab_offsets
        self.size = rows_dev // block_rows
        self.layers = layers
        self.offsets = slab_offsets * layers
        self.half = self.offsets // 2
        self.pair = 2 * slab_offsets
        self.reach_low, self.reach_high = self.half, self.half - 1
        self.columns = self.pair + block_rows - 1
        self.span = even_up(self.columns)
        self.far = even_up(max(len(self.reached(step)) for step in (-2, 2)))

    def needed(self, t, side):
        lo, hi = self.pair * side - t, self.pair * side - t + self.columns
        if t < 0:
            lo = max(lo, -t)
        if t >= self.rows:
            hi = min(hi, self.offsets - (t - self.rows + 1))
        lo, hi = max(lo, 0), min(hi, self.offsets)
        return lo, max(lo, hi)

    def reached(self, step):
        first = step * self.rows
        return [
            t
            for t in range(first, first + self.rows)
            if -self.reach_low <= t < self.rows + self.reach_high
        ]

    def inner_rows(self, side, part):
        if part == "early":
            return sorted(list(range(self.rows)) + self.reached(step_of(side, NEAR_THIN)))
        rows = []
        for name in ([NEAR_WIDE, FAR_WIDE] if part == "late" else [FAR_THIN]):
            reached = self.reached(step_of(side, name))
            rows += reached + [None] * (0 if name[0] == "near" else self.far - len(reached))
        return rows

    def inner_count(self, part):
        return len(self.inner_rows(0, part))

    def group(self, name):
        first = even_up(2 * self.rows // 5)
        count = first if name == "A" else self.rows - first
        return count, even_up(count - 1 + self.slab)

    def first(self, side, name):
        return 0 if (side == 0) == (name == "A") else self.rows - self.group(name)[0]

    def layout(self, side, name):
        step = step_of(side, name)
        found = []
        for t in self.reached(step):
            lo, hi = self.needed(t, side)
            lo, hi = max(lo, self.pair * side), min(hi, self.pair * (side + 1))
            if hi > lo:
                found.append((even_up(hi) - even_down(lo), t, even_down(lo), even_up(hi)))
        found.sort(reverse=True)
        slots = (len(found) + 1) // 2
        used = [0] * slots
        places = {}
        for n, (width, t, lo, hi) in enumerate(found):
            slot = n if n < slots else 2 * slots - 1 - n
            places[t] = (slot, used[slot], lo, hi)
            used[slot] += width
        return places, slots, max(used)


def even_down(n):
    return n // 2 * 2


def even_up(n):
    return (n + 1) // 2 * 2


def step_of(side, name):
    sign = 1 if (name[1] == "thin") == (side == 0) else -1
    return sign * (1 if name[0] == "near" else 2)


NEAR_WIDE, NEAR_THIN = ("near", "wide"), ("near", "thin")
FAR_WIDE, FAR_THIN = ("far", "wide"), ("far", "thin")


def message_shape(g, name):
    layouts = [g.layout(side, name) for side in (0, 1)]
    rows, cols = max(f[1] for f in layouts) * g.size // 2, max(f[2] for f in layouts) * g.size
    if name == FAR_WIDE:
        return rows + g.far * g.size, g.slab * g.size
    return rows, cols


def layer_index():
    return lax.axis_index("layer").astype(jnp.int32)


def mask_kernel(g, density_ref, pattern_ref, out_ref, keep, density, pattern, sems):
    copies = [
        pltpu.make_async_copy(source, target, sems.at[n])
        for n, (source, target) in enumerate(((pattern_ref, pattern), (density_ref, density)))
    ]
    for copy in copies:
        copy.start()
    copies[0].wait()
    offsets, cols = pattern.shape[0], keep.shape[1]
    block = lax.broadcasted_iota(jnp.int32, (offsets, cols), 1) // g.size
    row = lax.broadcasted_iota(jnp.int32, (offsets, cols), 0)
    spread = jnp.where(block == row, 1.0, 0.0).astype(jnp.float32)
    keep[: g.rows, :] = lax.dot_general(
        pattern[...].astype(jnp.float32), spread, (((0,), (0,)), ((), ())),
        preferred_element_type=jnp.float32,
    )
    keep[g.rows :, :] = jnp.zeros((keep.shape[0] - g.rows, cols), keep.dtype)
    copies[1].wait()
    for t in range(g.rows):
        rows = slice(t * g.size, (t + 1) * g.size)
        out_ref[rows, :] = density[rows, :] * keep[t : t + 1, :].astype(jnp.bfloat16)


def cross_rows(g, side):
    rows = [t - step_of(side, FAR_WIDE) * g.rows for t in g.reached(step_of(side, FAR_WIDE))]
    count = g.far
    return min(rows[0], g.rows - count), count


def place_row(dst_ref, dst_row, dst_lo, src_ref, src_row, height, lo, hi, shift, size, limit):
    first, last = max(lo, shift), min(hi, limit + shift)
    base = dst_lo - lo
    rows = slice(dst_row, dst_row + height)
    if first >= last:
        dst_ref[rows, dst_lo * size : (hi + base) * size] = jnp.zeros(
            (height, (hi - lo) * size), dst_ref.dtype
        )
        return
    value = src_ref[src_row : src_row + height, (first - shift) * size : (last - shift) * size]
    parts = []
    if first > lo:
        parts.append(jnp.zeros((height, (first - lo) * size), dst_ref.dtype))
    parts.append(value)
    if hi > last:
        parts.append(jnp.zeros((height, (hi - last) * size), dst_ref.dtype))
    if len(parts) > 1:
        value = jnp.concatenate(parts, axis=1)
    dst_ref[rows, dst_lo * size : (hi + base) * size] = value


def pack(g, side, name, source, row_of, lead, height, out):
    places, slots, _ = g.layout(side, name)
    filled = [0] * slots
    for t, (slot, col, lo, hi) in places.items():
        out[slot * height : (slot + 1) * height, col * g.size : (col + hi - lo) * g.size] = source[
            pl.ds(row_of(t - step_of(side, name) * g.rows), height), (lo - lead) * g.size : (hi - lead) * g.size
        ]
        filled[slot] = max(filled[slot], col + hi - lo)
    for slot, count in enumerate(filled):
        if count * g.size < out.shape[1]:
            out[slot * height : (slot + 1) * height, count * g.size :] = jnp.zeros(
                (height, out.shape[1] - count * g.size), out.dtype
            )
    if slots * height < out.shape[0] and name != FAR_WIDE:
        out[slots * height :, :] = jnp.zeros((out.shape[0] - slots * height, out.shape[1]), out.dtype)


def fill_near(g, core, slabs, near):
    half, cols = g.size // 2, g.slab * g.size
    for q, slab in enumerate(slabs):
        start = pl.multiple_of((core ^ q) * cols, cols)
        for t in range(g.rows):
            src = pl.multiple_of(t * g.size + half * core, half)
            near[t * half : (t + 1) * half, pl.ds(start, cols)] = slab[pl.ds(src, half), :]


def pack_kernel(g, own_ref, beside_ref, wide, far, near):
    side, core = layer_index() // 2, layer_index() % 2
    half = g.size // 2
    fill_near(g, core, (own_ref, beside_ref), near)

    def fill(side):
        for name, out in ((NEAR_WIDE, wide), (FAR_WIDE, far)):
            pack(g, side, name, near, lambda row: row * half, side * g.pair, half, out)

    for value in (0, 1):
        pl.when(side == value)(functools.partial(fill, value))


def relay_kernel(g, own_ref, relayed_ref, far_ref, other_ref, after_ref, out_ref, message):
    side, row = layer_index() // 2, lax.axis_index("row")
    pick((row % 2) == side, own_ref, relayed_ref, out_ref)
    message[: far_ref.shape[0], :] = far_ref[...]

    def fill(side):
        first, count = cross_rows(g, side)
        message[far_ref.shape[0] :, :] = other_ref[first * g.size : (first + count) * g.size, :]

    for value in (0, 1):
        pl.when(side == value)(functools.partial(fill, value))


def pass_kernel(in_ref, *refs):
    refs[-1][...] = in_ref[...]


def far_thin_kernel(g, far_own, far_beside, after_ref, message):
    side, core = layer_index() // 2, layer_index() % 2
    half = g.size // 2

    def fill(side, source):
        first, count = cross_rows(g, side)
        start = source.shape[0] - (count + first) * g.size
        row_of = lambda row: pl.multiple_of(start + row * g.size + half * core, half)
        pack(g, 1 - side, FAR_THIN, source, row_of, (1 - side) * (g.offsets - g.slab), half, message)

    for value in (0, 1):
        for held, source in ((True, far_own), (False, far_beside)):
            here = jnp.logical_and(side == value, (core == 1 - value) == held)
            pl.when(here)(functools.partial(fill, value, source))


def fill_pair(g, core, slabs, pair):
    cols = g.slab * g.size
    for q, slab in enumerate(slabs):
        pair[:, pl.ds(pl.multiple_of((core ^ q) * cols, cols), cols)] = slab[...]


def place_parts(g, dst, at, height, t, side, parts):
    shift = t - g.pair * side
    values, done = [], 0
    for lo, hi, load in parts:
        lo, hi = max(lo, done - shift), min(hi, g.span - shift)
        if lo >= hi:
            continue
        if lo + shift > done:
            values.append(jnp.zeros((height, (lo + shift - done) * g.size), dst.dtype))
        values.append(load(lo, hi))
        done = hi + shift
    if done < g.span:
        values.append(jnp.zeros((height, (g.span - done) * g.size), dst.dtype))
    dst[pl.ds(at, height), :] = jnp.concatenate(values, axis=1) if len(values) > 1 else values[0]


def left_rows(g, dst, inner_rows, rows, band, band_first, lead, limit):
    runs = []
    for k, t in enumerate(inner_rows):
        offset = None if t is None else t - k
        if runs and runs[-1][0] == offset:
            runs[-1][2] = k + 1
        else:
            runs.append([offset, k, k + 1])
    for n, i in enumerate(rows):
        for offset, lo, hi in runs:
            shift = hi if offset is None else i - g.reach_low - offset + lead
            place_row(
                dst, n * g.size, lo, band, (band_first + n) * g.size, g.size, lo, hi, shift, g.size, limit
            )


def window_of(g, core, inner, col, cols):
    start = pl.multiple_of((core * g.slab + col) * g.size, 2 * g.size)
    return inner[:, pl.ds(start, cols * g.size)]


def dot(left, right):
    return jnp.dot(left, right, preferred_element_type=jnp.float32)


def own_columns(g, product, n):
    return product[n * g.size : (n + 1) * g.size, n * g.size : (n + g.slab) * g.size]


def by_side(side, values):
    return jnp.where(side == 0, values[0], values[1])


def group_first(g, side, name):
    return by_side(side, [g.first(value, name) for value in (0, 1)])


def message_part(g, side, name, t, piece, height):
    places, _, _ = g.layout(side, name)
    if t not in places:
        return []
    slot, col, lo, hi = places[t]
    rows = slice(slot * height, (slot + 1) * height)
    return [(lo, hi, lambda a, b: piece[rows, (col + a - lo) * g.size : (col + b - lo) * g.size])]


def pair_part(g, pair_index, ref, row, height):
    base = g.pair * pair_index
    return (
        base,
        base + g.pair,
        lambda a, b: ref[pl.ds(row, height), (a - base) * g.size : (b - base) * g.size],
    )


def pick(condition, first, second, out):
    pl.when(condition)(lambda: out.__setitem__(..., first[...]))
    pl.when(jnp.logical_not(condition))(lambda: out.__setitem__(..., second[...]))


def group_rows(g, side, name):
    first = g.first(side, name)
    return range(first, first + g.group(name)[0])


def early_kernel(g, own, beside, *refs):
    others, thins = refs[:2], refs[2:4]
    inner, sum_a, left_b, late_a, late_b, far_b, band, left_a, pair = refs[4:]
    layer = layer_index()
    side, core = layer // 2, layer % 2
    cols = g.slab * g.size
    for q, slab in enumerate((own, beside, *others)):
        band[:, pl.ds(pl.multiple_of((layer ^ q) * cols, cols), cols)] = slab[...]
    fill_pair(g, core, thins, pair)

    def gather(side):
        near = g.reached(step_of(side, NEAR_THIN))
        early, late, far = (g.inner_rows(side, part) for part in ("early", "late", "far"))
        for k, t in enumerate(early):
            if 0 <= t < g.rows:
                part = (0, g.offsets, lambda a, b, t=t: band[
                    t * g.size : (t + 1) * g.size, a * g.size : b * g.size
                ])
            else:
                part = pair_part(g, side, pair, (t - near[0]) * g.size, g.size)
            place_parts(g, inner, k * g.size, g.size, t, side, [part])
        for name, lefts in (("A", ((left_a, early), (late_a, late))), ("B", ((left_b, early), (late_b, late), (far_b, far)))):
            rows = group_rows(g, side, name)
            for left, inner_rows in lefts:
                left_rows(g, left, inner_rows, rows, band, rows[0], 0, g.offsets)

    for value in (0, 1):
        pl.when(side == value)(functools.partial(gather, value))
    col, (_, cols) = group_first(g, side, "A"), g.group("A")
    sum_a[...] = dot(left_a[...], window_of(g, core, inner, col, cols))


def square_of(g, name, side, core, keep, lefts, inners, product=0.0):
    first, (_, cols) = group_first(g, side, name), g.group(name)
    for left, inner in zip(lefts, inners):
        product = product + dot(left[...], window_of(g, core, inner, first, cols))
    return lambda n: (own_columns(g, product, n) * keep[pl.ds(first + n, 1), :]).astype(jnp.bfloat16)


def late_kernel(g, keep, *refs):
    crossed, wides, wide_fars = (refs[2 * n : 2 * n + 2] for n in range(3))
    total, left, square, inner, pair, far_pair = refs[6:]
    layer = layer_index()
    side, core = layer // 2, layer % 2
    half = g.size // 2
    fill_pair(g, core, crossed, pair)
    tail = far_pair.shape[0]
    fill_pair(g, core, [piece.at[piece.shape[0] - tail :, :] for piece in wide_fars], far_pair)

    def gather(side):
        near = g.reached(step_of(side, NEAR_WIDE))
        for k, t in enumerate(g.inner_rows(side, "late")):
            if t is None:
                inner[k * g.size : (k + 1) * g.size, :] = jnp.zeros((g.size, inner.shape[1]), inner.dtype)
                continue
            if t in near:
                name, pieces, source, row = NEAR_WIDE, wides, pair, t - near[0]
            else:
                name, pieces, source = FAR_WIDE, wide_fars, far_pair
                row = t - step_of(side, FAR_WIDE) * g.rows - cross_rows(g, side)[0]
            for q, piece in enumerate(pieces):
                at = half * (core ^ q)
                parts = message_part(g, side, name, t, piece, half)
                parts.append(pair_part(g, 1 - side, source, pl.multiple_of(row * g.size + at, half), half))
                parts.sort(key=lambda part: part[0])
                place_parts(g, inner, pl.multiple_of(k * g.size + at, half), half, t, side, parts)

    for value in (0, 1):
        pl.when(side == value)(functools.partial(gather, value))
    row_of = square_of(g, "A", side, core, keep, [left], [inner], total[...])
    for n in range(g.group("A")[0]):
        square[n * g.size : (n + 1) * g.size, :] = row_of(n)


def sum_kernel(g, early_left, late_left, early, late, out):
    side, core = layer_index() // 2, layer_index() % 2
    first, (_, cols) = group_first(g, side, "B"), g.group("B")
    out[...] = dot(early_left[...], window_of(g, core, early, first, cols))
    out[...] += dot(late_left[...], window_of(g, core, late, first, cols))


def square_kernel(g, keep, far, far_beside, total, far_left, *refs):
    square, inner = refs
    side, core = layer_index() // 2, layer_index() % 2
    half = g.size // 2

    def gather(side):
        for k, t in enumerate(g.inner_rows(side, "far")):
            for q, piece in enumerate((far, far_beside)):
                at = pl.multiple_of(k * g.size + half * (core ^ q), half)
                parts = [] if t is None else message_part(g, side, FAR_THIN, t, piece, half)
                place_parts(g, inner, at, half, t or 0, side, parts)

    for value in (0, 1):
        pl.when(side == value)(functools.partial(gather, value))
    row_of = square_of(g, "B", side, core, keep, [far_left], [inner], total[...])
    for n in range(g.group("B")[0]):
        square[n * g.size : (n + 1) * g.size, :] = row_of(n)


def band_rows(g, side, name):
    return pl.ds(pl.multiple_of(group_first(g, side, name) * g.size, 2 * g.size), g.group(name)[0] * g.size)


def block_rows(g, t):
    return pl.ds(pl.multiple_of(t * g.size, g.size), g.size)


def early_span(g, part):
    spans = []
    for side in (0, 1):
        rows, pair = (range(g.rows), side) if part == "own" else (group_rows(g, 1 - side, part), 1 - side)
        lo = rows[0] - g.reach_low + g.pair * pair
        hi = rows[-1] - g.reach_low + g.pair * (pair + 1)
        met = [k for k, t in enumerate(g.inner_rows(side, "early")) if lo <= t < hi]
        spans.append((even_down(met[0]), met[-1] + 1))
    count = even_up(max(hi - lo for lo, hi in spans))
    total = len(g.inner_rows(0, "early"))
    return [min(lo, total - count) for lo, _ in spans], count


def far_span(g, part):
    spans = []
    for side in (0, 1):
        rows = group_rows(g, 1 - side, part)
        lo = rows[0] - g.reach_low + g.pair * (1 - side)
        hi = rows[-1] - g.reach_low + g.pair * (2 - side)
        met = [k for k, t in enumerate(g.inner_rows(side, "far")) if t is not None and lo <= t < hi]
        spans.append((even_down(met[0]), met[-1] + 1) if met else (0, 0))
    count = even_up(max(hi - lo for lo, hi in spans))
    return [min(lo, g.inner_count("far") - count) for lo, _ in spans], count


def cubic_left(g, side, part, rows, band, band_first, lefts):
    pair = side if part == "own" else 1 - side
    starts, count = early_span(g, part)
    lists = [g.inner_rows(side, "early")[starts[side] : starts[side] + count]]
    if part == "own":
        lists.append(g.inner_rows(side, "late"))
    else:
        starts, count = far_span(g, part)
        lists.append(g.inner_rows(side, "far")[starts[side] : starts[side] + count])
    for dst, inner_rows in zip(lefts, lists):
        left_rows(g, dst, inner_rows, rows, band, band_first, g.pair * pair, g.pair)


def cubic_right(g, side, part, inners):
    rights = []
    for inner, span in zip(inners, (early_span, far_span)):
        if span == far_span and part == "own":
            rights.append(inner)
            continue
        starts, count = span(g, part)
        start = pl.multiple_of(by_side(side, starts) * g.size, 2 * g.size)
        rights.append(inner.at[pl.ds(start, count * g.size), :])
    return rights


def left_scratch(g, part, count):
    sizes = [early_span(g, part)[1], g.inner_count("late") if part == "own" else far_span(g, part)[1]]
    return [pltpu.VMEM((count * g.size, n * g.size), jnp.bfloat16) for n in sizes]


def cubic_kernel(g, keep, *refs):
    squares, inners, (out, band, own, *lefts) = refs[:4], refs[4:6], refs[6:]
    layer = layer_index()
    side, core = layer // 2, layer % 2
    cols = g.slab * g.size
    for n, name in enumerate("AB"):
        rows = band_rows(g, side, name)
        own[rows, :] = squares[2 * n][...]
        for q in range(2):
            column = pl.ds(pl.multiple_of((core ^ q) * cols, cols), cols)
            band[rows, column] = squares[2 * n + q][...]
    rights = cubic_right(g, side, "own", inners)
    size = (g.rows + 1) // 2
    for n, first in enumerate(range(0, g.rows, size)):
        rows = range(first, min(first + size, g.rows))
        col = even_down(first)
        width = even_up(rows[-1] + g.slab) - col
        used = lefts[2 * n : 2 * n + 2]
        for value in (0, 1):
            pl.when(side == value)(functools.partial(cubic_left, g, value, "own", rows, band, first, used))
        product = sum(
            dot(left[: len(rows) * g.size, :], window_of(g, core, right, col, width))
            for left, right in zip(used, rights)
        )
        for k, t in enumerate(rows):
            at = (t - col) * g.size
            here = slice(t * g.size, (t + 1) * g.size)
            out[here, :] = 3.0 * own[here, :].astype(jnp.float32) - 2.0 * (
                product[k * g.size : (k + 1) * g.size, at : at + cols] * keep[t : t + 1, :]
            )


def other_part(g, layer, name, squares, inners, band, lefts):
    side, core = layer // 2, layer % 2
    cols = g.slab * g.size
    _, width = g.group(name)
    for q in range(2):
        band[:, pl.ds(pl.multiple_of((core ^ q) * cols, cols), cols)] = squares[q][...]
    for value in (0, 1):
        rows = group_rows(g, 1 - value, name)
        pl.when(side == value)(functools.partial(cubic_left, g, value, name, rows, band, 0, lefts))
    first = group_first(g, 1 - side, name)
    rights = cubic_right(g, side, name, inners)
    return first, sum(
        dot(left[...], window_of(g, core, right, first, width)) for left, right in zip(lefts, rights)
    )


def other_kernel(g, keep, *refs):
    squares, inners, (partial, out, band, *lefts) = refs[:2], refs[2:4], refs[4:]
    first, product = other_part(g, layer_index(), "A", squares, inners, band, lefts)
    for n in range(g.group("A")[0]):
        out[n * g.size : (n + 1) * g.size, :] = partial[block_rows(g, first + n), :] - 2.0 * (
            own_columns(g, product, n) * keep[pl.ds(first + n, 1), :]
        )


def slab_early(g, slab):
    side = 1 - slab // 2
    rows = group_rows(g, 1 - side, "B")
    early = g.inner_rows(side, "early")
    lo, hi = rows[0] - g.reach_low + g.slab * slab, rows[-1] - g.reach_low + g.slab * (slab + 1)
    met = [k for k, t in enumerate(early) if lo <= t < hi]
    count = even_up(len(rows) + g.slab - 1)
    return min(even_down(met[0]), len(early) - count), count


def slab_part(g, slab, square, early, far, lefts):
    side, core = layer_index() // 2, layer_index() % 2
    _, width = g.group("B")
    far_starts, far_count = far_span(g, "B")

    def gather(slab):
        here = 1 - slab // 2
        rows = group_rows(g, 1 - here, "B")
        start, count = slab_early(g, slab)
        far_start = far_starts[here]
        lists = (
            g.inner_rows(here, "early")[start : start + count],
            g.inner_rows(here, "far")[far_start : far_start + far_count],
        )
        for dst, inner_rows in zip(lefts, lists):
            left_rows(g, dst, inner_rows, rows, square, 0, g.slab * slab, g.slab)

    start = jnp.int32(0)
    for value in range(g.layers):
        pl.when(slab == value)(functools.partial(gather, value))
        start = jnp.where(slab == value, slab_early(g, value)[0], start)
    count = slab_early(g, 0)[1]
    first = group_first(g, 1 - side, "B")
    at = lambda start, count: pl.ds(pl.multiple_of(start * g.size, 2 * g.size), count * g.size)
    rights = early.at[at(start, count), :], far.at[at(by_side(side, far_starts), far_count), :]
    windows = [window_of(g, core, right, first, width) for right in rights]
    return first, lambda rows: sum(dot(left[rows, :], window) for left, window in zip(lefts, windows))


def slab_kernel(g, square, early, far, out, *lefts):
    out[...] = slab_part(g, layer_index() ^ 2, square, early, far, lefts)[1](slice(None))


def last_kernel(g, keep, square, early, far, partial, done, total, *refs):
    out, rows, sems, *lefts = refs
    side = layer_index() // 2
    copies = [pltpu.make_async_copy(done, out.at[band_rows(g, 1 - side, "A"), :], sems.at[0])]
    copies[0].start()
    first, product = slab_part(g, layer_index() ^ 3, square, early, far, lefts)
    count = g.group("B")[0]
    step = count // 2
    for begin in range(0, count, step):
        here = slice(begin * g.size, (begin + step) * g.size)
        part = product(here) + total[here, :]
        for n in range(begin, begin + step):
            value = part[(n - begin) * g.size : (n - begin + 1) * g.size, n * g.size : (n + g.slab) * g.size]
            rows[n * g.size : (n + 1) * g.size, :] = partial[block_rows(g, first + n), :] - 2.0 * (
                value * keep[pl.ds(first + n, 1), :]
            )
        to = pl.ds(pl.multiple_of((first + begin) * g.size, g.size), step * g.size)
        copies.append(pltpu.make_async_copy(rows.at[here, :], out.at[to, :], sems.at[len(copies)]))
        copies[-1].start()
    for copy in copies:
        copy.wait()


def call(kernel, out_shape, scratch, *args, after=(), placed=(), place=VMEM):
    specs = [VMEM] * len(args) + [pl.BlockSpec(memory_space=pl.ANY)] * len(after) + [HBM] * len(placed)
    return pl.pallas_call(
        kernel,
        out_shape=out_shape,
        in_specs=specs,
        out_specs=jax.tree.map(lambda _: place, out_shape),
        scratch_shapes=scratch,
        compiler_params=pltpu.CompilerParams(vmem_limit_bytes=LIMIT),
        cost_estimate=pl.CostEstimate(flops=0, bytes_accessed=0, transcendentals=0),
    )(*args, *after, *placed)


def body(density, pattern):
    layers, ring = lax.axis_size("layer"), lax.axis_size("row")
    g = Geometry(*density.shape, *pattern.shape, layers)
    rows_dev, cols = density.shape
    bf16 = functools.partial(jax.ShapeDtypeStruct, dtype=jnp.bfloat16)
    scratch = lambda *shape: pltpu.VMEM(shape, jnp.bfloat16)

    def swap(value, bit):
        return lax.ppermute(value, "layer", [(s, s ^ bit) for s in range(layers)])

    def send(value, name, keep=lambda layer, row: True):
        pairs = []
        for l in range(layers):
            step = step_of(l // 2, name)
            pairs += [
                (l * ring + r, l * ring + (r - step) % ring) for r in range(ring) if keep(l, r)
            ]
        return lax.ppermute(value, ("layer", "row"), pairs)

    half_rows, slab = rows_dev // 2, (rows_dev, cols)
    cross_shape = (g.far * g.size, cols)

    def put_after(value, *after):
        return call(pass_kernel, bf16(value.shape), [], value, after=after)

    sources = [pltpu.with_memory_space_constraint(value, pltpu.HBM) for value in (density, pattern.T)]
    masked, keep = call(
        functools.partial(mask_kernel, g),
        [bf16(slab), jax.ShapeDtypeStruct(((g.rows + 7) // 8 * 8, cols), jnp.float32)],
        [scratch(*slab), pltpu.VMEM(pattern.T.shape, pattern.dtype), pltpu.SemaphoreType.DMA((2,))],
        placed=sources,
    )
    thin = send(masked, NEAR_THIN)
    other = swap(masked, 2)
    beside = swap(masked, 1)
    far_shape = message_shape(g, FAR_WIDE)
    head_shape = (far_shape[0] - cross_shape[0], cols)
    wide, far_wide = call(
        functools.partial(pack_kernel, g),
        [bf16(message_shape(g, NEAR_WIDE)), bf16(head_shape)], [scratch(half_rows, 2 * cols)],
        masked, beside,
    )
    relayed = send(wide, FAR_WIDE, lambda layer, row: row % 2 != layer // 2)
    crossed = swap(thin, 2)
    wide, far_wide = call(
        functools.partial(relay_kernel, g),
        [bf16(wide.shape), bf16(far_shape)], [], wide, relayed, far_wide, other, after=(thin,),
    )
    wide = lax.ppermute(wide, "row", [(r, r ^ 1) for r in range(ring)])
    far_wide = send(far_wide, FAR_WIDE)

    early, late, far = (g.inner_count(part) * g.size for part in ("early", "late", "far"))
    (high_a, wide_a), (high_b, wide_b) = (tuple(n * g.size for n in g.group(name)) for name in "AB")
    span = g.span * g.size
    f32 = functools.partial(jax.ShapeDtypeStruct, dtype=jnp.float32)

    inner_early, sum_a, left_b, late_a, late_b, far_b = call(
        functools.partial(early_kernel, g),
        [
            bf16((early, span)), f32((high_a, wide_a)), bf16((high_b, early)), bf16((high_a, late)),
            bf16((high_b, late)), bf16((high_b, far)),
        ],
        [
            scratch(rows_dev, layers * cols), scratch(high_a, early),
            scratch(rows_dev, 2 * cols),
        ],
        masked, beside, other, swap(other, 1), thin, swap(thin, 1),
    )
    far_beside = swap(far_wide, 1)
    far_thin = call(
        functools.partial(far_thin_kernel, g),
        bf16(message_shape(g, FAR_THIN)), [], far_wide, far_beside, after=(sum_a,),
    )
    far_thin = swap(far_thin, 2)
    pieces = [crossed, swap(crossed, 1), wide, swap(wide, 1), far_wide, far_beside]
    square_a, inner_late = call(
        functools.partial(late_kernel, g),
        [bf16((high_a, cols)), bf16((late, span))],
        [scratch(rows_dev, 2 * cols), scratch(cross_shape[0], 2 * cols)],
        keep, *pieces, sum_a, late_a,
    )
    across_a, beside_a = swap(square_a, 2), swap(square_a, 1)
    sum_b = call(
        functools.partial(sum_kernel, g), f32((high_b, wide_b)), [], left_b, late_b, inner_early, inner_late
    )
    square_b, inner_far = call(
        functools.partial(square_kernel, g),
        [bf16((high_b, cols)), bf16((far, span))], [],
        keep, far_thin, swap(far_thin, 1), sum_b, far_b,
    )
    across_b, beside_b = swap(square_b, 2), swap(square_b, 1)
    partial = call(
        functools.partial(cubic_kernel, g),
        f32(slab),
        [scratch(rows_dev, 2 * cols), scratch(*slab)] + 2 * left_scratch(g, "own", (g.rows + 1) // 2),
        keep, square_a, beside_a, square_b, beside_b, inner_early, inner_late,
    )
    done = call(
        functools.partial(other_kernel, g),
        f32((high_a, cols)), [scratch(high_a, 2 * cols)] + left_scratch(g, "A", g.group("A")[0]),
        keep, across_a, swap(across_a, 1), inner_early, inner_far, partial,
    )
    across_b = put_after(across_b, done)
    lefts = [scratch(high_b, n * g.size) for n in (slab_early(g, 0)[1], far_span(g, "B")[1])]
    total = call(
        functools.partial(slab_kernel, g), f32((high_b, wide_b)), lefts, across_b, inner_early, inner_far
    )
    return call(
        functools.partial(last_kernel, g),
        f32(slab),
        [pltpu.VMEM((high_b, cols), jnp.float32), pltpu.SemaphoreType.DMA((3,))] + lefts,
        keep, swap(across_b, 1), inner_early, inner_far, partial, done, total,
        place=HBM,
    )


def solution(mesh):
    placed = (P("row", "layer"), P("row", "layer"))
    return jax.shard_map(
        body, mesh=mesh, in_specs=placed, out_specs=P("row", "layer"), check_vma=False
    )
```

```python
import functools

import jax
import jax.numpy as jnp
from jax import lax
from jax.experimental import pallas as pl
from jax.experimental.pallas import tpu as pltpu
from jax.sharding import PartitionSpec as P

VMEM = pl.BlockSpec(memory_space=pltpu.VMEM)
HBM = pl.BlockSpec(memory_space=pltpu.HBM)
LIMIT = 12 * 1024 * 1024


class Geometry:
    def __init__(self, rows_dev, slab_cols, block_rows, slab_offsets, layers):
        self.rows, self.slab = block_rows, slab_offsets
        self.size = rows_dev // block_rows
        self.layers = layers
        self.offsets = slab_offsets * layers
        self.half = self.offsets // 2
        self.pair = 2 * slab_offsets
        self.reach_low, self.reach_high = self.half, self.half - 1
        self.columns = self.pair + block_rows - 1
        self.span = even_up(self.columns)
        self.far = even_up(max(len(self.reached(step)) for step in (-2, 2)))

    def needed(self, t, side):
        lo, hi = self.pair * side - t, self.pair * side - t + self.columns
        if t < 0:
            lo = max(lo, -t)
        if t >= self.rows:
            hi = min(hi, self.offsets - (t - self.rows + 1))
        lo, hi = max(lo, 0), min(hi, self.offsets)
        return lo, max(lo, hi)

    def reached(self, step):
        first = step * self.rows
        return [
            t
            for t in range(first, first + self.rows)
            if -self.reach_low <= t < self.rows + self.reach_high
        ]

    def inner_rows(self, side, part):
        if part == "early":
            return sorted(list(range(self.rows)) + self.reached(step_of(side, NEAR_THIN)))
        rows = []
        for name in ([NEAR_WIDE, FAR_WIDE] if part == "late" else [FAR_THIN]):
            reached = self.reached(step_of(side, name))
            rows += reached + [None] * (0 if name[0] == "near" else self.far - len(reached))
        return rows

    def inner_count(self, part):
        return len(self.inner_rows(0, part))

    def group(self, name):
        first = even_up(2 * self.rows // 5)
        count = first if name == "A" else self.rows - first
        return count, even_up(count - 1 + self.slab)

    def first(self, side, name):
        return 0 if (side == 0) == (name == "A") else self.rows - self.group(name)[0]

    def layout(self, side, name):
        step = step_of(side, name)
        found = []
        for t in self.reached(step):
            lo, hi = self.needed(t, side)
            lo, hi = max(lo, self.pair * side), min(hi, self.pair * (side + 1))
            if hi > lo:
                found.append((even_up(hi) - even_down(lo), t, even_down(lo), even_up(hi)))
        found.sort(reverse=True)
        slots = (len(found) + 1) // 2
        used = [0] * slots
        places = {}
        for n, (width, t, lo, hi) in enumerate(found):
            slot = n if n < slots else 2 * slots - 1 - n
            places[t] = (slot, used[slot], lo, hi)
            used[slot] += width
        return places, slots, max(used)


def even_down(n):
    return n // 2 * 2


def even_up(n):
    return (n + 1) // 2 * 2


def step_of(side, name):
    sign = 1 if (name[1] == "thin") == (side == 0) else -1
    return sign * (1 if name[0] == "near" else 2)


NEAR_WIDE, NEAR_THIN = ("near", "wide"), ("near", "thin")
FAR_WIDE, FAR_THIN = ("far", "wide"), ("far", "thin")


def message_shape(g, name):
    layouts = [g.layout(side, name) for side in (0, 1)]
    rows, cols = max(f[1] for f in layouts) * g.size // 2, max(f[2] for f in layouts) * g.size
    if name == FAR_WIDE:
        return rows + g.far * g.size, g.slab * g.size
    return rows, cols


def layer_index():
    return lax.axis_index("layer").astype(jnp.int32)


def mask_kernel(g, density_ref, pattern_ref, out_ref, keep, density, pattern, sems):
    copies = [
        pltpu.make_async_copy(source, target, sems.at[n])
        for n, (source, target) in enumerate(((pattern_ref, pattern), (density_ref, density)))
    ]
    for copy in copies:
        copy.start()
    copies[0].wait()
    offsets, cols = pattern.shape[0], keep.shape[1]
    block = lax.broadcasted_iota(jnp.int32, (offsets, cols), 1) // g.size
    row = lax.broadcasted_iota(jnp.int32, (offsets, cols), 0)
    spread = jnp.where(block == row, 1.0, 0.0).astype(jnp.float32)
    keep[: g.rows, :] = lax.dot_general(
        pattern[...].astype(jnp.float32), spread, (((0,), (0,)), ((), ())),
        preferred_element_type=jnp.float32,
    )
    keep[g.rows :, :] = jnp.zeros((keep.shape[0] - g.rows, cols), keep.dtype)
    copies[1].wait()
    for t in range(g.rows):
        rows = slice(t * g.size, (t + 1) * g.size)
        out_ref[rows, :] = density[rows, :] * keep[t : t + 1, :].astype(jnp.bfloat16)


def cross_rows(g, side):
    rows = [t - step_of(side, FAR_WIDE) * g.rows for t in g.reached(step_of(side, FAR_WIDE))]
    count = g.far
    return min(rows[0], g.rows - count), count


def place_row(dst_ref, dst_row, dst_lo, src_ref, src_row, height, lo, hi, shift, size, limit):
    first, last = max(lo, shift), min(hi, limit + shift)
    base = dst_lo - lo
    rows = slice(dst_row, dst_row + height)
    if first >= last:
        dst_ref[rows, dst_lo * size : (hi + base) * size] = jnp.zeros(
            (height, (hi - lo) * size), dst_ref.dtype
        )
        return
    value = src_ref[src_row : src_row + height, (first - shift) * size : (last - shift) * size]
    parts = []
    if first > lo:
        parts.append(jnp.zeros((height, (first - lo) * size), dst_ref.dtype))
    parts.append(value)
    if hi > last:
        parts.append(jnp.zeros((height, (hi - last) * size), dst_ref.dtype))
    if len(parts) > 1:
        value = jnp.concatenate(parts, axis=1)
    dst_ref[rows, dst_lo * size : (hi + base) * size] = value


def pack(g, side, name, source, row_of, lead, height, out):
    places, slots, _ = g.layout(side, name)
    filled = [0] * slots
    for t, (slot, col, lo, hi) in places.items():
        out[slot * height : (slot + 1) * height, col * g.size : (col + hi - lo) * g.size] = source[
            pl.ds(row_of(t - step_of(side, name) * g.rows), height), (lo - lead) * g.size : (hi - lead) * g.size
        ]
        filled[slot] = max(filled[slot], col + hi - lo)
    for slot, count in enumerate(filled):
        if count * g.size < out.shape[1]:
            out[slot * height : (slot + 1) * height, count * g.size :] = jnp.zeros(
                (height, out.shape[1] - count * g.size), out.dtype
            )
    if slots * height < out.shape[0] and name != FAR_WIDE:
        out[slots * height :, :] = jnp.zeros((out.shape[0] - slots * height, out.shape[1]), out.dtype)


def fill_near(g, core, slabs, near):
    half, cols = g.size // 2, g.slab * g.size
    for q, slab in enumerate(slabs):
        start = pl.multiple_of((core ^ q) * cols, cols)
        for t in range(g.rows):
            src = pl.multiple_of(t * g.size + half * core, half)
            near[t * half : (t + 1) * half, pl.ds(start, cols)] = slab[pl.ds(src, half), :]


def pack_kernel(g, own_ref, beside_ref, wide, far, near):
    side, core = layer_index() // 2, layer_index() % 2
    half = g.size // 2
    fill_near(g, core, (own_ref, beside_ref), near)

    def fill(side):
        for name, out in ((NEAR_WIDE, wide), (FAR_WIDE, far)):
            pack(g, side, name, near, lambda row: row * half, side * g.pair, half, out)

    for value in (0, 1):
        pl.when(side == value)(functools.partial(fill, value))


def relay_kernel(g, own_ref, relayed_ref, far_ref, other_ref, after_ref, out_ref, message):
    side, row = layer_index() // 2, lax.axis_index("row")
    pick((row % 2) == side, own_ref, relayed_ref, out_ref)
    message[: far_ref.shape[0], :] = far_ref[...]

    def fill(side):
        first, count = cross_rows(g, side)
        message[far_ref.shape[0] :, :] = other_ref[first * g.size : (first + count) * g.size, :]

    for value in (0, 1):
        pl.when(side == value)(functools.partial(fill, value))


def pass_kernel(in_ref, *refs):
    refs[-1][...] = in_ref[...]


def far_thin_kernel(g, far_own, far_beside, after_ref, message):
    side, core = layer_index() // 2, layer_index() % 2
    half = g.size // 2

    def fill(side, source):
        first, count = cross_rows(g, side)
        start = source.shape[0] - (count + first) * g.size
        row_of = lambda row: pl.multiple_of(start + row * g.size + half * core, half)
        pack(g, 1 - side, FAR_THIN, source, row_of, (1 - side) * (g.offsets - g.slab), half, message)

    for value in (0, 1):
        for held, source in ((True, far_own), (False, far_beside)):
            here = jnp.logical_and(side == value, (core == 1 - value) == held)
            pl.when(here)(functools.partial(fill, value, source))


def fill_pair(g, core, slabs, pair):
    cols = g.slab * g.size
    for q, slab in enumerate(slabs):
        pair[:, pl.ds(pl.multiple_of((core ^ q) * cols, cols), cols)] = slab[...]


def place_parts(g, dst, at, height, t, side, parts):
    shift = t - g.pair * side
    values, done = [], 0
    for lo, hi, load in parts:
        lo, hi = max(lo, done - shift), min(hi, g.span - shift)
        if lo >= hi:
            continue
        if lo + shift > done:
            values.append(jnp.zeros((height, (lo + shift - done) * g.size), dst.dtype))
        values.append(load(lo, hi))
        done = hi + shift
    if done < g.span:
        values.append(jnp.zeros((height, (g.span - done) * g.size), dst.dtype))
    dst[pl.ds(at, height), :] = jnp.concatenate(values, axis=1) if len(values) > 1 else values[0]


def left_rows(g, dst, inner_rows, rows, band, band_first, lead, limit):
    runs = []
    for k, t in enumerate(inner_rows):
        offset = None if t is None else t - k
        if runs and runs[-1][0] == offset:
            runs[-1][2] = k + 1
        else:
            runs.append([offset, k, k + 1])
    for n, i in enumerate(rows):
        for offset, lo, hi in runs:
            shift = hi if offset is None else i - g.reach_low - offset + lead
            place_row(
                dst, n * g.size, lo, band, (band_first + n) * g.size, g.size, lo, hi, shift, g.size, limit
            )


def window_of(g, core, inner, col, cols):
    start = pl.multiple_of((core * g.slab + col) * g.size, 2 * g.size)
    return inner[:, pl.ds(start, cols * g.size)]


def dot(left, right):
    return jnp.dot(left, right, preferred_element_type=jnp.float32)


def own_columns(g, product, n):
    return product[n * g.size : (n + 1) * g.size, n * g.size : (n + g.slab) * g.size]


def by_side(side, values):
    return jnp.where(side == 0, values[0], values[1])


def group_first(g, side, name):
    return by_side(side, [g.first(value, name) for value in (0, 1)])


def message_part(g, side, name, t, piece, height):
    places, _, _ = g.layout(side, name)
    if t not in places:
        return []
    slot, col, lo, hi = places[t]
    rows = slice(slot * height, (slot + 1) * height)
    return [(lo, hi, lambda a, b: piece[rows, (col + a - lo) * g.size : (col + b - lo) * g.size])]


def pair_part(g, pair_index, ref, row, height):
    base = g.pair * pair_index
    return (
        base,
        base + g.pair,
        lambda a, b: ref[pl.ds(row, height), (a - base) * g.size : (b - base) * g.size],
    )


def pick(condition, first, second, out):
    pl.when(condition)(lambda: out.__setitem__(..., first[...]))
    pl.when(jnp.logical_not(condition))(lambda: out.__setitem__(..., second[...]))


def group_rows(g, side, name):
    first = g.first(side, name)
    return range(first, first + g.group(name)[0])


def early_kernel(g, own, beside, *refs):
    others, thins = refs[:2], refs[2:4]
    inner, sum_a, late_a, band, left_a, pair = refs[4:]
    layer = layer_index()
    side, core = layer // 2, layer % 2
    cols = g.slab * g.size
    for q, slab in enumerate((own, beside, *others)):
        band[:, pl.ds(pl.multiple_of((layer ^ q) * cols, cols), cols)] = slab[...]
    fill_pair(g, core, thins, pair)

    def gather(side):
        near = g.reached(step_of(side, NEAR_THIN))
        early, late = (g.inner_rows(side, part) for part in ("early", "late"))
        for k, t in enumerate(early):
            if 0 <= t < g.rows:
                part = (0, g.offsets, lambda a, b, t=t: band[
                    t * g.size : (t + 1) * g.size, a * g.size : b * g.size
                ])
            else:
                part = pair_part(g, side, pair, (t - near[0]) * g.size, g.size)
            place_parts(g, inner, k * g.size, g.size, t, side, [part])
        rows = group_rows(g, side, "A")
        for left, inner_rows in ((left_a, early), (late_a, late)):
            left_rows(g, left, inner_rows, rows, band, rows[0], 0, g.offsets)

    for value in (0, 1):
        pl.when(side == value)(functools.partial(gather, value))
    col, (_, cols) = group_first(g, side, "A"), g.group("A")
    sum_a[...] = dot(left_a[...], window_of(g, core, inner, col, cols))


def square_of(g, name, side, core, keep, lefts, inners, product=0.0):
    first, (_, cols) = group_first(g, side, name), g.group(name)
    for left, inner in zip(lefts, inners):
        product = product + dot(left[...], window_of(g, core, inner, first, cols))
    return lambda n: (own_columns(g, product, n) * keep[pl.ds(first + n, 1), :]).astype(jnp.bfloat16)


def late_kernel(g, keep, *refs):
    crossed, wides, wide_fars = (refs[2 * n : 2 * n + 2] for n in range(3))
    total, left, square, inner = refs[6:]
    layer = layer_index()
    side, core = layer // 2, layer % 2
    half = g.size // 2

    def slab_parts(side, core, slabs, row, height):
        base = g.pair * (1 - side)
        parts = []
        for c in (0, 1):
            lo, slab = base + c * g.slab, slabs[core ^ c]
            parts.append((lo, lo + g.slab, lambda a, b, lo=lo, slab=slab: slab[
                row : row + height, (a - lo) * g.size : (b - lo) * g.size
            ]))
        return parts

    def gather(layer):
        side, core = layer // 2, layer % 2
        near = g.reached(step_of(side, NEAR_WIDE))
        tail = wide_fars[0].shape[0] - g.far * g.size
        for k, t in enumerate(g.inner_rows(side, "late")):
            if t is None:
                inner[k * g.size : (k + 1) * g.size, :] = jnp.zeros((g.size, inner.shape[1]), inner.dtype)
                continue
            if t in near:
                name, pieces, slabs, row = NEAR_WIDE, wides, crossed, (t - near[0]) * g.size
            else:
                name, pieces, slabs = FAR_WIDE, wide_fars, wide_fars
                row = tail + (t - step_of(side, FAR_WIDE) * g.rows - cross_rows(g, side)[0]) * g.size
            for q, piece in enumerate(pieces):
                at = half * (core ^ q)
                parts = message_part(g, side, name, t, piece, half)
                parts += slab_parts(side, core, slabs, row + at, half)
                parts.sort(key=lambda part: part[0])
                place_parts(g, inner, k * g.size + at, half, t, side, parts)

    for value in range(g.layers):
        pl.when(layer == value)(functools.partial(gather, value))
    row_of = square_of(g, "A", side, core, keep, [left], [inner], total[...])
    for n in range(g.group("A")[0]):
        square[n * g.size : (n + 1) * g.size, :] = row_of(n)


def sum_kernel(g, band, early, late, out, far_left, early_left, late_left):
    side, core = layer_index() // 2, layer_index() % 2

    def fill(side):
        rows = group_rows(g, side, "B")
        for left, part in ((early_left, "early"), (late_left, "late"), (far_left, "far")):
            left_rows(g, left, g.inner_rows(side, part), rows, band, rows[0], 0, g.offsets)

    for value in (0, 1):
        pl.when(side == value)(functools.partial(fill, value))
    first, (_, cols) = group_first(g, side, "B"), g.group("B")
    out[...] = dot(early_left[...], window_of(g, core, early, first, cols))
    out[...] += dot(late_left[...], window_of(g, core, late, first, cols))


def square_kernel(g, keep, far, far_beside, total, far_left, *refs):
    square, inner = refs
    side, core = layer_index() // 2, layer_index() % 2
    half = g.size // 2

    def gather(side):
        for k, t in enumerate(g.inner_rows(side, "far")):
            for q, piece in enumerate((far, far_beside)):
                at = pl.multiple_of(k * g.size + half * (core ^ q), half)
                parts = [] if t is None else message_part(g, side, FAR_THIN, t, piece, half)
                place_parts(g, inner, at, half, t or 0, side, parts)

    for value in (0, 1):
        pl.when(side == value)(functools.partial(gather, value))
    row_of = square_of(g, "B", side, core, keep, [far_left], [inner], total[...])
    for n in range(g.group("B")[0]):
        square[n * g.size : (n + 1) * g.size, :] = row_of(n)


def band_rows(g, side, name):
    return pl.ds(pl.multiple_of(group_first(g, side, name) * g.size, 2 * g.size), g.group(name)[0] * g.size)


def block_rows(g, t):
    return pl.ds(pl.multiple_of(t * g.size, g.size), g.size)


def early_span(g, part):
    spans = []
    for side in (0, 1):
        rows, pair = (range(g.rows), side) if part == "own" else (group_rows(g, 1 - side, part), 1 - side)
        lo = rows[0] - g.reach_low + g.pair * pair
        hi = rows[-1] - g.reach_low + g.pair * (pair + 1)
        met = [k for k, t in enumerate(g.inner_rows(side, "early")) if lo <= t < hi]
        spans.append((even_down(met[0]), met[-1] + 1))
    count = even_up(max(hi - lo for lo, hi in spans))
    total = len(g.inner_rows(0, "early"))
    return [min(lo, total - count) for lo, _ in spans], count


def far_span(g, part):
    spans = []
    for side in (0, 1):
        rows = group_rows(g, 1 - side, part)
        lo = rows[0] - g.reach_low + g.pair * (1 - side)
        hi = rows[-1] - g.reach_low + g.pair * (2 - side)
        met = [k for k, t in enumerate(g.inner_rows(side, "far")) if t is not None and lo <= t < hi]
        spans.append((even_down(met[0]), met[-1] + 1) if met else (0, 0))
    count = even_up(max(hi - lo for lo, hi in spans))
    return [min(lo, g.inner_count("far") - count) for lo, _ in spans], count


def cubic_left(g, side, part, rows, band, band_first, lefts):
    pair = side if part == "own" else 1 - side
    starts, count = early_span(g, part)
    lists = [g.inner_rows(side, "early")[starts[side] : starts[side] + count]]
    if part == "own":
        lists.append(g.inner_rows(side, "late"))
    else:
        starts, count = far_span(g, part)
        lists.append(g.inner_rows(side, "far")[starts[side] : starts[side] + count])
    for dst, inner_rows in zip(lefts, lists):
        left_rows(g, dst, inner_rows, rows, band, band_first, g.pair * pair, g.pair)


def cubic_right(g, side, part, inners):
    rights = []
    for inner, span in zip(inners, (early_span, far_span)):
        if span == far_span and part == "own":
            rights.append(inner)
            continue
        starts, count = span(g, part)
        start = pl.multiple_of(by_side(side, starts) * g.size, 2 * g.size)
        rights.append(inner.at[pl.ds(start, count * g.size), :])
    return rights


def left_scratch(g, part, count):
    sizes = [early_span(g, part)[1], g.inner_count("late") if part == "own" else far_span(g, part)[1]]
    return [pltpu.VMEM((count * g.size, n * g.size), jnp.bfloat16) for n in sizes]


def cubic_kernel(g, keep, *refs):
    squares, inners, (out, band, own, *lefts) = refs[:4], refs[4:6], refs[6:]
    layer = layer_index()
    side, core = layer // 2, layer % 2
    cols = g.slab * g.size
    for n, name in enumerate("AB"):
        rows = band_rows(g, side, name)
        own[rows, :] = squares[2 * n][...]
        for q in range(2):
            column = pl.ds(pl.multiple_of((core ^ q) * cols, cols), cols)
            band[rows, column] = squares[2 * n + q][...]
    rights = cubic_right(g, side, "own", inners)
    size = (g.rows + 1) // 2
    for n, first in enumerate(range(0, g.rows, size)):
        rows = range(first, min(first + size, g.rows))
        col = even_down(first)
        width = even_up(rows[-1] + g.slab) - col
        used = lefts[2 * n : 2 * n + 2]
        for value in (0, 1):
            pl.when(side == value)(functools.partial(cubic_left, g, value, "own", rows, band, first, used))
        product = sum(
            dot(left[: len(rows) * g.size, :], window_of(g, core, right, col, width))
            for left, right in zip(used, rights)
        )
        for k, t in enumerate(rows):
            at = (t - col) * g.size
            here = slice(t * g.size, (t + 1) * g.size)
            out[here, :] = 3.0 * own[here, :].astype(jnp.float32) - 2.0 * (
                product[k * g.size : (k + 1) * g.size, at : at + cols] * keep[t : t + 1, :]
            )


def other_part(g, layer, name, squares, inners, band, lefts):
    side, core = layer // 2, layer % 2
    cols = g.slab * g.size
    _, width = g.group(name)
    for q in range(2):
        band[:, pl.ds(pl.multiple_of((core ^ q) * cols, cols), cols)] = squares[q][...]
    for value in (0, 1):
        rows = group_rows(g, 1 - value, name)
        pl.when(side == value)(functools.partial(cubic_left, g, value, name, rows, band, 0, lefts))
    first = group_first(g, 1 - side, name)
    rights = cubic_right(g, side, name, inners)
    return first, sum(
        dot(left[...], window_of(g, core, right, first, width)) for left, right in zip(lefts, rights)
    )


def slab_early(g, slab):
    side = 1 - slab // 2
    rows = group_rows(g, 1 - side, "B")
    early = g.inner_rows(side, "early")
    lo, hi = rows[0] - g.reach_low + g.slab * slab, rows[-1] - g.reach_low + g.slab * (slab + 1)
    met = [k for k, t in enumerate(early) if lo <= t < hi]
    count = even_up(len(rows) + g.slab - 1)
    return min(even_down(met[0]), len(early) - count), count


def slab_rights(g, slab, early, far, out):
    side, core = layer_index() // 2, layer_index() % 2
    _, width = g.group("B")
    first = group_first(g, 1 - side, "B")
    start, count = jnp.int32(0), slab_early(g, 0)[1]
    for value in range(g.layers):
        start = jnp.where(slab == value, slab_early(g, value)[0], start)
    far_starts, far_count = far_span(g, "B")
    split = count * g.size
    at = lambda start, count: pl.ds(pl.multiple_of(start * g.size, 2 * g.size), count * g.size)
    out[:split, :] = window_of(g, core, early.at[at(start, count), :], first, width)
    out[split:, :] = window_of(g, core, far.at[at(by_side(side, far_starts), far_count), :], first, width)


def slab_left(g, slab, square, left):
    far_starts, far_count = far_span(g, "B")

    def gather(slab):
        here = 1 - slab // 2
        start, count = slab_early(g, slab)
        inner_rows = g.inner_rows(here, "early")[start : start + count]
        inner_rows = inner_rows + g.inner_rows(here, "far")[far_starts[here] : far_starts[here] + far_count]
        left_rows(g, left, inner_rows, group_rows(g, 1 - here, "B"), square, 0, g.slab * slab, g.slab)

    for value in range(g.layers):
        pl.when(slab == value)(functools.partial(gather, value))


def other_kernel(g, keep, *refs):
    squares, inners, (partial, out, straight, beside, band, *lefts) = refs[:2], refs[2:4], refs[4:]
    first, product = other_part(g, layer_index(), "A", squares, inners, band, lefts)
    for n in range(g.group("A")[0]):
        out[n * g.size : (n + 1) * g.size, :] = partial[block_rows(g, first + n), :] - 2.0 * (
            own_columns(g, product, n) * keep[pl.ds(first + n, 1), :]
        )
    for q, right in ((2, straight), (3, beside)):
        slab_rights(g, layer_index() ^ q, *inners, right)


def slab_kernel(g, keep, square, right, partial, out, left):
    slab_left(g, layer_index() ^ 2, square, left)
    first = group_first(g, 1 - layer_index() // 2, "B")
    product = dot(left[...], right[...])
    for n in range(g.group("B")[0]):
        out[n * g.size : (n + 1) * g.size, :] = partial[block_rows(g, first + n), :] - 2.0 * (
            own_columns(g, product, n) * keep[pl.ds(first + n, 1), :]
        )


def last_kernel(g, keep, square, right, partial, done, out, rows, sems, left):
    side = layer_index() // 2
    copies = [pltpu.make_async_copy(done, out.at[band_rows(g, 1 - side, "A"), :], sems.at[0])]
    copies[0].start()
    slab_left(g, layer_index() ^ 3, square, left)
    first, count = group_first(g, 1 - side, "B"), g.group("B")[0]
    step = count // 2
    for begin in range(0, count, step):
        here = slice(begin * g.size, (begin + step) * g.size)
        part = dot(left[here, :], right[...])
        for n in range(begin, begin + step):
            value = part[(n - begin) * g.size : (n - begin + 1) * g.size, n * g.size : (n + g.slab) * g.size]
            row = slice(n * g.size, (n + 1) * g.size)
            rows[row, :] = partial[row, :] - 2.0 * (value * keep[pl.ds(first + n, 1), :])
        to = pl.ds(pl.multiple_of((first + begin) * g.size, g.size), step * g.size)
        copies.append(pltpu.make_async_copy(rows.at[here, :], out.at[to, :], sems.at[len(copies)]))
        copies[-1].start()
    for copy in copies:
        copy.wait()


def call(kernel, out_shape, scratch, *args, after=(), placed=(), place=VMEM):
    specs = [VMEM] * len(args) + [pl.BlockSpec(memory_space=pl.ANY)] * len(after) + [HBM] * len(placed)
    return pl.pallas_call(
        kernel,
        out_shape=out_shape,
        in_specs=specs,
        out_specs=jax.tree.map(lambda _: place, out_shape),
        scratch_shapes=scratch,
        compiler_params=pltpu.CompilerParams(vmem_limit_bytes=LIMIT),
        cost_estimate=pl.CostEstimate(flops=0, bytes_accessed=0, transcendentals=0),
    )(*args, *after, *placed)


def body(density, pattern):
    layers, ring = lax.axis_size("layer"), lax.axis_size("row")
    g = Geometry(*density.shape, *pattern.shape, layers)
    rows_dev, cols = density.shape
    bf16 = functools.partial(jax.ShapeDtypeStruct, dtype=jnp.bfloat16)
    scratch = lambda *shape: pltpu.VMEM(shape, jnp.bfloat16)

    def swap(value, bit):
        return lax.ppermute(value, "layer", [(s, s ^ bit) for s in range(layers)])

    def send(value, name, keep=lambda layer, row: True):
        pairs = []
        for l in range(layers):
            step = step_of(l // 2, name)
            pairs += [
                (l * ring + r, l * ring + (r - step) % ring) for r in range(ring) if keep(l, r)
            ]
        return lax.ppermute(value, ("layer", "row"), pairs)

    half_rows, slab = rows_dev // 2, (rows_dev, cols)
    cross_shape = (g.far * g.size, cols)

    def put_after(value, *after):
        return call(pass_kernel, bf16(value.shape), [], value, after=after)

    sources = [pltpu.with_memory_space_constraint(value, pltpu.HBM) for value in (density, pattern.T)]
    masked, keep = call(
        functools.partial(mask_kernel, g),
        [bf16(slab), jax.ShapeDtypeStruct(((g.rows + 7) // 8 * 8, cols), jnp.float32)],
        [scratch(*slab), pltpu.VMEM(pattern.T.shape, pattern.dtype), pltpu.SemaphoreType.DMA((2,))],
        placed=sources,
    )
    thin = send(masked, NEAR_THIN)
    other = swap(masked, 2)
    beside = swap(masked, 1)
    far_shape = message_shape(g, FAR_WIDE)
    head_shape = (far_shape[0] - cross_shape[0], cols)
    wide, far_wide = call(
        functools.partial(pack_kernel, g),
        [bf16(message_shape(g, NEAR_WIDE)), bf16(head_shape)], [scratch(half_rows, 2 * cols)],
        masked, beside,
    )
    relayed = send(wide, FAR_WIDE, lambda layer, row: row % 2 != layer // 2)
    crossed = swap(thin, 2)
    wide, far_wide = call(
        functools.partial(relay_kernel, g),
        [bf16(wide.shape), bf16(far_shape)], [], wide, relayed, far_wide, other, after=(thin,),
    )
    wide = lax.ppermute(wide, "row", [(r, r ^ 1) for r in range(ring)])
    far_wide = send(far_wide, FAR_WIDE)

    early, late, far = (g.inner_count(part) * g.size for part in ("early", "late", "far"))
    (high_a, wide_a), (high_b, wide_b) = (tuple(n * g.size for n in g.group(name)) for name in "AB")
    span = g.span * g.size
    f32 = functools.partial(jax.ShapeDtypeStruct, dtype=jnp.float32)

    inner_early, sum_a, late_a, band = call(
        functools.partial(early_kernel, g),
        [
            bf16((early, span)), f32((high_a, wide_a)), bf16((high_a, late)),
            bf16((rows_dev, layers * cols)),
        ],
        [scratch(high_a, early), scratch(rows_dev, 2 * cols)],
        masked, beside, other, swap(other, 1), thin, swap(thin, 1),
    )
    far_beside = swap(far_wide, 1)
    far_thin = call(
        functools.partial(far_thin_kernel, g),
        bf16(message_shape(g, FAR_THIN)), [], far_wide, far_beside, after=(sum_a,),
    )
    far_thin = swap(far_thin, 2)
    pieces = [crossed, swap(crossed, 1), wide, swap(wide, 1), far_wide, far_beside]
    square_a, inner_late = call(
        functools.partial(late_kernel, g),
        [bf16((high_a, cols)), bf16((late, span))],
        [],
        keep, *pieces, sum_a, late_a,
    )
    across_a, beside_a = swap(square_a, 2), swap(square_a, 1)
    sum_b, far_b = call(
        functools.partial(sum_kernel, g),
        [f32((high_b, wide_b)), bf16((high_b, far))], [scratch(high_b, early), scratch(high_b, late)],
        band, inner_early, inner_late,
    )
    square_b, inner_far = call(
        functools.partial(square_kernel, g),
        [bf16((high_b, cols)), bf16((far, span))], [],
        keep, far_thin, swap(far_thin, 1), sum_b, far_b,
    )
    across_b, beside_b = swap(square_b, 2), swap(square_b, 1)
    partial = call(
        functools.partial(cubic_kernel, g),
        f32(slab),
        [scratch(rows_dev, 2 * cols), scratch(*slab)] + 2 * left_scratch(g, "own", (g.rows + 1) // 2),
        keep, square_a, beside_a, square_b, beside_b, inner_early, inner_late,
    )
    meet = (slab_early(g, 0)[1] + far_span(g, "B")[1]) * g.size
    done, straight, next_to = call(
        functools.partial(other_kernel, g),
        [f32((high_a, cols)), bf16((meet, wide_b)), bf16((meet, wide_b))],
        [scratch(high_a, 2 * cols)] + left_scratch(g, "A", g.group("A")[0]),
        keep, across_a, swap(across_a, 1), inner_early, inner_far, partial,
    )
    across_b = put_after(across_b, done)
    left = scratch(high_b, meet)
    partial = call(
        functools.partial(slab_kernel, g), f32((high_b, cols)), [left], keep, across_b, straight, partial
    )
    return call(
        functools.partial(last_kernel, g),
        f32(slab),
        [pltpu.VMEM((high_b, cols), jnp.float32), pltpu.SemaphoreType.DMA((3,)), left],
        keep, swap(across_b, 1), next_to, partial, done,
        place=HBM,
    )


def solution(mesh):
    placed = (P("row", "layer"), P("row", "layer"))
    return jax.shard_map(
        body, mesh=mesh, in_specs=placed, out_specs=P("row", "layer"), check_vma=False
    )
```

```python
import functools

import jax
import jax.numpy as jnp
from jax import lax
from jax.experimental import pallas as pl
from jax.experimental.pallas import tpu as pltpu
from jax.sharding import PartitionSpec as P

VMEM = pl.BlockSpec(memory_space=pltpu.VMEM)
HBM = pl.BlockSpec(memory_space=pltpu.HBM)
LIMIT = 12 * 1024 * 1024


class Geometry:
    def __init__(self, rows_dev, slab_cols, block_rows, slab_offsets, layers):
        self.rows, self.slab = block_rows, slab_offsets
        self.size = rows_dev // block_rows
        self.layers = layers
        self.offsets = slab_offsets * layers
        self.half = self.offsets // 2
        self.pair = 2 * slab_offsets
        self.reach_low, self.reach_high = self.half, self.half - 1
        self.columns = self.pair + block_rows - 1
        self.span = even_up(self.columns)
        self.far = even_up(max(len(self.reached(step)) for step in (-2, 2)))

    def needed(self, t, side):
        lo, hi = self.pair * side - t, self.pair * side - t + self.columns
        if t < 0:
            lo = max(lo, -t)
        if t >= self.rows:
            hi = min(hi, self.offsets - (t - self.rows + 1))
        lo, hi = max(lo, 0), min(hi, self.offsets)
        return lo, max(lo, hi)

    def reached(self, step):
        first = step * self.rows
        return [
            t
            for t in range(first, first + self.rows)
            if -self.reach_low <= t < self.rows + self.reach_high
        ]

    def inner_rows(self, side, part):
        if part == "early":
            return sorted(list(range(self.rows)) + self.reached(step_of(side, NEAR_THIN)))
        rows = []
        for name in ([NEAR_WIDE, FAR_WIDE] if part == "late" else [FAR_THIN]):
            reached = self.reached(step_of(side, name))
            rows += reached + [None] * (0 if name[0] == "near" else self.far - len(reached))
        return rows

    def inner_count(self, part):
        return len(self.inner_rows(0, part))

    def group(self, name):
        first = even_up(2 * self.rows // 5)
        count = first if name == "A" else self.rows - first
        return count, even_up(count - 1 + self.slab)

    def first(self, side, name):
        return 0 if (side == 0) == (name == "A") else self.rows - self.group(name)[0]

    def layout(self, side, name):
        step = step_of(side, name)
        found = []
        for t in self.reached(step):
            lo, hi = self.needed(t, side)
            lo, hi = max(lo, self.pair * side), min(hi, self.pair * (side + 1))
            if hi > lo:
                found.append((even_up(hi) - even_down(lo), t, even_down(lo), even_up(hi)))
        found.sort(reverse=True)
        slots = (len(found) + 1) // 2
        used = [0] * slots
        places = {}
        for n, (width, t, lo, hi) in enumerate(found):
            slot = n if n < slots else 2 * slots - 1 - n
            places[t] = (slot, used[slot], lo, hi)
            used[slot] += width
        return places, slots, max(used)


def even_down(n):
    return n // 2 * 2


def even_up(n):
    return (n + 1) // 2 * 2


def step_of(side, name):
    sign = 1 if (name[1] == "thin") == (side == 0) else -1
    return sign * (1 if name[0] == "near" else 2)


NEAR_WIDE, NEAR_THIN = ("near", "wide"), ("near", "thin")
FAR_WIDE, FAR_THIN = ("far", "wide"), ("far", "thin")


def message_shape(g, name):
    layouts = [g.layout(side, name) for side in (0, 1)]
    rows, cols = max(f[1] for f in layouts) * g.size // 2, max(f[2] for f in layouts) * g.size
    if name == FAR_WIDE:
        return rows + g.far * g.size, g.slab * g.size
    return rows, cols


def layer_index():
    return lax.axis_index("layer").astype(jnp.int32)


def mask_kernel(g, density_ref, pattern_ref, out_ref, keep, give, density, pattern, sems):
    copies = [
        pltpu.make_async_copy(source, target, sems.at[n])
        for n, (source, target) in enumerate(((pattern_ref, pattern), (density_ref, density)))
    ]
    for copy in copies:
        copy.start()
    copies[0].wait()
    offsets, cols = pattern.shape[0], keep.shape[1]
    block = lax.broadcasted_iota(jnp.int32, (offsets, cols), 1) // g.size
    row = lax.broadcasted_iota(jnp.int32, (offsets, cols), 0)
    spread = jnp.where(block == row, 1.0, 0.0).astype(jnp.float32)
    keep[: g.rows, :] = lax.dot_general(
        pattern[...].astype(jnp.float32), spread, (((0,), (0,)), ((), ())),
        preferred_element_type=jnp.float32,
    )
    keep[g.rows :, :] = jnp.zeros((keep.shape[0] - g.rows, cols), keep.dtype)
    copies[1].wait()
    half = g.size // 2
    for t in range(g.rows):
        rows = slice(t * g.size, (t + 1) * g.size)
        out_ref[rows, :] = density[rows, :] * keep[t : t + 1, :].astype(jnp.bfloat16)
        start = pl.multiple_of(t * g.size + half * (1 - layer_index() % 2), half)
        give[t * half : (t + 1) * half, :] = out_ref[pl.ds(start, half), :]


def cross_rows(g, side):
    rows = [t - step_of(side, FAR_WIDE) * g.rows for t in g.reached(step_of(side, FAR_WIDE))]
    count = g.far
    return min(rows[0], g.rows - count), count


def place_row(dst_ref, dst_row, dst_lo, src_ref, src_row, height, lo, hi, shift, size, limit):
    first, last = max(lo, shift), min(hi, limit + shift)
    base = dst_lo - lo
    rows = slice(dst_row, dst_row + height)
    if first >= last:
        dst_ref[rows, dst_lo * size : (hi + base) * size] = jnp.zeros(
            (height, (hi - lo) * size), dst_ref.dtype
        )
        return
    value = src_ref[src_row : src_row + height, (first - shift) * size : (last - shift) * size]
    parts = []
    if first > lo:
        parts.append(jnp.zeros((height, (first - lo) * size), dst_ref.dtype))
    parts.append(value)
    if hi > last:
        parts.append(jnp.zeros((height, (hi - last) * size), dst_ref.dtype))
    if len(parts) > 1:
        value = jnp.concatenate(parts, axis=1)
    dst_ref[rows, dst_lo * size : (hi + base) * size] = value


def pack(g, side, name, source, row_of, lead, height, out):
    places, slots, _ = g.layout(side, name)
    filled = [0] * slots
    for t, (slot, col, lo, hi) in places.items():
        out[slot * height : (slot + 1) * height, col * g.size : (col + hi - lo) * g.size] = source[
            pl.ds(row_of(t - step_of(side, name) * g.rows), height), (lo - lead) * g.size : (hi - lead) * g.size
        ]
        filled[slot] = max(filled[slot], col + hi - lo)
    for slot, count in enumerate(filled):
        if count * g.size < out.shape[1]:
            out[slot * height : (slot + 1) * height, count * g.size :] = jnp.zeros(
                (height, out.shape[1] - count * g.size), out.dtype
            )
    if slots * height < out.shape[0] and name != FAR_WIDE:
        out[slots * height :, :] = jnp.zeros((out.shape[0] - slots * height, out.shape[1]), out.dtype)


def fill_near(g, core, own, given, near):
    half, cols = g.size // 2, g.slab * g.size
    here, there = (pl.ds(pl.multiple_of(c * cols, cols), cols) for c in (core, 1 - core))
    for t in range(g.rows):
        src = pl.multiple_of(t * g.size + half * core, half)
        near[t * half : (t + 1) * half, here] = own[pl.ds(src, half), :]
    near[:, there] = given[...]


def pack_kernel(g, own_ref, given_ref, wide, far, near):
    side, core = layer_index() // 2, layer_index() % 2
    half = g.size // 2
    fill_near(g, core, own_ref, given_ref, near)

    def fill(side):
        for name, out in ((NEAR_WIDE, wide), (FAR_WIDE, far)):
            pack(g, side, name, near, lambda row: row * half, side * g.pair, half, out)

    for value in (0, 1):
        pl.when(side == value)(functools.partial(fill, value))


def relay_kernel(g, own_ref, relayed_ref, far_ref, other_ref, after_ref, out_ref, message):
    side, row = layer_index() // 2, lax.axis_index("row")
    pick((row % 2) == side, own_ref, relayed_ref, out_ref)
    message[: far_ref.shape[0], :] = far_ref[...]

    def fill(side):
        first, count = cross_rows(g, side)
        message[far_ref.shape[0] :, :] = other_ref[first * g.size : (first + count) * g.size, :]

    for value in (0, 1):
        pl.when(side == value)(functools.partial(fill, value))


def pass_kernel(in_ref, *refs):
    refs[-1][...] = in_ref[...]


def far_thin_kernel(g, far_own, far_beside, after_ref, message):
    side, core = layer_index() // 2, layer_index() % 2
    half = g.size // 2

    def fill(side, source):
        first, count = cross_rows(g, side)
        start = source.shape[0] - (count + first) * g.size
        row_of = lambda row: pl.multiple_of(start + row * g.size + half * core, half)
        pack(g, 1 - side, FAR_THIN, source, row_of, (1 - side) * (g.offsets - g.slab), half, message)

    for value in (0, 1):
        for held, source in ((True, far_own), (False, far_beside)):
            here = jnp.logical_and(side == value, (core == 1 - value) == held)
            pl.when(here)(functools.partial(fill, value, source))


def fill_pair(g, core, slabs, pair):
    cols = g.slab * g.size
    for q, slab in enumerate(slabs):
        pair[:, pl.ds(pl.multiple_of((core ^ q) * cols, cols), cols)] = slab[...]


def place_parts(g, dst, at, height, t, side, parts):
    shift = t - g.pair * side
    values, done = [], 0
    for lo, hi, load in parts:
        lo, hi = max(lo, done - shift), min(hi, g.span - shift)
        if lo >= hi:
            continue
        if lo + shift > done:
            values.append(jnp.zeros((height, (lo + shift - done) * g.size), dst.dtype))
        values.append(load(lo, hi))
        done = hi + shift
    if done < g.span:
        values.append(jnp.zeros((height, (g.span - done) * g.size), dst.dtype))
    dst[pl.ds(at, height), :] = jnp.concatenate(values, axis=1) if len(values) > 1 else values[0]


def left_rows(g, dst, inner_rows, rows, band, band_first, lead, limit):
    runs = []
    for k, t in enumerate(inner_rows):
        offset = None if t is None else t - k
        if runs and runs[-1][0] == offset:
            runs[-1][2] = k + 1
        else:
            runs.append([offset, k, k + 1])
    for n, i in enumerate(rows):
        for offset, lo, hi in runs:
            shift = hi if offset is None else i - g.reach_low - offset + lead
            place_row(
                dst, n * g.size, lo, band, (band_first + n) * g.size, g.size, lo, hi, shift, g.size, limit
            )


def window_of(g, core, inner, col, cols):
    start = pl.multiple_of((core * g.slab + col) * g.size, 2 * g.size)
    return inner[:, pl.ds(start, cols * g.size)]


def dot(left, right):
    return jnp.dot(left, right, preferred_element_type=jnp.float32)


def own_columns(g, product, n):
    return product[n * g.size : (n + 1) * g.size, n * g.size : (n + g.slab) * g.size]


def by_side(side, values):
    return jnp.where(side == 0, values[0], values[1])


def group_first(g, side, name):
    return by_side(side, [g.first(value, name) for value in (0, 1)])


def message_part(g, side, name, t, piece, height):
    places, _, _ = g.layout(side, name)
    if t not in places:
        return []
    slot, col, lo, hi = places[t]
    rows = slice(slot * height, (slot + 1) * height)
    return [(lo, hi, lambda a, b: piece[rows, (col + a - lo) * g.size : (col + b - lo) * g.size])]


def pair_part(g, pair_index, ref, row, height):
    base = g.pair * pair_index
    return (
        base,
        base + g.pair,
        lambda a, b: ref[pl.ds(row, height), (a - base) * g.size : (b - base) * g.size],
    )


def pick(condition, first, second, out):
    pl.when(condition)(lambda: out.__setitem__(..., first[...]))
    pl.when(jnp.logical_not(condition))(lambda: out.__setitem__(..., second[...]))


def group_rows(g, side, name):
    first = g.first(side, name)
    return range(first, first + g.group(name)[0])


def early_kernel(g, own, beside, *refs):
    others, thins = refs[:2], refs[2:4]
    inner, sum_a, late_a, band, left_a, pair = refs[4:]
    layer = layer_index()
    side, core = layer // 2, layer % 2
    cols = g.slab * g.size
    for q, slab in enumerate((own, beside, *others)):
        band[:, pl.ds(pl.multiple_of((layer ^ q) * cols, cols), cols)] = slab[...]
    fill_pair(g, core, thins, pair)

    def gather(side):
        near = g.reached(step_of(side, NEAR_THIN))
        early, late = (g.inner_rows(side, part) for part in ("early", "late"))
        for k, t in enumerate(early):
            if 0 <= t < g.rows:
                part = (0, g.offsets, lambda a, b, t=t: band[
                    t * g.size : (t + 1) * g.size, a * g.size : b * g.size
                ])
            else:
                part = pair_part(g, side, pair, (t - near[0]) * g.size, g.size)
            place_parts(g, inner, k * g.size, g.size, t, side, [part])
        rows = group_rows(g, side, "A")
        for left, inner_rows in ((left_a, early), (late_a, late)):
            left_rows(g, left, inner_rows, rows, band, rows[0], 0, g.offsets)

    for value in (0, 1):
        pl.when(side == value)(functools.partial(gather, value))
    col, (_, cols) = group_first(g, side, "A"), g.group("A")
    sum_a[...] = dot(left_a[...], window_of(g, core, inner, col, cols))


def square_of(g, name, side, core, keep, lefts, inners, product=0.0):
    first, (_, cols) = group_first(g, side, name), g.group(name)
    for left, inner in zip(lefts, inners):
        product = product + dot(left[...], window_of(g, core, inner, first, cols))
    return lambda n: (own_columns(g, product, n) * keep[pl.ds(first + n, 1), :]).astype(jnp.bfloat16)


def late_kernel(g, keep, *refs):
    crossed, wides, wide_fars = (refs[2 * n : 2 * n + 2] for n in range(3))
    total, left, square, inner = refs[6:]
    layer = layer_index()
    side, core = layer // 2, layer % 2
    half = g.size // 2

    def slab_parts(side, core, slabs, row, height):
        base = g.pair * (1 - side)
        parts = []
        for c in (0, 1):
            lo, slab = base + c * g.slab, slabs[core ^ c]
            parts.append((lo, lo + g.slab, lambda a, b, lo=lo, slab=slab: slab[
                row : row + height, (a - lo) * g.size : (b - lo) * g.size
            ]))
        return parts

    def gather(layer):
        side, core = layer // 2, layer % 2
        near = g.reached(step_of(side, NEAR_WIDE))
        tail = wide_fars[0].shape[0] - g.far * g.size
        for k, t in enumerate(g.inner_rows(side, "late")):
            if t is None:
                inner[k * g.size : (k + 1) * g.size, :] = jnp.zeros((g.size, inner.shape[1]), inner.dtype)
                continue
            if t in near:
                name, pieces, slabs, row = NEAR_WIDE, wides, crossed, (t - near[0]) * g.size
            else:
                name, pieces, slabs = FAR_WIDE, wide_fars, wide_fars
                row = tail + (t - step_of(side, FAR_WIDE) * g.rows - cross_rows(g, side)[0]) * g.size
            for q, piece in enumerate(pieces):
                at = half * (core ^ q)
                parts = message_part(g, side, name, t, piece, half)
                parts += slab_parts(side, core, slabs, row + at, half)
                parts.sort(key=lambda part: part[0])
                place_parts(g, inner, k * g.size + at, half, t, side, parts)

    for value in range(g.layers):
        pl.when(layer == value)(functools.partial(gather, value))
    row_of = square_of(g, "A", side, core, keep, [left], [inner], total[...])
    for n in range(g.group("A")[0]):
        square[n * g.size : (n + 1) * g.size, :] = row_of(n)


def sum_kernel(g, band, early, late, out, far_left, early_left, late_left):
    side, core = layer_index() // 2, layer_index() % 2

    def fill(side):
        rows = group_rows(g, side, "B")
        for left, part in ((early_left, "early"), (late_left, "late"), (far_left, "far")):
            left_rows(g, left, g.inner_rows(side, part), rows, band, rows[0], 0, g.offsets)

    for value in (0, 1):
        pl.when(side == value)(functools.partial(fill, value))
    first, (_, cols) = group_first(g, side, "B"), g.group("B")
    out[...] = dot(early_left[...], window_of(g, core, early, first, cols))
    out[...] += dot(late_left[...], window_of(g, core, late, first, cols))


def square_kernel(g, keep, far, far_beside, total, far_left, *refs):
    square, inner = refs
    side, core = layer_index() // 2, layer_index() % 2
    half = g.size // 2

    def gather(side):
        for k, t in enumerate(g.inner_rows(side, "far")):
            for q, piece in enumerate((far, far_beside)):
                at = pl.multiple_of(k * g.size + half * (core ^ q), half)
                parts = [] if t is None else message_part(g, side, FAR_THIN, t, piece, half)
                place_parts(g, inner, at, half, t or 0, side, parts)

    for value in (0, 1):
        pl.when(side == value)(functools.partial(gather, value))
    row_of = square_of(g, "B", side, core, keep, [far_left], [inner], total[...])
    for n in range(g.group("B")[0]):
        square[n * g.size : (n + 1) * g.size, :] = row_of(n)


def band_rows(g, side, name):
    return pl.ds(pl.multiple_of(group_first(g, side, name) * g.size, 2 * g.size), g.group(name)[0] * g.size)


def block_rows(g, t):
    return pl.ds(pl.multiple_of(t * g.size, g.size), g.size)


def early_span(g, part):
    spans = []
    for side in (0, 1):
        rows, pair = (range(g.rows), side) if part == "own" else (group_rows(g, 1 - side, part), 1 - side)
        lo = rows[0] - g.reach_low + g.pair * pair
        hi = rows[-1] - g.reach_low + g.pair * (pair + 1)
        met = [k for k, t in enumerate(g.inner_rows(side, "early")) if lo <= t < hi]
        spans.append((even_down(met[0]), met[-1] + 1))
    count = even_up(max(hi - lo for lo, hi in spans))
    total = len(g.inner_rows(0, "early"))
    return [min(lo, total - count) for lo, _ in spans], count


def far_span(g, part):
    spans = []
    for side in (0, 1):
        rows = group_rows(g, 1 - side, part)
        lo = rows[0] - g.reach_low + g.pair * (1 - side)
        hi = rows[-1] - g.reach_low + g.pair * (2 - side)
        met = [k for k, t in enumerate(g.inner_rows(side, "far")) if t is not None and lo <= t < hi]
        spans.append((even_down(met[0]), met[-1] + 1) if met else (0, 0))
    count = even_up(max(hi - lo for lo, hi in spans))
    return [min(lo, g.inner_count("far") - count) for lo, _ in spans], count


def cubic_left(g, side, part, rows, band, band_first, lefts):
    pair = side if part == "own" else 1 - side
    starts, count = early_span(g, part)
    lists = [g.inner_rows(side, "early")[starts[side] : starts[side] + count]]
    if part == "own":
        lists.append(g.inner_rows(side, "late"))
    else:
        starts, count = far_span(g, part)
        lists.append(g.inner_rows(side, "far")[starts[side] : starts[side] + count])
    for dst, inner_rows in zip(lefts, lists):
        left_rows(g, dst, inner_rows, rows, band, band_first, g.pair * pair, g.pair)


def cubic_right(g, side, part, inners):
    rights = []
    for inner, span in zip(inners, (early_span, far_span)):
        if span == far_span and part == "own":
            rights.append(inner)
            continue
        starts, count = span(g, part)
        start = pl.multiple_of(by_side(side, starts) * g.size, 2 * g.size)
        rights.append(inner.at[pl.ds(start, count * g.size), :])
    return rights


def left_scratch(g, part, count):
    sizes = [early_span(g, part)[1], g.inner_count("late") if part == "own" else far_span(g, part)[1]]
    return [pltpu.VMEM((count * g.size, n * g.size), jnp.bfloat16) for n in sizes]


def cubic_kernel(g, keep, *refs):
    squares, inners, (out, band, own, *lefts) = refs[:4], refs[4:6], refs[6:]
    layer = layer_index()
    side, core = layer // 2, layer % 2
    cols = g.slab * g.size
    for n, name in enumerate("AB"):
        rows = band_rows(g, side, name)
        own[rows, :] = squares[2 * n][...]
        for q in range(2):
            column = pl.ds(pl.multiple_of((core ^ q) * cols, cols), cols)
            band[rows, column] = squares[2 * n + q][...]
    rights = cubic_right(g, side, "own", inners)
    size = (g.rows + 1) // 2
    for n, first in enumerate(range(0, g.rows, size)):
        rows = range(first, min(first + size, g.rows))
        col = even_down(first)
        width = even_up(rows[-1] + g.slab) - col
        used = lefts[2 * n : 2 * n + 2]
        for value in (0, 1):
            pl.when(side == value)(functools.partial(cubic_left, g, value, "own", rows, band, first, used))
        product = sum(
            dot(left[: len(rows) * g.size, :], window_of(g, core, right, col, width))
            for left, right in zip(used, rights)
        )
        for k, t in enumerate(rows):
            at = (t - col) * g.size
            here = slice(t * g.size, (t + 1) * g.size)
            out[here, :] = 3.0 * own[here, :].astype(jnp.float32) - 2.0 * (
                product[k * g.size : (k + 1) * g.size, at : at + cols] * keep[t : t + 1, :]
            )


def other_part(g, layer, name, squares, inners, band, lefts):
    side, core = layer // 2, layer % 2
    cols = g.slab * g.size
    _, width = g.group(name)
    for q in range(2):
        band[:, pl.ds(pl.multiple_of((core ^ q) * cols, cols), cols)] = squares[q][...]
    for value in (0, 1):
        rows = group_rows(g, 1 - value, name)
        pl.when(side == value)(functools.partial(cubic_left, g, value, name, rows, band, 0, lefts))
    first = group_first(g, 1 - side, name)
    rights = cubic_right(g, side, name, inners)
    return first, sum(
        dot(left[...], window_of(g, core, right, first, width)) for left, right in zip(lefts, rights)
    )


def slab_early(g, slab):
    side = 1 - slab // 2
    rows = group_rows(g, 1 - side, "B")
    early = g.inner_rows(side, "early")
    lo, hi = rows[0] - g.reach_low + g.slab * slab, rows[-1] - g.reach_low + g.slab * (slab + 1)
    met = [k for k, t in enumerate(early) if lo <= t < hi]
    count = even_up(len(rows) + g.slab - 1)
    return min(even_down(met[0]), len(early) - count), count


def slab_rights(g, slab, early, far, out):
    side, core = layer_index() // 2, layer_index() % 2
    _, width = g.group("B")
    first = group_first(g, 1 - side, "B")
    start, count = jnp.int32(0), slab_early(g, 0)[1]
    for value in range(g.layers):
        start = jnp.where(slab == value, slab_early(g, value)[0], start)
    far_starts, far_count = far_span(g, "B")
    split = count * g.size
    at = lambda start, count: pl.ds(pl.multiple_of(start * g.size, 2 * g.size), count * g.size)
    out[:split, :] = window_of(g, core, early.at[at(start, count), :], first, width)
    out[split:, :] = window_of(g, core, far.at[at(by_side(side, far_starts), far_count), :], first, width)


def slab_left(g, slab, square, left):
    far_starts, far_count = far_span(g, "B")

    def gather(slab):
        here = 1 - slab // 2
        start, count = slab_early(g, slab)
        inner_rows = g.inner_rows(here, "early")[start : start + count]
        inner_rows = inner_rows + g.inner_rows(here, "far")[far_starts[here] : far_starts[here] + far_count]
        left_rows(g, left, inner_rows, group_rows(g, 1 - here, "B"), square, 0, g.slab * slab, g.slab)

    for value in range(g.layers):
        pl.when(slab == value)(functools.partial(gather, value))


def other_kernel(g, keep, *refs):
    squares, inners, (partial, out, straight, beside, band, *lefts) = refs[:2], refs[2:4], refs[4:]
    first, product = other_part(g, layer_index(), "A", squares, inners, band, lefts)
    for n in range(g.group("A")[0]):
        out[n * g.size : (n + 1) * g.size, :] = partial[block_rows(g, first + n), :] - 2.0 * (
            own_columns(g, product, n) * keep[pl.ds(first + n, 1), :]
        )
    for q, right in ((2, straight), (3, beside)):
        slab_rights(g, layer_index() ^ q, *inners, right)


def slab_kernel(g, keep, square, right, partial, out, left):
    slab_left(g, layer_index() ^ 2, square, left)
    first = group_first(g, 1 - layer_index() // 2, "B")
    product = dot(left[...], right[...])
    for n in range(g.group("B")[0]):
        out[n * g.size : (n + 1) * g.size, :] = partial[block_rows(g, first + n), :] - 2.0 * (
            own_columns(g, product, n) * keep[pl.ds(first + n, 1), :]
        )


def last_kernel(g, keep, square, right, partial, done, out, rows, sems, left):
    side = layer_index() // 2
    copies = [pltpu.make_async_copy(done, out.at[band_rows(g, 1 - side, "A"), :], sems.at[0])]
    copies[0].start()
    slab_left(g, layer_index() ^ 3, square, left)
    first, count = group_first(g, 1 - side, "B"), g.group("B")[0]
    step = count // 2
    for begin in range(0, count, step):
        here = slice(begin * g.size, (begin + step) * g.size)
        part = dot(left[here, :], right[...])
        for n in range(begin, begin + step):
            value = part[(n - begin) * g.size : (n - begin + 1) * g.size, n * g.size : (n + g.slab) * g.size]
            row = slice(n * g.size, (n + 1) * g.size)
            rows[row, :] = partial[row, :] - 2.0 * (value * keep[pl.ds(first + n, 1), :])
        to = pl.ds(pl.multiple_of((first + begin) * g.size, g.size), step * g.size)
        copies.append(pltpu.make_async_copy(rows.at[here, :], out.at[to, :], sems.at[len(copies)]))
        copies[-1].start()
    for copy in copies:
        copy.wait()


def call(kernel, out_shape, scratch, *args, after=(), placed=(), place=VMEM):
    specs = [VMEM] * len(args) + [pl.BlockSpec(memory_space=pl.ANY)] * len(after) + [HBM] * len(placed)
    return pl.pallas_call(
        kernel,
        out_shape=out_shape,
        in_specs=specs,
        out_specs=jax.tree.map(lambda _: place, out_shape),
        scratch_shapes=scratch,
        compiler_params=pltpu.CompilerParams(vmem_limit_bytes=LIMIT),
        cost_estimate=pl.CostEstimate(flops=0, bytes_accessed=0, transcendentals=0),
    )(*args, *after, *placed)


def body(density, pattern):
    layers, ring = lax.axis_size("layer"), lax.axis_size("row")
    g = Geometry(*density.shape, *pattern.shape, layers)
    rows_dev, cols = density.shape
    bf16 = functools.partial(jax.ShapeDtypeStruct, dtype=jnp.bfloat16)
    scratch = lambda *shape: pltpu.VMEM(shape, jnp.bfloat16)

    def swap(value, bit):
        return lax.ppermute(value, "layer", [(s, s ^ bit) for s in range(layers)])

    def send(value, name, keep=lambda layer, row: True):
        pairs = []
        for l in range(layers):
            step = step_of(l // 2, name)
            pairs += [
                (l * ring + r, l * ring + (r - step) % ring) for r in range(ring) if keep(l, r)
            ]
        return lax.ppermute(value, ("layer", "row"), pairs)

    half_rows, slab = rows_dev // 2, (rows_dev, cols)
    cross_shape = (g.far * g.size, cols)

    def put_after(value, *after):
        return call(pass_kernel, bf16(value.shape), [], value, after=after)

    sources = [pltpu.with_memory_space_constraint(value, pltpu.HBM) for value in (density, pattern.T)]
    masked, keep, give = call(
        functools.partial(mask_kernel, g),
        [
            bf16(slab), jax.ShapeDtypeStruct(((g.rows + 7) // 8 * 8, cols), jnp.float32),
            bf16((half_rows, cols)),
        ],
        [scratch(*slab), pltpu.VMEM(pattern.T.shape, pattern.dtype), pltpu.SemaphoreType.DMA((2,))],
        placed=sources,
    )
    thin = send(masked, NEAR_THIN)
    other = swap(masked, 2)
    beside = swap(masked, 1)
    far_shape = message_shape(g, FAR_WIDE)
    head_shape = (far_shape[0] - cross_shape[0], cols)
    wide, far_wide = call(
        functools.partial(pack_kernel, g),
        [bf16(message_shape(g, NEAR_WIDE)), bf16(head_shape)], [scratch(half_rows, 2 * cols)],
        masked, swap(give, 1),
    )
    relayed = send(wide, FAR_WIDE, lambda layer, row: row % 2 != layer // 2)
    crossed = swap(thin, 2)
    wide, far_wide = call(
        functools.partial(relay_kernel, g),
        [bf16(wide.shape), bf16(far_shape)], [], wide, relayed, far_wide, other, after=(thin,),
    )
    wide = lax.ppermute(wide, "row", [(r, r ^ 1) for r in range(ring)])
    far_wide = send(far_wide, FAR_WIDE)

    early, late, far = (g.inner_count(part) * g.size for part in ("early", "late", "far"))
    (high_a, wide_a), (high_b, wide_b) = (tuple(n * g.size for n in g.group(name)) for name in "AB")
    span = g.span * g.size
    f32 = functools.partial(jax.ShapeDtypeStruct, dtype=jnp.float32)

    inner_early, sum_a, late_a, band = call(
        functools.partial(early_kernel, g),
        [
            bf16((early, span)), f32((high_a, wide_a)), bf16((high_a, late)),
            bf16((rows_dev, layers * cols)),
        ],
        [scratch(high_a, early), scratch(rows_dev, 2 * cols)],
        masked, beside, other, swap(other, 1), thin, swap(thin, 1),
    )
    far_beside = swap(far_wide, 1)
    far_thin = call(
        functools.partial(far_thin_kernel, g),
        bf16(message_shape(g, FAR_THIN)), [], far_wide, far_beside, after=(sum_a,),
    )
    far_thin = swap(far_thin, 2)
    pieces = [crossed, swap(crossed, 1), wide, swap(wide, 1), far_wide, far_beside]
    square_a, inner_late = call(
        functools.partial(late_kernel, g),
        [bf16((high_a, cols)), bf16((late, span))],
        [],
        keep, *pieces, sum_a, late_a,
    )
    across_a, beside_a = swap(square_a, 2), swap(square_a, 1)
    sum_b, far_b = call(
        functools.partial(sum_kernel, g),
        [f32((high_b, wide_b)), bf16((high_b, far))], [scratch(high_b, early), scratch(high_b, late)],
        band, inner_early, inner_late,
    )
    square_b, inner_far = call(
        functools.partial(square_kernel, g),
        [bf16((high_b, cols)), bf16((far, span))], [],
        keep, far_thin, swap(far_thin, 1), sum_b, far_b,
    )
    across_b, beside_b = swap(square_b, 2), swap(square_b, 1)
    partial = call(
        functools.partial(cubic_kernel, g),
        f32(slab),
        [scratch(rows_dev, 2 * cols), scratch(*slab)] + 2 * left_scratch(g, "own", (g.rows + 1) // 2),
        keep, square_a, beside_a, square_b, beside_b, inner_early, inner_late,
    )
    meet = (slab_early(g, 0)[1] + far_span(g, "B")[1]) * g.size
    done, straight, next_to = call(
        functools.partial(other_kernel, g),
        [f32((high_a, cols)), bf16((meet, wide_b)), bf16((meet, wide_b))],
        [scratch(high_a, 2 * cols)] + left_scratch(g, "A", g.group("A")[0]),
        keep, across_a, swap(across_a, 1), inner_early, inner_far, partial,
    )
    across_b = put_after(across_b, done)
    left = scratch(high_b, meet)
    partial = call(
        functools.partial(slab_kernel, g), f32((high_b, cols)), [left], keep, across_b, straight, partial
    )
    return call(
        functools.partial(last_kernel, g),
        f32(slab),
        [pltpu.VMEM((high_b, cols), jnp.float32), pltpu.SemaphoreType.DMA((3,)), left],
        keep, swap(across_b, 1), next_to, partial, done,
        place=HBM,
    )


def solution(mesh):
    placed = (P("row", "layer"), P("row", "layer"))
    return jax.shard_map(
        body, mesh=mesh, in_specs=placed, out_specs=P("row", "layer"), check_vma=False
    )
```

```python
import functools

import jax
import jax.numpy as jnp
from jax import lax
from jax.experimental import pallas as pl
from jax.experimental.pallas import tpu as pltpu
from jax.sharding import PartitionSpec as P

VMEM = pl.BlockSpec(memory_space=pltpu.VMEM)
HBM = pl.BlockSpec(memory_space=pltpu.HBM)
LIMIT = 12 * 1024 * 1024


class Geometry:
    def __init__(self, rows_dev, slab_cols, block_rows, slab_offsets, layers):
        self.rows, self.slab = block_rows, slab_offsets
        self.size = rows_dev // block_rows
        self.layers = layers
        self.offsets = slab_offsets * layers
        self.half = self.offsets // 2
        self.pair = 2 * slab_offsets
        self.reach_low, self.reach_high = self.half, self.half - 1
        self.columns = self.pair + block_rows - 1
        self.span = even_up(self.columns)
        self.far = even_up(max(len(self.reached(step)) for step in (-2, 2)))

    def needed(self, t, side):
        lo, hi = self.pair * side - t, self.pair * side - t + self.columns
        if t < 0:
            lo = max(lo, -t)
        if t >= self.rows:
            hi = min(hi, self.offsets - (t - self.rows + 1))
        lo, hi = max(lo, 0), min(hi, self.offsets)
        return lo, max(lo, hi)

    def reached(self, step):
        first = step * self.rows
        return [
            t
            for t in range(first, first + self.rows)
            if -self.reach_low <= t < self.rows + self.reach_high
        ]

    def inner_rows(self, side, part):
        if part == "early":
            return sorted(list(range(self.rows)) + self.reached(step_of(side, NEAR_THIN)))
        rows = []
        for name in ([NEAR_WIDE, FAR_WIDE] if part == "late" else [FAR_THIN]):
            reached = self.reached(step_of(side, name))
            rows += reached + [None] * (0 if name[0] == "near" else self.far - len(reached))
        return rows

    def inner_count(self, part):
        return len(self.inner_rows(0, part))

    def group(self, name):
        first = even_up(2 * self.rows // 5)
        count = first if name == "A" else self.rows - first
        return count, even_up(count - 1 + self.slab)

    def first(self, side, name):
        return 0 if (side == 0) == (name == "A") else self.rows - self.group(name)[0]

    def layout(self, side, name):
        step = step_of(side, name)
        found = []
        for t in self.reached(step):
            lo, hi = self.needed(t, side)
            lo, hi = max(lo, self.pair * side), min(hi, self.pair * (side + 1))
            if hi > lo:
                found.append((even_up(hi) - even_down(lo), t, even_down(lo), even_up(hi)))
        found.sort(reverse=True)
        slots = (len(found) + 1) // 2
        used = [0] * slots
        places = {}
        for n, (width, t, lo, hi) in enumerate(found):
            slot = n if n < slots else 2 * slots - 1 - n
            places[t] = (slot, used[slot], lo, hi)
            used[slot] += width
        return places, slots, max(used)


def even_down(n):
    return n // 2 * 2


def even_up(n):
    return (n + 1) // 2 * 2


def step_of(side, name):
    sign = 1 if (name[1] == "thin") == (side == 0) else -1
    return sign * (1 if name[0] == "near" else 2)


NEAR_WIDE, NEAR_THIN = ("near", "wide"), ("near", "thin")
FAR_WIDE, FAR_THIN = ("far", "wide"), ("far", "thin")


def message_shape(g, name):
    layouts = [g.layout(side, name) for side in (0, 1)]
    rows, cols = max(f[1] for f in layouts) * g.size // 2, max(f[2] for f in layouts) * g.size
    if name == FAR_WIDE:
        return rows + g.far * g.size, g.slab * g.size
    return rows, cols


def layer_index():
    return lax.axis_index("layer").astype(jnp.int32)


def mask_kernel(g, density_ref, pattern_ref, out_ref, keep, give, density, pattern, sems):
    copies = [
        pltpu.make_async_copy(source, target, sems.at[n])
        for n, (source, target) in enumerate(((pattern_ref, pattern), (density_ref, density)))
    ]
    for copy in copies:
        copy.start()
    copies[0].wait()
    offsets, cols = pattern.shape[0], keep.shape[1]
    block = lax.broadcasted_iota(jnp.int32, (offsets, cols), 1) // g.size
    row = lax.broadcasted_iota(jnp.int32, (offsets, cols), 0)
    spread = jnp.where(block == row, 1.0, 0.0).astype(jnp.float32)
    keep[: g.rows, :] = lax.dot_general(
        pattern[...].astype(jnp.float32), spread, (((0,), (0,)), ((), ())),
        preferred_element_type=jnp.float32,
    )
    keep[g.rows :, :] = jnp.zeros((keep.shape[0] - g.rows, cols), keep.dtype)
    copies[1].wait()
    half = g.size // 2
    for t in range(g.rows):
        rows = slice(t * g.size, (t + 1) * g.size)
        out_ref[rows, :] = density[rows, :] * keep[t : t + 1, :].astype(jnp.bfloat16)
        start = pl.multiple_of(t * g.size + half * (1 - layer_index() % 2), half)
        give[t * half : (t + 1) * half, :] = out_ref[pl.ds(start, half), :]


def cross_rows(g, side):
    rows = [t - step_of(side, FAR_WIDE) * g.rows for t in g.reached(step_of(side, FAR_WIDE))]
    count = g.far
    return min(rows[0], g.rows - count), count


def place_row(dst_ref, dst_row, dst_lo, src_ref, src_row, height, lo, hi, shift, size, limit):
    first, last = max(lo, shift), min(hi, limit + shift)
    base = dst_lo - lo
    rows = slice(dst_row, dst_row + height)
    if first >= last:
        dst_ref[rows, dst_lo * size : (hi + base) * size] = jnp.zeros(
            (height, (hi - lo) * size), dst_ref.dtype
        )
        return
    value = src_ref[src_row : src_row + height, (first - shift) * size : (last - shift) * size]
    parts = []
    if first > lo:
        parts.append(jnp.zeros((height, (first - lo) * size), dst_ref.dtype))
    parts.append(value)
    if hi > last:
        parts.append(jnp.zeros((height, (hi - last) * size), dst_ref.dtype))
    if len(parts) > 1:
        value = jnp.concatenate(parts, axis=1)
    dst_ref[rows, dst_lo * size : (hi + base) * size] = value


def pack(g, side, name, source, row_of, lead, height, out):
    places, slots, _ = g.layout(side, name)
    filled = [0] * slots
    for t, (slot, col, lo, hi) in places.items():
        out[slot * height : (slot + 1) * height, col * g.size : (col + hi - lo) * g.size] = source[
            pl.ds(row_of(t - step_of(side, name) * g.rows), height), (lo - lead) * g.size : (hi - lead) * g.size
        ]
        filled[slot] = max(filled[slot], col + hi - lo)
    for slot, count in enumerate(filled):
        if count * g.size < out.shape[1]:
            out[slot * height : (slot + 1) * height, count * g.size :] = jnp.zeros(
                (height, out.shape[1] - count * g.size), out.dtype
            )
    if slots * height < out.shape[0] and name != FAR_WIDE:
        out[slots * height :, :] = jnp.zeros((out.shape[0] - slots * height, out.shape[1]), out.dtype)


def fill_near(g, core, own, given, near):
    half, cols = g.size // 2, g.slab * g.size
    here, there = (pl.ds(pl.multiple_of(c * cols, cols), cols) for c in (core, 1 - core))
    for t in range(g.rows):
        src = pl.multiple_of(t * g.size + half * core, half)
        near[t * half : (t + 1) * half, here] = own[pl.ds(src, half), :]
    near[:, there] = given[...]


def pack_kernel(g, own_ref, given_ref, wide, far, near):
    side, core = layer_index() // 2, layer_index() % 2
    half = g.size // 2
    fill_near(g, core, own_ref, given_ref, near)

    def fill(side):
        for name, out in ((NEAR_WIDE, wide), (FAR_WIDE, far)):
            pack(g, side, name, near, lambda row: row * half, side * g.pair, half, out)

    for value in (0, 1):
        pl.when(side == value)(functools.partial(fill, value))


def relay_kernel(g, own_ref, relayed_ref, far_ref, other_ref, after_ref, out_ref, message):
    side, row = layer_index() // 2, lax.axis_index("row")
    pick((row % 2) == side, own_ref, relayed_ref, out_ref)
    message[: far_ref.shape[0], :] = far_ref[...]

    def fill(side):
        first, count = cross_rows(g, side)
        message[far_ref.shape[0] :, :] = other_ref[first * g.size : (first + count) * g.size, :]

    for value in (0, 1):
        pl.when(side == value)(functools.partial(fill, value))


def pass_kernel(in_ref, *refs):
    refs[-1][...] = in_ref[...]


def far_thin_kernel(g, far_own, far_beside, after_ref, message):
    side, core = layer_index() // 2, layer_index() % 2
    half = g.size // 2

    def fill(side, source):
        first, count = cross_rows(g, side)
        start = source.shape[0] - (count + first) * g.size
        row_of = lambda row: pl.multiple_of(start + row * g.size + half * core, half)
        pack(g, 1 - side, FAR_THIN, source, row_of, (1 - side) * (g.offsets - g.slab), half, message)

    for value in (0, 1):
        for held, source in ((True, far_own), (False, far_beside)):
            here = jnp.logical_and(side == value, (core == 1 - value) == held)
            pl.when(here)(functools.partial(fill, value, source))


def fill_pair(g, core, slabs, pair):
    cols = g.slab * g.size
    for q, slab in enumerate(slabs):
        pair[:, pl.ds(pl.multiple_of((core ^ q) * cols, cols), cols)] = slab[...]


def place_parts(g, dst, at, height, t, side, parts):
    shift = t - g.pair * side
    values, done = [], 0
    for lo, hi, load in parts:
        lo, hi = max(lo, done - shift), min(hi, g.span - shift)
        if lo >= hi:
            continue
        if lo + shift > done:
            values.append(jnp.zeros((height, (lo + shift - done) * g.size), dst.dtype))
        values.append(load(lo, hi))
        done = hi + shift
    if done < g.span:
        values.append(jnp.zeros((height, (g.span - done) * g.size), dst.dtype))
    dst[pl.ds(at, height), :] = jnp.concatenate(values, axis=1) if len(values) > 1 else values[0]


def left_rows(g, dst, inner_rows, rows, band, band_first, lead, limit):
    runs = []
    for k, t in enumerate(inner_rows):
        offset = None if t is None else t - k
        if runs and runs[-1][0] == offset:
            runs[-1][2] = k + 1
        else:
            runs.append([offset, k, k + 1])
    for n, i in enumerate(rows):
        for offset, lo, hi in runs:
            shift = hi if offset is None else i - g.reach_low - offset + lead
            place_row(
                dst, n * g.size, lo, band, (band_first + n) * g.size, g.size, lo, hi, shift, g.size, limit
            )


def window_of(g, core, inner, col, cols):
    start = pl.multiple_of((core * g.slab + col) * g.size, 2 * g.size)
    return inner[:, pl.ds(start, cols * g.size)]


def dot(left, right):
    return jnp.dot(left, right, preferred_element_type=jnp.float32)


def own_columns(g, product, n):
    return product[n * g.size : (n + 1) * g.size, n * g.size : (n + g.slab) * g.size]


def by_side(side, values):
    return jnp.where(side == 0, values[0], values[1])


def group_first(g, side, name):
    return by_side(side, [g.first(value, name) for value in (0, 1)])


def message_part(g, side, name, t, piece, height):
    places, _, _ = g.layout(side, name)
    if t not in places:
        return []
    slot, col, lo, hi = places[t]
    rows = slice(slot * height, (slot + 1) * height)
    return [(lo, hi, lambda a, b: piece[rows, (col + a - lo) * g.size : (col + b - lo) * g.size])]


def pair_part(g, pair_index, ref, row, height):
    base = g.pair * pair_index
    return (
        base,
        base + g.pair,
        lambda a, b: ref[pl.ds(row, height), (a - base) * g.size : (b - base) * g.size],
    )


def pick(condition, first, second, out):
    pl.when(condition)(lambda: out.__setitem__(..., first[...]))
    pl.when(jnp.logical_not(condition))(lambda: out.__setitem__(..., second[...]))


def group_rows(g, side, name):
    first = g.first(side, name)
    return range(first, first + g.group(name)[0])


class Slabs:
    def __init__(self, g, layer, slabs):
        self.width, self.slabs, self.layer = g.slab * g.size, slabs, layer

    def __getitem__(self, at):
        rows, cols = at
        found = []
        for place in range(len(self.slabs)):
            lo, hi = max(cols.start, place * self.width), min(cols.stop, (place + 1) * self.width)
            if lo < hi:
                here = slice(lo - place * self.width, hi - place * self.width)
                found.append(self.slabs[self.layer ^ place][rows, here])
        return found[0] if len(found) == 1 else jnp.concatenate(found, axis=1)


def early_kernel(g, *refs):
    owns, thins = refs[:4], refs[4:6]
    inner, sum_a, late_a, left_a = refs[6:]
    side, core = layer_index() // 2, layer_index() % 2

    def gather(layer):
        side, core = layer // 2, layer % 2
        band, pair = Slabs(g, layer, owns), Slabs(g, core, thins)
        near = g.reached(step_of(side, NEAR_THIN))
        early, late = (g.inner_rows(side, part) for part in ("early", "late"))
        for k, t in enumerate(early):
            if 0 <= t < g.rows:
                source, row, lead, limit = band, t, 0, g.offsets
            else:
                source, row, lead, limit = pair, t - near[0], g.pair * side, g.pair
            rows = slice(row * g.size, (row + 1) * g.size)
            part = (lead, lead + limit, lambda a, b, source=source, rows=rows, lead=lead: source[
                rows, (a - lead) * g.size : (b - lead) * g.size
            ])
            place_parts(g, inner, k * g.size, g.size, t, side, [part])
        rows = group_rows(g, side, "A")
        for left, inner_rows in ((left_a, early), (late_a, late)):
            left_rows(g, left, inner_rows, rows, band, rows[0], 0, g.offsets)

    for value in range(g.layers):
        pl.when(layer_index() == value)(functools.partial(gather, value))
    col, (_, cols) = group_first(g, side, "A"), g.group("A")
    sum_a[...] = dot(left_a[...], window_of(g, core, inner, col, cols))


def square_of(g, name, side, core, keep, lefts, inners, product=0.0):
    first, (_, cols) = group_first(g, side, name), g.group(name)
    for left, inner in zip(lefts, inners):
        product = product + dot(left[...], window_of(g, core, inner, first, cols))
    return lambda n: (own_columns(g, product, n) * keep[pl.ds(first + n, 1), :]).astype(jnp.bfloat16)


def late_kernel(g, keep, *refs):
    crossed, wides, wide_fars = (refs[2 * n : 2 * n + 2] for n in range(3))
    total, left, square, inner = refs[6:]
    layer = layer_index()
    side, core = layer // 2, layer % 2
    half = g.size // 2

    def slab_parts(side, core, slabs, row, height):
        base = g.pair * (1 - side)
        parts = []
        for c in (0, 1):
            lo, slab = base + c * g.slab, slabs[core ^ c]
            parts.append((lo, lo + g.slab, lambda a, b, lo=lo, slab=slab: slab[
                row : row + height, (a - lo) * g.size : (b - lo) * g.size
            ]))
        return parts

    def gather(layer):
        side, core = layer // 2, layer % 2
        near = g.reached(step_of(side, NEAR_WIDE))
        tail = wide_fars[0].shape[0] - g.far * g.size
        for k, t in enumerate(g.inner_rows(side, "late")):
            if t is None:
                inner[k * g.size : (k + 1) * g.size, :] = jnp.zeros((g.size, inner.shape[1]), inner.dtype)
                continue
            if t in near:
                name, pieces, slabs, row = NEAR_WIDE, wides, crossed, (t - near[0]) * g.size
            else:
                name, pieces, slabs = FAR_WIDE, wide_fars, wide_fars
                row = tail + (t - step_of(side, FAR_WIDE) * g.rows - cross_rows(g, side)[0]) * g.size
            for q, piece in enumerate(pieces):
                at = half * (core ^ q)
                parts = message_part(g, side, name, t, piece, half)
                parts += slab_parts(side, core, slabs, row + at, half)
                parts.sort(key=lambda part: part[0])
                place_parts(g, inner, k * g.size + at, half, t, side, parts)

    for value in range(g.layers):
        pl.when(layer == value)(functools.partial(gather, value))
    row_of = square_of(g, "A", side, core, keep, [left], [inner], total[...])
    for n in range(g.group("A")[0]):
        square[n * g.size : (n + 1) * g.size, :] = row_of(n)


def sum_kernel(g, *refs):
    owns, (early, late, out, far_left, early_left, late_left) = refs[:4], refs[4:]
    side, core = layer_index() // 2, layer_index() % 2

    def fill(layer):
        side = layer // 2
        rows = group_rows(g, side, "B")
        for left, part in ((early_left, "early"), (late_left, "late"), (far_left, "far")):
            inner_rows = g.inner_rows(side, part)
            left_rows(g, left, inner_rows, rows, Slabs(g, layer, owns), rows[0], 0, g.offsets)

    for value in range(g.layers):
        pl.when(layer_index() == value)(functools.partial(fill, value))
    first, (_, cols) = group_first(g, side, "B"), g.group("B")
    out[...] = dot(early_left[...], window_of(g, core, early, first, cols))
    out[...] += dot(late_left[...], window_of(g, core, late, first, cols))


def square_kernel(g, keep, far, far_beside, total, far_left, *refs):
    square, inner = refs
    side, core = layer_index() // 2, layer_index() % 2
    half = g.size // 2

    def gather(side):
        for k, t in enumerate(g.inner_rows(side, "far")):
            for q, piece in enumerate((far, far_beside)):
                at = pl.multiple_of(k * g.size + half * (core ^ q), half)
                parts = [] if t is None else message_part(g, side, FAR_THIN, t, piece, half)
                place_parts(g, inner, at, half, t or 0, side, parts)

    for value in (0, 1):
        pl.when(side == value)(functools.partial(gather, value))
    row_of = square_of(g, "B", side, core, keep, [far_left], [inner], total[...])
    for n in range(g.group("B")[0]):
        square[n * g.size : (n + 1) * g.size, :] = row_of(n)


def band_rows(g, side, name):
    return pl.ds(pl.multiple_of(group_first(g, side, name) * g.size, 2 * g.size), g.group(name)[0] * g.size)


def block_rows(g, t):
    return pl.ds(pl.multiple_of(t * g.size, g.size), g.size)


def early_span(g, part):
    spans = []
    for side in (0, 1):
        rows, pair = (range(g.rows), side) if part == "own" else (group_rows(g, 1 - side, part), 1 - side)
        lo = rows[0] - g.reach_low + g.pair * pair
        hi = rows[-1] - g.reach_low + g.pair * (pair + 1)
        met = [k for k, t in enumerate(g.inner_rows(side, "early")) if lo <= t < hi]
        spans.append((even_down(met[0]), met[-1] + 1))
    count = even_up(max(hi - lo for lo, hi in spans))
    total = len(g.inner_rows(0, "early"))
    return [min(lo, total - count) for lo, _ in spans], count


def far_span(g, part):
    spans = []
    for side in (0, 1):
        rows = group_rows(g, 1 - side, part)
        lo = rows[0] - g.reach_low + g.pair * (1 - side)
        hi = rows[-1] - g.reach_low + g.pair * (2 - side)
        met = [k for k, t in enumerate(g.inner_rows(side, "far")) if t is not None and lo <= t < hi]
        spans.append((even_down(met[0]), met[-1] + 1) if met else (0, 0))
    count = even_up(max(hi - lo for lo, hi in spans))
    return [min(lo, g.inner_count("far") - count) for lo, _ in spans], count


def cubic_left(g, side, part, rows, band, band_first, lefts):
    pair = side if part == "own" else 1 - side
    starts, count = early_span(g, part)
    lists = [g.inner_rows(side, "early")[starts[side] : starts[side] + count]]
    if part == "own":
        lists.append(g.inner_rows(side, "late"))
    else:
        starts, count = far_span(g, part)
        lists.append(g.inner_rows(side, "far")[starts[side] : starts[side] + count])
    for dst, inner_rows in zip(lefts, lists):
        left_rows(g, dst, inner_rows, rows, band, band_first, g.pair * pair, g.pair)


def cubic_right(g, side, part, inners):
    rights = []
    for inner, span in zip(inners, (early_span, far_span)):
        if span == far_span and part == "own":
            rights.append(inner)
            continue
        starts, count = span(g, part)
        start = pl.multiple_of(by_side(side, starts) * g.size, 2 * g.size)
        rights.append(inner.at[pl.ds(start, count * g.size), :])
    return rights


def left_scratch(g, part, count):
    sizes = [early_span(g, part)[1], g.inner_count("late") if part == "own" else far_span(g, part)[1]]
    return [pltpu.VMEM((count * g.size, n * g.size), jnp.bfloat16) for n in sizes]


def cubic_kernel(g, keep, *refs):
    squares, inners, (out, band, own, *lefts) = refs[:4], refs[4:6], refs[6:]
    layer = layer_index()
    side, core = layer // 2, layer % 2
    cols = g.slab * g.size
    for n, name in enumerate("AB"):
        rows = band_rows(g, side, name)
        own[rows, :] = squares[2 * n][...]
        for q in range(2):
            column = pl.ds(pl.multiple_of((core ^ q) * cols, cols), cols)
            band[rows, column] = squares[2 * n + q][...]
    rights = cubic_right(g, side, "own", inners)
    size = (g.rows + 1) // 2
    for n, first in enumerate(range(0, g.rows, size)):
        rows = range(first, min(first + size, g.rows))
        col = even_down(first)
        width = even_up(rows[-1] + g.slab) - col
        used = lefts[2 * n : 2 * n + 2]
        for value in (0, 1):
            pl.when(side == value)(functools.partial(cubic_left, g, value, "own", rows, band, first, used))
        product = sum(
            dot(left[: len(rows) * g.size, :], window_of(g, core, right, col, width))
            for left, right in zip(used, rights)
        )
        for k, t in enumerate(rows):
            at = (t - col) * g.size
            here = slice(t * g.size, (t + 1) * g.size)
            out[here, :] = 3.0 * own[here, :].astype(jnp.float32) - 2.0 * (
                product[k * g.size : (k + 1) * g.size, at : at + cols] * keep[t : t + 1, :]
            )


def other_part(g, layer, name, squares, inners, band, lefts):
    side, core = layer // 2, layer % 2
    cols = g.slab * g.size
    _, width = g.group(name)
    for q in range(2):
        band[:, pl.ds(pl.multiple_of((core ^ q) * cols, cols), cols)] = squares[q][...]
    for value in (0, 1):
        rows = group_rows(g, 1 - value, name)
        pl.when(side == value)(functools.partial(cubic_left, g, value, name, rows, band, 0, lefts))
    first = group_first(g, 1 - side, name)
    rights = cubic_right(g, side, name, inners)
    return first, sum(
        dot(left[...], window_of(g, core, right, first, width)) for left, right in zip(lefts, rights)
    )


def slab_early(g, slab):
    side = 1 - slab // 2
    rows = group_rows(g, 1 - side, "B")
    early = g.inner_rows(side, "early")
    lo, hi = rows[0] - g.reach_low + g.slab * slab, rows[-1] - g.reach_low + g.slab * (slab + 1)
    met = [k for k, t in enumerate(early) if lo <= t < hi]
    count = even_up(len(rows) + g.slab - 1)
    return min(even_down(met[0]), len(early) - count), count


def slab_rights(g, slab, early, far, out):
    side, core = layer_index() // 2, layer_index() % 2
    _, width = g.group("B")
    first = group_first(g, 1 - side, "B")
    start, count = jnp.int32(0), slab_early(g, 0)[1]
    for value in range(g.layers):
        start = jnp.where(slab == value, slab_early(g, value)[0], start)
    far_starts, far_count = far_span(g, "B")
    split = count * g.size
    at = lambda start, count: pl.ds(pl.multiple_of(start * g.size, 2 * g.size), count * g.size)
    out[:split, :] = window_of(g, core, early.at[at(start, count), :], first, width)
    out[split:, :] = window_of(g, core, far.at[at(by_side(side, far_starts), far_count), :], first, width)


def slab_left(g, slab, square, left):
    far_starts, far_count = far_span(g, "B")

    def gather(slab):
        here = 1 - slab // 2
        start, count = slab_early(g, slab)
        inner_rows = g.inner_rows(here, "early")[start : start + count]
        inner_rows = inner_rows + g.inner_rows(here, "far")[far_starts[here] : far_starts[here] + far_count]
        left_rows(g, left, inner_rows, group_rows(g, 1 - here, "B"), square, 0, g.slab * slab, g.slab)

    for value in range(g.layers):
        pl.when(slab == value)(functools.partial(gather, value))


def other_kernel(g, keep, *refs):
    squares, inners, (partial, out, straight, beside, band, *lefts) = refs[:2], refs[2:4], refs[4:]
    first, product = other_part(g, layer_index(), "A", squares, inners, band, lefts)
    for n in range(g.group("A")[0]):
        out[n * g.size : (n + 1) * g.size, :] = partial[block_rows(g, first + n), :] - 2.0 * (
            own_columns(g, product, n) * keep[pl.ds(first + n, 1), :]
        )
    for q, right in ((2, straight), (3, beside)):
        slab_rights(g, layer_index() ^ q, *inners, right)


def slab_kernel(g, keep, square, right, partial, out, left):
    slab_left(g, layer_index() ^ 2, square, left)
    first = group_first(g, 1 - layer_index() // 2, "B")
    product = dot(left[...], right[...])
    for n in range(g.group("B")[0]):
        out[n * g.size : (n + 1) * g.size, :] = partial[block_rows(g, first + n), :] - 2.0 * (
            own_columns(g, product, n) * keep[pl.ds(first + n, 1), :]
        )


def last_kernel(g, keep, square, right, partial, done, out, rows, sems, left):
    side = layer_index() // 2
    copies = [pltpu.make_async_copy(done, out.at[band_rows(g, 1 - side, "A"), :], sems.at[0])]
    copies[0].start()
    slab_left(g, layer_index() ^ 3, square, left)
    first, count = group_first(g, 1 - side, "B"), g.group("B")[0]
    step = count // 2
    for begin in range(0, count, step):
        here = slice(begin * g.size, (begin + step) * g.size)
        part = dot(left[here, :], right[...])
        for n in range(begin, begin + step):
            value = part[(n - begin) * g.size : (n - begin + 1) * g.size, n * g.size : (n + g.slab) * g.size]
            row = slice(n * g.size, (n + 1) * g.size)
            rows[row, :] = partial[row, :] - 2.0 * (value * keep[pl.ds(first + n, 1), :])
        to = pl.ds(pl.multiple_of((first + begin) * g.size, g.size), step * g.size)
        copies.append(pltpu.make_async_copy(rows.at[here, :], out.at[to, :], sems.at[len(copies)]))
        copies[-1].start()
    for copy in copies:
        copy.wait()


def call(kernel, out_shape, scratch, *args, after=(), placed=(), place=VMEM):
    specs = [VMEM] * len(args) + [pl.BlockSpec(memory_space=pl.ANY)] * len(after) + [HBM] * len(placed)
    return pl.pallas_call(
        kernel,
        out_shape=out_shape,
        in_specs=specs,
        out_specs=jax.tree.map(lambda _: place, out_shape),
        scratch_shapes=scratch,
        compiler_params=pltpu.CompilerParams(vmem_limit_bytes=LIMIT),
        cost_estimate=pl.CostEstimate(flops=0, bytes_accessed=0, transcendentals=0),
    )(*args, *after, *placed)


def body(density, pattern):
    layers, ring = lax.axis_size("layer"), lax.axis_size("row")
    g = Geometry(*density.shape, *pattern.shape, layers)
    rows_dev, cols = density.shape
    bf16 = functools.partial(jax.ShapeDtypeStruct, dtype=jnp.bfloat16)
    scratch = lambda *shape: pltpu.VMEM(shape, jnp.bfloat16)

    def swap(value, bit):
        return lax.ppermute(value, "layer", [(s, s ^ bit) for s in range(layers)])

    def send(value, name, keep=lambda layer, row: True):
        pairs = []
        for l in range(layers):
            step = step_of(l // 2, name)
            pairs += [
                (l * ring + r, l * ring + (r - step) % ring) for r in range(ring) if keep(l, r)
            ]
        return lax.ppermute(value, ("layer", "row"), pairs)

    half_rows, slab = rows_dev // 2, (rows_dev, cols)
    cross_shape = (g.far * g.size, cols)

    def put_after(value, *after):
        return call(pass_kernel, bf16(value.shape), [], value, after=after)

    sources = [pltpu.with_memory_space_constraint(value, pltpu.HBM) for value in (density, pattern.T)]
    masked, keep, give = call(
        functools.partial(mask_kernel, g),
        [
            bf16(slab), jax.ShapeDtypeStruct(((g.rows + 7) // 8 * 8, cols), jnp.float32),
            bf16((half_rows, cols)),
        ],
        [scratch(*slab), pltpu.VMEM(pattern.T.shape, pattern.dtype), pltpu.SemaphoreType.DMA((2,))],
        placed=sources,
    )
    thin = send(masked, NEAR_THIN)
    other = swap(masked, 2)
    beside = swap(masked, 1)
    far_shape = message_shape(g, FAR_WIDE)
    head_shape = (far_shape[0] - cross_shape[0], cols)
    wide, far_wide = call(
        functools.partial(pack_kernel, g),
        [bf16(message_shape(g, NEAR_WIDE)), bf16(head_shape)], [scratch(half_rows, 2 * cols)],
        masked, swap(give, 1),
    )
    relayed = send(wide, FAR_WIDE, lambda layer, row: row % 2 != layer // 2)
    crossed = swap(thin, 2)
    wide, far_wide = call(
        functools.partial(relay_kernel, g),
        [bf16(wide.shape), bf16(far_shape)], [], wide, relayed, far_wide, other, after=(thin,),
    )
    wide = lax.ppermute(wide, "row", [(r, r ^ 1) for r in range(ring)])
    far_wide = send(far_wide, FAR_WIDE)

    early, late, far = (g.inner_count(part) * g.size for part in ("early", "late", "far"))
    (high_a, wide_a), (high_b, wide_b) = (tuple(n * g.size for n in g.group(name)) for name in "AB")
    span = g.span * g.size
    f32 = functools.partial(jax.ShapeDtypeStruct, dtype=jnp.float32)

    slabs = (masked, beside, other, swap(other, 1))
    inner_early, sum_a, late_a = call(
        functools.partial(early_kernel, g),
        [bf16((early, span)), f32((high_a, wide_a)), bf16((high_a, late))], [scratch(high_a, early)],
        *slabs, thin, swap(thin, 1),
    )
    far_beside = swap(far_wide, 1)
    far_thin = call(
        functools.partial(far_thin_kernel, g),
        bf16(message_shape(g, FAR_THIN)), [], far_wide, far_beside, after=(sum_a,),
    )
    far_thin = swap(far_thin, 2)
    pieces = [crossed, swap(crossed, 1), wide, swap(wide, 1), far_wide, far_beside]
    square_a, inner_late = call(
        functools.partial(late_kernel, g),
        [bf16((high_a, cols)), bf16((late, span))],
        [],
        keep, *pieces, sum_a, late_a,
    )
    across_a, beside_a = swap(square_a, 2), swap(square_a, 1)
    sum_b, far_b = call(
        functools.partial(sum_kernel, g),
        [f32((high_b, wide_b)), bf16((high_b, far))], [scratch(high_b, early), scratch(high_b, late)],
        *slabs, inner_early, inner_late,
    )
    square_b, inner_far = call(
        functools.partial(square_kernel, g),
        [bf16((high_b, cols)), bf16((far, span))], [],
        keep, far_thin, swap(far_thin, 1), sum_b, far_b,
    )
    across_b, beside_b = swap(square_b, 2), swap(square_b, 1)
    partial = call(
        functools.partial(cubic_kernel, g),
        f32(slab),
        [scratch(rows_dev, 2 * cols), scratch(*slab)] + 2 * left_scratch(g, "own", (g.rows + 1) // 2),
        keep, square_a, beside_a, square_b, beside_b, inner_early, inner_late,
    )
    meet = (slab_early(g, 0)[1] + far_span(g, "B")[1]) * g.size
    done, straight, next_to = call(
        functools.partial(other_kernel, g),
        [f32((high_a, cols)), bf16((meet, wide_b)), bf16((meet, wide_b))],
        [scratch(high_a, 2 * cols)] + left_scratch(g, "A", g.group("A")[0]),
        keep, across_a, swap(across_a, 1), inner_early, inner_far, partial,
    )
    across_b = put_after(across_b, done)
    left = scratch(high_b, meet)
    partial = call(
        functools.partial(slab_kernel, g), f32((high_b, cols)), [left], keep, across_b, straight, partial
    )
    return call(
        functools.partial(last_kernel, g),
        f32(slab),
        [pltpu.VMEM((high_b, cols), jnp.float32), pltpu.SemaphoreType.DMA((3,)), left],
        keep, swap(across_b, 1), next_to, partial, done,
        place=HBM,
    )


def solution(mesh):
    placed = (P("row", "layer"), P("row", "layer"))
    return jax.shard_map(
        body, mesh=mesh, in_specs=placed, out_specs=P("row", "layer"), check_vma=False
    )
```

```python
import functools

import jax
import jax.numpy as jnp
from jax import lax
from jax.experimental import pallas as pl
from jax.experimental.pallas import tpu as pltpu
from jax.sharding import PartitionSpec as P

VMEM = pl.BlockSpec(memory_space=pltpu.VMEM)
HBM = pl.BlockSpec(memory_space=pltpu.HBM)
LIMIT = 12 * 1024 * 1024


class Geometry:
    def __init__(self, rows_dev, slab_cols, block_rows, slab_offsets, layers):
        self.rows, self.slab = block_rows, slab_offsets
        self.size = rows_dev // block_rows
        self.layers = layers
        self.offsets = slab_offsets * layers
        self.half = self.offsets // 2
        self.pair = 2 * slab_offsets
        self.reach_low, self.reach_high = self.half, self.half - 1
        self.columns = self.pair + block_rows - 1
        self.span = even_up(self.columns)
        self.far = even_up(max(len(self.reached(step)) for step in (-2, 2)))

    def needed(self, t, side):
        lo, hi = self.pair * side - t, self.pair * side - t + self.columns
        if t < 0:
            lo = max(lo, -t)
        if t >= self.rows:
            hi = min(hi, self.offsets - (t - self.rows + 1))
        lo, hi = max(lo, 0), min(hi, self.offsets)
        return lo, max(lo, hi)

    def reached(self, step):
        first = step * self.rows
        return [
            t
            for t in range(first, first + self.rows)
            if -self.reach_low <= t < self.rows + self.reach_high
        ]

    def inner_rows(self, side, part):
        if part == "early":
            return sorted(list(range(self.rows)) + self.reached(step_of(side, NEAR_THIN)))
        rows = []
        for name in ([NEAR_WIDE, FAR_WIDE] if part == "late" else [FAR_THIN]):
            reached = self.reached(step_of(side, name))
            rows += reached + [None] * (0 if name[0] == "near" else self.far - len(reached))
        return rows

    def inner_count(self, part):
        return len(self.inner_rows(0, part))

    def group(self, name):
        first = even_up(2 * self.rows // 5)
        count = first if name == "A" else self.rows - first
        return count, even_up(count - 1 + self.slab)

    def first(self, side, name):
        return 0 if (side == 0) == (name == "A") else self.rows - self.group(name)[0]

    def layout(self, side, name):
        step = step_of(side, name)
        found = []
        for t in self.reached(step):
            lo, hi = self.needed(t, side)
            lo, hi = max(lo, self.pair * side), min(hi, self.pair * (side + 1))
            if hi > lo:
                if name != FAR_WIDE:
                    lo, hi = even_down(lo), even_up(hi)
                found.append((hi - lo, t, lo, hi))
        found.sort(reverse=True)
        if name == FAR_WIDE:
            places, used = {}, []
            for width, t, lo, hi in found:
                free = [n for n, taken in enumerate(used) if taken + width <= self.slab]
                slot = free[0] if free else len(used)
                used += [] if free else [0]
                places[t] = (slot, used[slot], lo, hi)
                used[slot] += width
            return places, len(used), max(used)
        slots = (len(found) + 1) // 2
        used = [0] * slots
        places = {}
        for n, (width, t, lo, hi) in enumerate(found):
            slot = n if n < slots else 2 * slots - 1 - n
            places[t] = (slot, used[slot], lo, hi)
            used[slot] += width
        return places, slots, max(used)


def even_down(n):
    return n // 2 * 2


def even_up(n):
    return (n + 1) // 2 * 2


def step_of(side, name):
    sign = 1 if (name[1] == "thin") == (side == 0) else -1
    return sign * (1 if name[0] == "near" else 2)


NEAR_WIDE, NEAR_THIN = ("near", "wide"), ("near", "thin")
FAR_WIDE, FAR_THIN = ("far", "wide"), ("far", "thin")


def message_shape(g, name):
    layouts = [g.layout(side, name) for side in (0, 1)]
    rows, cols = max(f[1] for f in layouts) * g.size // 2, max(f[2] for f in layouts) * g.size
    if name == FAR_WIDE:
        return rows + g.far * g.size, g.slab * g.size
    return rows, cols


def layer_index():
    return lax.axis_index("layer").astype(jnp.int32)


def mask_kernel(g, density_ref, pattern_ref, out_ref, keep, give, density, pattern, sems):
    copies = [
        pltpu.make_async_copy(source, target, sems.at[n])
        for n, (source, target) in enumerate(((pattern_ref, pattern), (density_ref, density)))
    ]
    for copy in copies:
        copy.start()
    copies[0].wait()
    offsets, cols = pattern.shape[0], keep.shape[1]
    block = lax.broadcasted_iota(jnp.int32, (offsets, cols), 1) // g.size
    row = lax.broadcasted_iota(jnp.int32, (offsets, cols), 0)
    spread = jnp.where(block == row, 1.0, 0.0).astype(jnp.float32)
    keep[: g.rows, :] = lax.dot_general(
        pattern[...].astype(jnp.float32), spread, (((0,), (0,)), ((), ())),
        preferred_element_type=jnp.float32,
    )
    keep[g.rows :, :] = jnp.zeros((keep.shape[0] - g.rows, cols), keep.dtype)
    copies[1].wait()
    half = g.size // 2
    for t in range(g.rows):
        rows = slice(t * g.size, (t + 1) * g.size)
        out_ref[rows, :] = density[rows, :] * keep[t : t + 1, :].astype(jnp.bfloat16)
        start = pl.multiple_of(t * g.size + half * (1 - layer_index() % 2), half)
        give[t * half : (t + 1) * half, :] = out_ref[pl.ds(start, half), :]


def cross_rows(g, side):
    rows = [t - step_of(side, FAR_WIDE) * g.rows for t in g.reached(step_of(side, FAR_WIDE))]
    count = g.far
    return min(rows[0], g.rows - count), count


def place_row(dst_ref, dst_row, dst_lo, src_ref, src_row, height, lo, hi, shift, size, limit):
    first, last = max(lo, shift), min(hi, limit + shift)
    base = dst_lo - lo
    rows = slice(dst_row, dst_row + height)
    if first >= last:
        dst_ref[rows, dst_lo * size : (hi + base) * size] = jnp.zeros(
            (height, (hi - lo) * size), dst_ref.dtype
        )
        return
    value = src_ref[src_row : src_row + height, (first - shift) * size : (last - shift) * size]
    parts = []
    if first > lo:
        parts.append(jnp.zeros((height, (first - lo) * size), dst_ref.dtype))
    parts.append(value)
    if hi > last:
        parts.append(jnp.zeros((height, (hi - last) * size), dst_ref.dtype))
    if len(parts) > 1:
        value = jnp.concatenate(parts, axis=1)
    dst_ref[rows, dst_lo * size : (hi + base) * size] = value


def pack(g, side, name, source, row_of, lead, height, out):
    places, slots, _ = g.layout(side, name)
    filled = [0] * slots
    for t, (slot, col, lo, hi) in places.items():
        out[slot * height : (slot + 1) * height, col * g.size : (col + hi - lo) * g.size] = source[
            pl.ds(row_of(t - step_of(side, name) * g.rows), height), (lo - lead) * g.size : (hi - lead) * g.size
        ]
        filled[slot] = max(filled[slot], col + hi - lo)
    for slot, count in enumerate(filled):
        if count * g.size < out.shape[1]:
            out[slot * height : (slot + 1) * height, count * g.size :] = jnp.zeros(
                (height, out.shape[1] - count * g.size), out.dtype
            )
    if slots * height < out.shape[0] and name != FAR_WIDE:
        out[slots * height :, :] = jnp.zeros((out.shape[0] - slots * height, out.shape[1]), out.dtype)


def fill_near(g, core, own, given, near):
    half, cols = g.size // 2, g.slab * g.size
    here, there = (pl.ds(pl.multiple_of(c * cols, cols), cols) for c in (core, 1 - core))
    for t in range(g.rows):
        src = pl.multiple_of(t * g.size + half * core, half)
        near[t * half : (t + 1) * half, here] = own[pl.ds(src, half), :]
    near[:, there] = given[...]


def pack_kernel(g, own_ref, given_ref, wide, far, near):
    side, core = layer_index() // 2, layer_index() % 2
    half = g.size // 2
    fill_near(g, core, own_ref, given_ref, near)

    def fill(side):
        for name, out in ((NEAR_WIDE, wide), (FAR_WIDE, far)):
            pack(g, side, name, near, lambda row: row * half, side * g.pair, half, out)

    for value in (0, 1):
        pl.when(side == value)(functools.partial(fill, value))


def relay_kernel(g, own_ref, relayed_ref, far_ref, other_ref, after_ref, out_ref, message):
    side, row = layer_index() // 2, lax.axis_index("row")
    pick((row % 2) == side, own_ref, relayed_ref, out_ref)
    message[: far_ref.shape[0], :] = far_ref[...]

    def fill(side):
        first, count = cross_rows(g, side)
        message[far_ref.shape[0] :, :] = other_ref[first * g.size : (first + count) * g.size, :]

    for value in (0, 1):
        pl.when(side == value)(functools.partial(fill, value))


def pass_kernel(in_ref, *refs):
    refs[-1][...] = in_ref[...]


def far_thin_kernel(g, far_own, far_beside, after_ref, message):
    side, core = layer_index() // 2, layer_index() % 2
    half = g.size // 2

    def fill(side, source):
        first, count = cross_rows(g, side)
        start = source.shape[0] - (count + first) * g.size
        row_of = lambda row: pl.multiple_of(start + row * g.size + half * core, half)
        pack(g, 1 - side, FAR_THIN, source, row_of, (1 - side) * (g.offsets - g.slab), half, message)

    for value in (0, 1):
        for held, source in ((True, far_own), (False, far_beside)):
            here = jnp.logical_and(side == value, (core == 1 - value) == held)
            pl.when(here)(functools.partial(fill, value, source))


def fill_pair(g, core, slabs, pair):
    cols = g.slab * g.size
    for q, slab in enumerate(slabs):
        pair[:, pl.ds(pl.multiple_of((core ^ q) * cols, cols), cols)] = slab[...]


def place_parts(g, dst, at, height, t, side, parts):
    shift = t - g.pair * side
    values, done = [], 0
    for lo, hi, load in parts:
        lo, hi = max(lo, done - shift), min(hi, g.span - shift)
        if lo >= hi:
            continue
        if lo + shift > done:
            values.append(jnp.zeros((height, (lo + shift - done) * g.size), dst.dtype))
        values.append(load(lo, hi))
        done = hi + shift
    if done < g.span:
        values.append(jnp.zeros((height, (g.span - done) * g.size), dst.dtype))
    dst[pl.ds(at, height), :] = jnp.concatenate(values, axis=1) if len(values) > 1 else values[0]


def left_rows(g, dst, inner_rows, rows, band, band_first, lead, limit):
    runs = []
    for k, t in enumerate(inner_rows):
        offset = None if t is None else t - k
        if runs and runs[-1][0] == offset:
            runs[-1][2] = k + 1
        else:
            runs.append([offset, k, k + 1])
    for n, i in enumerate(rows):
        for offset, lo, hi in runs:
            shift = hi if offset is None else i - g.reach_low - offset + lead
            place_row(
                dst, n * g.size, lo, band, (band_first + n) * g.size, g.size, lo, hi, shift, g.size, limit
            )


def window_of(g, core, inner, col, cols):
    start = pl.multiple_of((core * g.slab + col) * g.size, 2 * g.size)
    return inner[:, pl.ds(start, cols * g.size)]


def dot(left, right):
    return jnp.dot(left, right, preferred_element_type=jnp.float32)


def own_columns(g, product, n):
    return product[n * g.size : (n + 1) * g.size, n * g.size : (n + g.slab) * g.size]


def by_side(side, values):
    return jnp.where(side == 0, values[0], values[1])


def group_first(g, side, name):
    return by_side(side, [g.first(value, name) for value in (0, 1)])


def message_part(g, side, name, t, piece, height):
    places, _, _ = g.layout(side, name)
    if t not in places:
        return []
    slot, col, lo, hi = places[t]
    rows = slice(slot * height, (slot + 1) * height)
    return [(lo, hi, lambda a, b: piece[rows, (col + a - lo) * g.size : (col + b - lo) * g.size])]


def pair_part(g, pair_index, ref, row, height):
    base = g.pair * pair_index
    return (
        base,
        base + g.pair,
        lambda a, b: ref[pl.ds(row, height), (a - base) * g.size : (b - base) * g.size],
    )


def pick(condition, first, second, out):
    pl.when(condition)(lambda: out.__setitem__(..., first[...]))
    pl.when(jnp.logical_not(condition))(lambda: out.__setitem__(..., second[...]))


def group_rows(g, side, name):
    first = g.first(side, name)
    return range(first, first + g.group(name)[0])


class Slabs:
    def __init__(self, g, layer, slabs):
        self.width, self.slabs, self.layer = g.slab * g.size, slabs, layer

    def __getitem__(self, at):
        rows, cols = at
        found = []
        for place in range(len(self.slabs)):
            lo, hi = max(cols.start, place * self.width), min(cols.stop, (place + 1) * self.width)
            if lo < hi:
                here = slice(lo - place * self.width, hi - place * self.width)
                found.append(self.slabs[self.layer ^ place][rows, here])
        return found[0] if len(found) == 1 else jnp.concatenate(found, axis=1)


def early_kernel(g, *refs):
    owns, thins = refs[:4], refs[4:6]
    inner, sum_a, late_a, left_a = refs[6:]
    side, core = layer_index() // 2, layer_index() % 2

    def gather(layer):
        side, core = layer // 2, layer % 2
        band, pair = Slabs(g, layer, owns), Slabs(g, core, thins)
        near = g.reached(step_of(side, NEAR_THIN))
        early, late = (g.inner_rows(side, part) for part in ("early", "late"))
        for k, t in enumerate(early):
            if 0 <= t < g.rows:
                source, row, lead, limit = band, t, 0, g.offsets
            else:
                source, row, lead, limit = pair, t - near[0], g.pair * side, g.pair
            rows = slice(row * g.size, (row + 1) * g.size)
            part = (lead, lead + limit, lambda a, b, source=source, rows=rows, lead=lead: source[
                rows, (a - lead) * g.size : (b - lead) * g.size
            ])
            place_parts(g, inner, k * g.size, g.size, t, side, [part])
        rows = group_rows(g, side, "A")
        for left, inner_rows in ((left_a, early), (late_a, late)):
            left_rows(g, left, inner_rows, rows, band, rows[0], 0, g.offsets)

    for value in range(g.layers):
        pl.when(layer_index() == value)(functools.partial(gather, value))
    col, (_, cols) = group_first(g, side, "A"), g.group("A")
    sum_a[...] = dot(left_a[...], window_of(g, core, inner, col, cols))


def square_of(g, name, side, core, keep, lefts, inners, product=0.0):
    first, (_, cols) = group_first(g, side, name), g.group(name)
    for left, inner in zip(lefts, inners):
        product = product + dot(left[...], window_of(g, core, inner, first, cols))
    return lambda n: (own_columns(g, product, n) * keep[pl.ds(first + n, 1), :]).astype(jnp.bfloat16)


def late_kernel(g, keep, *refs):
    crossed, wides, wide_fars = (refs[2 * n : 2 * n + 2] for n in range(3))
    total, left, square, inner = refs[6:]
    layer = layer_index()
    side, core = layer // 2, layer % 2
    half = g.size // 2

    def slab_parts(side, core, slabs, row, height):
        base = g.pair * (1 - side)
        parts = []
        for c in (0, 1):
            lo, slab = base + c * g.slab, slabs[core ^ c]
            parts.append((lo, lo + g.slab, lambda a, b, lo=lo, slab=slab: slab[
                row : row + height, (a - lo) * g.size : (b - lo) * g.size
            ]))
        return parts

    def gather(layer):
        side, core = layer // 2, layer % 2
        near = g.reached(step_of(side, NEAR_WIDE))
        tail = wide_fars[0].shape[0] - g.far * g.size
        for k, t in enumerate(g.inner_rows(side, "late")):
            if t is None:
                inner[k * g.size : (k + 1) * g.size, :] = jnp.zeros((g.size, inner.shape[1]), inner.dtype)
                continue
            if t in near:
                name, pieces, slabs, row = NEAR_WIDE, wides, crossed, (t - near[0]) * g.size
            else:
                name, pieces, slabs = FAR_WIDE, wide_fars, wide_fars
                row = tail + (t - step_of(side, FAR_WIDE) * g.rows - cross_rows(g, side)[0]) * g.size
            for q, piece in enumerate(pieces):
                at = half * (core ^ q)
                parts = message_part(g, side, name, t, piece, half)
                parts += slab_parts(side, core, slabs, row + at, half)
                parts.sort(key=lambda part: part[0])
                place_parts(g, inner, k * g.size + at, half, t, side, parts)

    for value in range(g.layers):
        pl.when(layer == value)(functools.partial(gather, value))
    row_of = square_of(g, "A", side, core, keep, [left], [inner], total[...])
    for n in range(g.group("A")[0]):
        square[n * g.size : (n + 1) * g.size, :] = row_of(n)


def sum_kernel(g, *refs):
    owns, (early, late, out, far_left, early_left, late_left) = refs[:4], refs[4:]
    side, core = layer_index() // 2, layer_index() % 2

    def fill(layer):
        side = layer // 2
        rows = group_rows(g, side, "B")
        for left, part in ((early_left, "early"), (late_left, "late"), (far_left, "far")):
            inner_rows = g.inner_rows(side, part)
            left_rows(g, left, inner_rows, rows, Slabs(g, layer, owns), rows[0], 0, g.offsets)

    for value in range(g.layers):
        pl.when(layer_index() == value)(functools.partial(fill, value))
    first, (_, cols) = group_first(g, side, "B"), g.group("B")
    out[...] = dot(early_left[...], window_of(g, core, early, first, cols))
    out[...] += dot(late_left[...], window_of(g, core, late, first, cols))


def square_kernel(g, keep, far, far_beside, total, far_left, *refs):
    square, inner = refs
    side, core = layer_index() // 2, layer_index() % 2
    half = g.size // 2

    def gather(side):
        for k, t in enumerate(g.inner_rows(side, "far")):
            for q, piece in enumerate((far, far_beside)):
                at = pl.multiple_of(k * g.size + half * (core ^ q), half)
                parts = [] if t is None else message_part(g, side, FAR_THIN, t, piece, half)
                place_parts(g, inner, at, half, t or 0, side, parts)

    for value in (0, 1):
        pl.when(side == value)(functools.partial(gather, value))
    row_of = square_of(g, "B", side, core, keep, [far_left], [inner], total[...])
    for n in range(g.group("B")[0]):
        square[n * g.size : (n + 1) * g.size, :] = row_of(n)


def band_rows(g, side, name):
    return pl.ds(pl.multiple_of(group_first(g, side, name) * g.size, 2 * g.size), g.group(name)[0] * g.size)


def block_rows(g, t):
    return pl.ds(pl.multiple_of(t * g.size, g.size), g.size)


def early_span(g, part):
    spans = []
    for side in (0, 1):
        rows, pair = (range(g.rows), side) if part == "own" else (group_rows(g, 1 - side, part), 1 - side)
        lo = rows[0] - g.reach_low + g.pair * pair
        hi = rows[-1] - g.reach_low + g.pair * (pair + 1)
        met = [k for k, t in enumerate(g.inner_rows(side, "early")) if lo <= t < hi]
        spans.append((even_down(met[0]), met[-1] + 1))
    count = even_up(max(hi - lo for lo, hi in spans))
    total = len(g.inner_rows(0, "early"))
    return [min(lo, total - count) for lo, _ in spans], count


def far_span(g, part):
    spans = []
    for side in (0, 1):
        rows = group_rows(g, 1 - side, part)
        lo = rows[0] - g.reach_low + g.pair * (1 - side)
        hi = rows[-1] - g.reach_low + g.pair * (2 - side)
        met = [k for k, t in enumerate(g.inner_rows(side, "far")) if t is not None and lo <= t < hi]
        spans.append((even_down(met[0]), met[-1] + 1) if met else (0, 0))
    count = even_up(max(hi - lo for lo, hi in spans))
    return [min(lo, g.inner_count("far") - count) for lo, _ in spans], count


def cubic_left(g, side, part, rows, band, band_first, lefts):
    pair = side if part == "own" else 1 - side
    starts, count = early_span(g, part)
    lists = [g.inner_rows(side, "early")[starts[side] : starts[side] + count]]
    if part == "own":
        lists.append(g.inner_rows(side, "late"))
    else:
        starts, count = far_span(g, part)
        lists.append(g.inner_rows(side, "far")[starts[side] : starts[side] + count])
    for dst, inner_rows in zip(lefts, lists):
        left_rows(g, dst, inner_rows, rows, band, band_first, g.pair * pair, g.pair)


def cubic_right(g, side, part, inners):
    rights = []
    for inner, span in zip(inners, (early_span, far_span)):
        if span == far_span and part == "own":
            rights.append(inner)
            continue
        starts, count = span(g, part)
        start = pl.multiple_of(by_side(side, starts) * g.size, 2 * g.size)
        rights.append(inner.at[pl.ds(start, count * g.size), :])
    return rights


def left_scratch(g, part, count):
    sizes = [early_span(g, part)[1], g.inner_count("late") if part == "own" else far_span(g, part)[1]]
    return [pltpu.VMEM((count * g.size, n * g.size), jnp.bfloat16) for n in sizes]


def cubic_kernel(g, keep, *refs):
    squares, inners, (out, band, own, *lefts) = refs[:4], refs[4:6], refs[6:]
    layer = layer_index()
    side, core = layer // 2, layer % 2
    cols = g.slab * g.size
    for n, name in enumerate("AB"):
        rows = band_rows(g, side, name)
        own[rows, :] = squares[2 * n][...]
        for q in range(2):
            column = pl.ds(pl.multiple_of((core ^ q) * cols, cols), cols)
            band[rows, column] = squares[2 * n + q][...]
    rights = cubic_right(g, side, "own", inners)
    size = (g.rows + 1) // 2
    for n, first in enumerate(range(0, g.rows, size)):
        rows = range(first, min(first + size, g.rows))
        col = even_down(first)
        width = even_up(rows[-1] + g.slab) - col
        used = lefts[2 * n : 2 * n + 2]
        for value in (0, 1):
            pl.when(side == value)(functools.partial(cubic_left, g, value, "own", rows, band, first, used))
        product = sum(
            dot(left[: len(rows) * g.size, :], window_of(g, core, right, col, width))
            for left, right in zip(used, rights)
        )
        for k, t in enumerate(rows):
            at = (t - col) * g.size
            here = slice(t * g.size, (t + 1) * g.size)
            out[here, :] = 3.0 * own[here, :].astype(jnp.float32) - 2.0 * (
                product[k * g.size : (k + 1) * g.size, at : at + cols] * keep[t : t + 1, :]
            )


def other_part(g, layer, name, squares, inners, band, lefts):
    side, core = layer // 2, layer % 2
    cols = g.slab * g.size
    _, width = g.group(name)
    for q in range(2):
        band[:, pl.ds(pl.multiple_of((core ^ q) * cols, cols), cols)] = squares[q][...]
    for value in (0, 1):
        rows = group_rows(g, 1 - value, name)
        pl.when(side == value)(functools.partial(cubic_left, g, value, name, rows, band, 0, lefts))
    first = group_first(g, 1 - side, name)
    rights = cubic_right(g, side, name, inners)
    return first, sum(
        dot(left[...], window_of(g, core, right, first, width)) for left, right in zip(lefts, rights)
    )


def slab_early(g, slab):
    side = 1 - slab // 2
    rows = group_rows(g, 1 - side, "B")
    early = g.inner_rows(side, "early")
    lo, hi = rows[0] - g.reach_low + g.slab * slab, rows[-1] - g.reach_low + g.slab * (slab + 1)
    met = [k for k, t in enumerate(early) if lo <= t < hi]
    count = even_up(len(rows) + g.slab - 1)
    return min(even_down(met[0]), len(early) - count), count


def slab_rights(g, slab, early, far, out):
    side, core = layer_index() // 2, layer_index() % 2
    _, width = g.group("B")
    first = group_first(g, 1 - side, "B")
    start, count = jnp.int32(0), slab_early(g, 0)[1]
    for value in range(g.layers):
        start = jnp.where(slab == value, slab_early(g, value)[0], start)
    far_starts, far_count = far_span(g, "B")
    split = count * g.size
    at = lambda start, count: pl.ds(pl.multiple_of(start * g.size, 2 * g.size), count * g.size)
    out[:split, :] = window_of(g, core, early.at[at(start, count), :], first, width)
    out[split:, :] = window_of(g, core, far.at[at(by_side(side, far_starts), far_count), :], first, width)


def slab_left(g, slab, square, left):
    far_starts, far_count = far_span(g, "B")

    def gather(slab):
        here = 1 - slab // 2
        start, count = slab_early(g, slab)
        inner_rows = g.inner_rows(here, "early")[start : start + count]
        inner_rows = inner_rows + g.inner_rows(here, "far")[far_starts[here] : far_starts[here] + far_count]
        left_rows(g, left, inner_rows, group_rows(g, 1 - here, "B"), square, 0, g.slab * slab, g.slab)

    for value in range(g.layers):
        pl.when(slab == value)(functools.partial(gather, value))


def other_kernel(g, keep, *refs):
    squares, inners, (partial, out, straight, beside, band, *lefts) = refs[:2], refs[2:4], refs[4:]
    first, product = other_part(g, layer_index(), "A", squares, inners, band, lefts)
    for n in range(g.group("A")[0]):
        out[n * g.size : (n + 1) * g.size, :] = partial[block_rows(g, first + n), :] - 2.0 * (
            own_columns(g, product, n) * keep[pl.ds(first + n, 1), :]
        )
    for q, right in ((2, straight), (3, beside)):
        slab_rights(g, layer_index() ^ q, *inners, right)


def slab_kernel(g, keep, square, right, partial, out, left):
    slab_left(g, layer_index() ^ 2, square, left)
    first = group_first(g, 1 - layer_index() // 2, "B")
    product = dot(left[...], right[...])
    for n in range(g.group("B")[0]):
        out[n * g.size : (n + 1) * g.size, :] = partial[block_rows(g, first + n), :] - 2.0 * (
            own_columns(g, product, n) * keep[pl.ds(first + n, 1), :]
        )


def last_kernel(g, keep, square, right, partial, done, out, rows, sems, left):
    side = layer_index() // 2
    copies = [pltpu.make_async_copy(done, out.at[band_rows(g, 1 - side, "A"), :], sems.at[0])]
    copies[0].start()
    slab_left(g, layer_index() ^ 3, square, left)
    first, count = group_first(g, 1 - side, "B"), g.group("B")[0]
    step = count // 2
    for begin in range(0, count, step):
        here = slice(begin * g.size, (begin + step) * g.size)
        part = dot(left[here, :], right[...])
        for n in range(begin, begin + step):
            value = part[(n - begin) * g.size : (n - begin + 1) * g.size, n * g.size : (n + g.slab) * g.size]
            row = slice(n * g.size, (n + 1) * g.size)
            rows[row, :] = partial[row, :] - 2.0 * (value * keep[pl.ds(first + n, 1), :])
        to = pl.ds(pl.multiple_of((first + begin) * g.size, g.size), step * g.size)
        copies.append(pltpu.make_async_copy(rows.at[here, :], out.at[to, :], sems.at[len(copies)]))
        copies[-1].start()
    for copy in copies:
        copy.wait()


def call(kernel, out_shape, scratch, *args, after=(), placed=(), place=VMEM):
    specs = [VMEM] * len(args) + [pl.BlockSpec(memory_space=pl.ANY)] * len(after) + [HBM] * len(placed)
    return pl.pallas_call(
        kernel,
        out_shape=out_shape,
        in_specs=specs,
        out_specs=jax.tree.map(lambda _: place, out_shape),
        scratch_shapes=scratch,
        compiler_params=pltpu.CompilerParams(vmem_limit_bytes=LIMIT),
        cost_estimate=pl.CostEstimate(flops=0, bytes_accessed=0, transcendentals=0),
    )(*args, *after, *placed)


def body(density, pattern):
    layers, ring = lax.axis_size("layer"), lax.axis_size("row")
    g = Geometry(*density.shape, *pattern.shape, layers)
    rows_dev, cols = density.shape
    bf16 = functools.partial(jax.ShapeDtypeStruct, dtype=jnp.bfloat16)
    scratch = lambda *shape: pltpu.VMEM(shape, jnp.bfloat16)

    def swap(value, bit):
        return lax.ppermute(value, "layer", [(s, s ^ bit) for s in range(layers)])

    def send(value, name, keep=lambda layer, row: True):
        pairs = []
        for l in range(layers):
            step = step_of(l // 2, name)
            pairs += [
                (l * ring + r, l * ring + (r - step) % ring) for r in range(ring) if keep(l, r)
            ]
        return lax.ppermute(value, ("layer", "row"), pairs)

    half_rows, slab = rows_dev // 2, (rows_dev, cols)
    cross_shape = (g.far * g.size, cols)

    def put_after(value, *after):
        return call(pass_kernel, bf16(value.shape), [], value, after=after)

    sources = [pltpu.with_memory_space_constraint(value, pltpu.HBM) for value in (density, pattern.T)]
    masked, keep, give = call(
        functools.partial(mask_kernel, g),
        [
            bf16(slab), jax.ShapeDtypeStruct(((g.rows + 7) // 8 * 8, cols), jnp.float32),
            bf16((half_rows, cols)),
        ],
        [scratch(*slab), pltpu.VMEM(pattern.T.shape, pattern.dtype), pltpu.SemaphoreType.DMA((2,))],
        placed=sources,
    )
    thin = send(masked, NEAR_THIN)
    other = swap(masked, 2)
    beside = swap(masked, 1)
    far_shape = message_shape(g, FAR_WIDE)
    head_shape = (far_shape[0] - cross_shape[0], cols)
    wide, far_wide = call(
        functools.partial(pack_kernel, g),
        [bf16(message_shape(g, NEAR_WIDE)), bf16(head_shape)], [scratch(half_rows, 2 * cols)],
        masked, swap(give, 1),
    )
    relayed = send(wide, FAR_WIDE, lambda layer, row: row % 2 != layer // 2)
    crossed = swap(thin, 2)
    wide, far_wide = call(
        functools.partial(relay_kernel, g),
        [bf16(wide.shape), bf16(far_shape)], [], wide, relayed, far_wide, other, after=(thin,),
    )
    wide = lax.ppermute(wide, "row", [(r, r ^ 1) for r in range(ring)])
    far_wide = send(far_wide, FAR_WIDE)

    early, late, far = (g.inner_count(part) * g.size for part in ("early", "late", "far"))
    (high_a, wide_a), (high_b, wide_b) = (tuple(n * g.size for n in g.group(name)) for name in "AB")
    span = g.span * g.size
    f32 = functools.partial(jax.ShapeDtypeStruct, dtype=jnp.float32)

    slabs = (masked, beside, other, swap(other, 1))
    inner_early, sum_a, late_a = call(
        functools.partial(early_kernel, g),
        [bf16((early, span)), f32((high_a, wide_a)), bf16((high_a, late))], [scratch(high_a, early)],
        *slabs, thin, swap(thin, 1),
    )
    far_beside = swap(far_wide, 1)
    far_thin = call(
        functools.partial(far_thin_kernel, g),
        bf16(message_shape(g, FAR_THIN)), [], far_wide, far_beside, after=(sum_a,),
    )
    far_thin = swap(far_thin, 2)
    pieces = [crossed, swap(crossed, 1), wide, swap(wide, 1), far_wide, far_beside]
    square_a, inner_late = call(
        functools.partial(late_kernel, g),
        [bf16((high_a, cols)), bf16((late, span))],
        [],
        keep, *pieces, sum_a, late_a,
    )
    across_a, beside_a = swap(square_a, 2), swap(square_a, 1)
    sum_b, far_b = call(
        functools.partial(sum_kernel, g),
        [f32((high_b, wide_b)), bf16((high_b, far))], [scratch(high_b, early), scratch(high_b, late)],
        *slabs, inner_early, inner_late,
    )
    square_b, inner_far = call(
        functools.partial(square_kernel, g),
        [bf16((high_b, cols)), bf16((far, span))], [],
        keep, far_thin, swap(far_thin, 1), sum_b, far_b,
    )
    across_b, beside_b = swap(square_b, 2), swap(square_b, 1)
    partial = call(
        functools.partial(cubic_kernel, g),
        f32(slab),
        [scratch(rows_dev, 2 * cols), scratch(*slab)] + 2 * left_scratch(g, "own", (g.rows + 1) // 2),
        keep, square_a, beside_a, square_b, beside_b, inner_early, inner_late,
    )
    meet = (slab_early(g, 0)[1] + far_span(g, "B")[1]) * g.size
    done, straight, next_to = call(
        functools.partial(other_kernel, g),
        [f32((high_a, cols)), bf16((meet, wide_b)), bf16((meet, wide_b))],
        [scratch(high_a, 2 * cols)] + left_scratch(g, "A", g.group("A")[0]),
        keep, across_a, swap(across_a, 1), inner_early, inner_far, partial,
    )
    across_b = put_after(across_b, done)
    left = scratch(high_b, meet)
    partial = call(
        functools.partial(slab_kernel, g), f32((high_b, cols)), [left], keep, across_b, straight, partial
    )
    return call(
        functools.partial(last_kernel, g),
        f32(slab),
        [pltpu.VMEM((high_b, cols), jnp.float32), pltpu.SemaphoreType.DMA((3,)), left],
        keep, swap(across_b, 1), next_to, partial, done,
        place=HBM,
    )


def solution(mesh):
    placed = (P("row", "layer"), P("row", "layer"))
    return jax.shard_map(
        body, mesh=mesh, in_specs=placed, out_specs=P("row", "layer"), check_vma=False
    )
```

```python
import functools

import jax
import jax.numpy as jnp
from jax import lax
from jax.experimental import pallas as pl
from jax.experimental.pallas import tpu as pltpu
from jax.sharding import PartitionSpec as P

VMEM = pl.BlockSpec(memory_space=pltpu.VMEM)
HBM = pl.BlockSpec(memory_space=pltpu.HBM)
LIMIT = 12 * 1024 * 1024


class Geometry:
    def __init__(self, rows_dev, slab_cols, block_rows, slab_offsets, layers):
        self.rows, self.slab = block_rows, slab_offsets
        self.size = rows_dev // block_rows
        self.layers = layers
        self.offsets = slab_offsets * layers
        self.half = self.offsets // 2
        self.pair = 2 * slab_offsets
        self.reach_low, self.reach_high = self.half, self.half - 1
        self.columns = self.pair + block_rows - 1
        self.span = even_up(self.columns)
        self.far = even_up(max(len(self.reached(step)) for step in (-2, 2)))

    def needed(self, t, side):
        lo, hi = self.pair * side - t, self.pair * side - t + self.columns
        if t < 0:
            lo = max(lo, -t)
        if t >= self.rows:
            hi = min(hi, self.offsets - (t - self.rows + 1))
        lo, hi = max(lo, 0), min(hi, self.offsets)
        return lo, max(lo, hi)

    def reached(self, step):
        first = step * self.rows
        return [
            t
            for t in range(first, first + self.rows)
            if -self.reach_low <= t < self.rows + self.reach_high
        ]

    def inner_rows(self, side, part):
        if part == "early":
            return sorted(list(range(self.rows)) + self.reached(step_of(side, NEAR_THIN)))
        rows = []
        for name in ([NEAR_WIDE, FAR_WIDE] if part == "late" else [FAR_THIN]):
            reached = self.reached(step_of(side, name))
            rows += reached + [None] * (0 if name[0] == "near" else self.far - len(reached))
        return rows

    def inner_count(self, part):
        return len(self.inner_rows(0, part))

    def group(self, name):
        first = even_up(2 * self.rows // 5)
        count = first if name == "A" else self.rows - first
        return count, even_up(count - 1 + self.slab)

    def first(self, side, name):
        return 0 if (side == 0) == (name == "A") else self.rows - self.group(name)[0]

    def layout(self, side, name):
        step = step_of(side, name)
        found = []
        for t in self.reached(step):
            lo, hi = self.needed(t, side)
            lo, hi = max(lo, self.pair * side), min(hi, self.pair * (side + 1))
            if hi > lo:
                if name[0] == "near":
                    lo, hi = even_down(lo), even_up(hi)
                found.append((hi - lo, t, lo, hi))
        found.sort(reverse=True)
        if name[0] == "far":
            places, used = {}, []
            for width, t, lo, hi in found:
                free = [n for n, taken in enumerate(used) if taken + width <= self.slab]
                slot = free[0] if free else len(used)
                used += [] if free else [0]
                places[t] = (slot, used[slot], lo, hi)
                used[slot] += width
            return places, len(used), max(used)
        slots = (len(found) + 1) // 2
        used = [0] * slots
        places = {}
        for n, (width, t, lo, hi) in enumerate(found):
            slot = n if n < slots else 2 * slots - 1 - n
            places[t] = (slot, used[slot], lo, hi)
            used[slot] += width
        return places, slots, max(used)


def even_down(n):
    return n // 2 * 2


def even_up(n):
    return (n + 1) // 2 * 2


def step_of(side, name):
    sign = 1 if (name[1] == "thin") == (side == 0) else -1
    return sign * (1 if name[0] == "near" else 2)


NEAR_WIDE, NEAR_THIN = ("near", "wide"), ("near", "thin")
FAR_WIDE, FAR_THIN = ("far", "wide"), ("far", "thin")


def message_shape(g, name):
    layouts = [g.layout(side, name) for side in (0, 1)]
    rows, cols = max(f[1] for f in layouts) * g.size // 2, max(f[2] for f in layouts) * g.size
    if name == FAR_WIDE:
        return rows + g.far * g.size, g.slab * g.size
    return rows, cols


def layer_index():
    return lax.axis_index("layer").astype(jnp.int32)


def mask_kernel(g, density_ref, pattern_ref, out_ref, keep, give, density, pattern, sems):
    copies = [
        pltpu.make_async_copy(source, target, sems.at[n])
        for n, (source, target) in enumerate(((pattern_ref, pattern), (density_ref, density)))
    ]
    for copy in copies:
        copy.start()
    copies[0].wait()
    offsets, cols = pattern.shape[0], keep.shape[1]
    block = lax.broadcasted_iota(jnp.int32, (offsets, cols), 1) // g.size
    row = lax.broadcasted_iota(jnp.int32, (offsets, cols), 0)
    spread = jnp.where(block == row, 1.0, 0.0).astype(jnp.float32)
    keep[: g.rows, :] = lax.dot_general(
        pattern[...].astype(jnp.float32), spread, (((0,), (0,)), ((), ())),
        preferred_element_type=jnp.float32,
    )
    keep[g.rows :, :] = jnp.zeros((keep.shape[0] - g.rows, cols), keep.dtype)
    copies[1].wait()
    half = g.size // 2
    for t in range(g.rows):
        rows = slice(t * g.size, (t + 1) * g.size)
        out_ref[rows, :] = density[rows, :] * keep[t : t + 1, :].astype(jnp.bfloat16)
        start = pl.multiple_of(t * g.size + half * (1 - layer_index() % 2), half)
        give[t * half : (t + 1) * half, :] = out_ref[pl.ds(start, half), :]


def cross_rows(g, side):
    rows = [t - step_of(side, FAR_WIDE) * g.rows for t in g.reached(step_of(side, FAR_WIDE))]
    count = g.far
    return min(rows[0], g.rows - count), count


def place_row(dst_ref, dst_row, dst_lo, src_ref, src_row, height, lo, hi, shift, size, limit):
    first, last = max(lo, shift), min(hi, limit + shift)
    base = dst_lo - lo
    rows = slice(dst_row, dst_row + height)
    if first >= last:
        dst_ref[rows, dst_lo * size : (hi + base) * size] = jnp.zeros(
            (height, (hi - lo) * size), dst_ref.dtype
        )
        return
    value = src_ref[src_row : src_row + height, (first - shift) * size : (last - shift) * size]
    parts = []
    if first > lo:
        parts.append(jnp.zeros((height, (first - lo) * size), dst_ref.dtype))
    parts.append(value)
    if hi > last:
        parts.append(jnp.zeros((height, (hi - last) * size), dst_ref.dtype))
    if len(parts) > 1:
        value = jnp.concatenate(parts, axis=1)
    dst_ref[rows, dst_lo * size : (hi + base) * size] = value


def pack(g, side, name, source, row_of, lead, height, out):
    places, slots, _ = g.layout(side, name)
    filled = [0] * slots
    for t, (slot, col, lo, hi) in places.items():
        out[slot * height : (slot + 1) * height, col * g.size : (col + hi - lo) * g.size] = source[
            pl.ds(row_of(t - step_of(side, name) * g.rows), height), (lo - lead) * g.size : (hi - lead) * g.size
        ]
        filled[slot] = max(filled[slot], col + hi - lo)
    for slot, count in enumerate(filled):
        if count * g.size < out.shape[1]:
            out[slot * height : (slot + 1) * height, count * g.size :] = jnp.zeros(
                (height, out.shape[1] - count * g.size), out.dtype
            )
    if slots * height < out.shape[0] and name != FAR_WIDE:
        out[slots * height :, :] = jnp.zeros((out.shape[0] - slots * height, out.shape[1]), out.dtype)


def fill_near(g, core, own, given, near):
    half, cols = g.size // 2, g.slab * g.size
    here, there = (pl.ds(pl.multiple_of(c * cols, cols), cols) for c in (core, 1 - core))
    for t in range(g.rows):
        src = pl.multiple_of(t * g.size + half * core, half)
        near[t * half : (t + 1) * half, here] = own[pl.ds(src, half), :]
    near[:, there] = given[...]


def pack_kernel(g, own_ref, given_ref, wide, far, near):
    side, core = layer_index() // 2, layer_index() % 2
    half = g.size // 2
    fill_near(g, core, own_ref, given_ref, near)

    def fill(side):
        for name, out in ((NEAR_WIDE, wide), (FAR_WIDE, far)):
            pack(g, side, name, near, lambda row: row * half, side * g.pair, half, out)

    for value in (0, 1):
        pl.when(side == value)(functools.partial(fill, value))


def relay_kernel(g, own_ref, relayed_ref, far_ref, other_ref, after_ref, out_ref, message):
    side, row = layer_index() // 2, lax.axis_index("row")
    pick((row % 2) == side, own_ref, relayed_ref, out_ref)
    message[: far_ref.shape[0], :] = far_ref[...]

    def fill(side):
        first, count = cross_rows(g, side)
        message[far_ref.shape[0] :, :] = other_ref[first * g.size : (first + count) * g.size, :]

    for value in (0, 1):
        pl.when(side == value)(functools.partial(fill, value))


def pass_kernel(in_ref, *refs):
    refs[-1][...] = in_ref[...]


def far_thin_kernel(g, far_own, far_beside, after_ref, message):
    side, core = layer_index() // 2, layer_index() % 2
    half = g.size // 2

    def fill(side, source):
        first, count = cross_rows(g, side)
        start = source.shape[0] - (count + first) * g.size
        row_of = lambda row: pl.multiple_of(start + row * g.size + half * core, half)
        pack(g, 1 - side, FAR_THIN, source, row_of, (1 - side) * (g.offsets - g.slab), half, message)

    for value in (0, 1):
        for held, source in ((True, far_own), (False, far_beside)):
            here = jnp.logical_and(side == value, (core == 1 - value) == held)
            pl.when(here)(functools.partial(fill, value, source))


def fill_pair(g, core, slabs, pair):
    cols = g.slab * g.size
    for q, slab in enumerate(slabs):
        pair[:, pl.ds(pl.multiple_of((core ^ q) * cols, cols), cols)] = slab[...]


def place_parts(g, dst, at, height, t, side, parts):
    shift = t - g.pair * side
    values, done = [], 0
    for lo, hi, load in parts:
        lo, hi = max(lo, done - shift), min(hi, g.span - shift)
        if lo >= hi:
            continue
        if lo + shift > done:
            values.append(jnp.zeros((height, (lo + shift - done) * g.size), dst.dtype))
        values.append(load(lo, hi))
        done = hi + shift
    if done < g.span:
        values.append(jnp.zeros((height, (g.span - done) * g.size), dst.dtype))
    dst[pl.ds(at, height), :] = jnp.concatenate(values, axis=1) if len(values) > 1 else values[0]


def left_rows(g, dst, inner_rows, rows, band, band_first, lead, limit):
    runs = []
    for k, t in enumerate(inner_rows):
        offset = None if t is None else t - k
        if runs and runs[-1][0] == offset:
            runs[-1][2] = k + 1
        else:
            runs.append([offset, k, k + 1])
    for n, i in enumerate(rows):
        for offset, lo, hi in runs:
            shift = hi if offset is None else i - g.reach_low - offset + lead
            place_row(
                dst, n * g.size, lo, band, (band_first + n) * g.size, g.size, lo, hi, shift, g.size, limit
            )


def window_of(g, core, inner, col, cols):
    start = pl.multiple_of((core * g.slab + col) * g.size, 2 * g.size)
    return inner[:, pl.ds(start, cols * g.size)]


def dot(left, right):
    return jnp.dot(left, right, preferred_element_type=jnp.float32)


def own_columns(g, product, n):
    return product[n * g.size : (n + 1) * g.size, n * g.size : (n + g.slab) * g.size]


def by_side(side, values):
    return jnp.where(side == 0, values[0], values[1])


def group_first(g, side, name):
    return by_side(side, [g.first(value, name) for value in (0, 1)])


def message_part(g, side, name, t, piece, height):
    places, _, _ = g.layout(side, name)
    if t not in places:
        return []
    slot, col, lo, hi = places[t]
    rows = slice(slot * height, (slot + 1) * height)
    return [(lo, hi, lambda a, b: piece[rows, (col + a - lo) * g.size : (col + b - lo) * g.size])]


def pair_part(g, pair_index, ref, row, height):
    base = g.pair * pair_index
    return (
        base,
        base + g.pair,
        lambda a, b: ref[pl.ds(row, height), (a - base) * g.size : (b - base) * g.size],
    )


def pick(condition, first, second, out):
    pl.when(condition)(lambda: out.__setitem__(..., first[...]))
    pl.when(jnp.logical_not(condition))(lambda: out.__setitem__(..., second[...]))


def group_rows(g, side, name):
    first = g.first(side, name)
    return range(first, first + g.group(name)[0])


class Slabs:
    def __init__(self, g, layer, slabs):
        self.width, self.slabs, self.layer = g.slab * g.size, slabs, layer

    def __getitem__(self, at):
        rows, cols = at
        found = []
        for place in range(len(self.slabs)):
            lo, hi = max(cols.start, place * self.width), min(cols.stop, (place + 1) * self.width)
            if lo < hi:
                here = slice(lo - place * self.width, hi - place * self.width)
                found.append(self.slabs[self.layer ^ place][rows, here])
        return found[0] if len(found) == 1 else jnp.concatenate(found, axis=1)


def early_kernel(g, *refs):
    owns, thins = refs[:4], refs[4:6]
    inner, sum_a, late_a, left_a = refs[6:]
    side, core = layer_index() // 2, layer_index() % 2

    def gather(layer):
        side, core = layer // 2, layer % 2
        band, pair = Slabs(g, layer, owns), Slabs(g, core, thins)
        near = g.reached(step_of(side, NEAR_THIN))
        early, late = (g.inner_rows(side, part) for part in ("early", "late"))
        for k, t in enumerate(early):
            if 0 <= t < g.rows:
                source, row, lead, limit = band, t, 0, g.offsets
            else:
                source, row, lead, limit = pair, t - near[0], g.pair * side, g.pair
            rows = slice(row * g.size, (row + 1) * g.size)
            part = (lead, lead + limit, lambda a, b, source=source, rows=rows, lead=lead: source[
                rows, (a - lead) * g.size : (b - lead) * g.size
            ])
            place_parts(g, inner, k * g.size, g.size, t, side, [part])
        rows = group_rows(g, side, "A")
        for left, inner_rows in ((left_a, early), (late_a, late)):
            left_rows(g, left, inner_rows, rows, band, rows[0], 0, g.offsets)

    for value in range(g.layers):
        pl.when(layer_index() == value)(functools.partial(gather, value))
    col, (_, cols) = group_first(g, side, "A"), g.group("A")
    sum_a[...] = dot(left_a[...], window_of(g, core, inner, col, cols))


def square_of(g, name, side, core, keep, lefts, inners, product=0.0):
    first, (_, cols) = group_first(g, side, name), g.group(name)
    for left, inner in zip(lefts, inners):
        product = product + dot(left[...], window_of(g, core, inner, first, cols))
    return lambda n: (own_columns(g, product, n) * keep[pl.ds(first + n, 1), :]).astype(jnp.bfloat16)


def late_kernel(g, keep, *refs):
    crossed, wides, wide_fars = (refs[2 * n : 2 * n + 2] for n in range(3))
    total, left, square, inner = refs[6:]
    layer = layer_index()
    side, core = layer // 2, layer % 2
    half = g.size // 2

    def slab_parts(side, core, slabs, row, height):
        base = g.pair * (1 - side)
        parts = []
        for c in (0, 1):
            lo, slab = base + c * g.slab, slabs[core ^ c]
            parts.append((lo, lo + g.slab, lambda a, b, lo=lo, slab=slab: slab[
                row : row + height, (a - lo) * g.size : (b - lo) * g.size
            ]))
        return parts

    def gather(layer):
        side, core = layer // 2, layer % 2
        near = g.reached(step_of(side, NEAR_WIDE))
        tail = wide_fars[0].shape[0] - g.far * g.size
        for k, t in enumerate(g.inner_rows(side, "late")):
            if t is None:
                inner[k * g.size : (k + 1) * g.size, :] = jnp.zeros((g.size, inner.shape[1]), inner.dtype)
                continue
            if t in near:
                name, pieces, slabs, row = NEAR_WIDE, wides, crossed, (t - near[0]) * g.size
            else:
                name, pieces, slabs = FAR_WIDE, wide_fars, wide_fars
                row = tail + (t - step_of(side, FAR_WIDE) * g.rows - cross_rows(g, side)[0]) * g.size
            for q, piece in enumerate(pieces):
                at = half * (core ^ q)
                parts = message_part(g, side, name, t, piece, half)
                parts += slab_parts(side, core, slabs, row + at, half)
                parts.sort(key=lambda part: part[0])
                place_parts(g, inner, k * g.size + at, half, t, side, parts)

    for value in range(g.layers):
        pl.when(layer == value)(functools.partial(gather, value))
    row_of = square_of(g, "A", side, core, keep, [left], [inner], total[...])
    for n in range(g.group("A")[0]):
        square[n * g.size : (n + 1) * g.size, :] = row_of(n)


def sum_kernel(g, *refs):
    owns, (early, late, out, far_left, early_left, late_left) = refs[:4], refs[4:]
    side, core = layer_index() // 2, layer_index() % 2

    def fill(layer):
        side = layer // 2
        rows = group_rows(g, side, "B")
        for left, part in ((early_left, "early"), (late_left, "late"), (far_left, "far")):
            inner_rows = g.inner_rows(side, part)
            left_rows(g, left, inner_rows, rows, Slabs(g, layer, owns), rows[0], 0, g.offsets)

    for value in range(g.layers):
        pl.when(layer_index() == value)(functools.partial(fill, value))
    first, (_, cols) = group_first(g, side, "B"), g.group("B")
    out[...] = dot(early_left[...], window_of(g, core, early, first, cols))
    out[...] += dot(late_left[...], window_of(g, core, late, first, cols))


def square_kernel(g, keep, far, far_beside, total, far_left, *refs):
    square, inner = refs
    side, core = layer_index() // 2, layer_index() % 2
    half = g.size // 2

    def gather(side):
        for k, t in enumerate(g.inner_rows(side, "far")):
            for q, piece in enumerate((far, far_beside)):
                at = pl.multiple_of(k * g.size + half * (core ^ q), half)
                parts = [] if t is None else message_part(g, side, FAR_THIN, t, piece, half)
                place_parts(g, inner, at, half, t or 0, side, parts)

    for value in (0, 1):
        pl.when(side == value)(functools.partial(gather, value))
    row_of = square_of(g, "B", side, core, keep, [far_left], [inner], total[...])
    for n in range(g.group("B")[0]):
        square[n * g.size : (n + 1) * g.size, :] = row_of(n)


def band_rows(g, side, name):
    return pl.ds(pl.multiple_of(group_first(g, side, name) * g.size, 2 * g.size), g.group(name)[0] * g.size)


def block_rows(g, t):
    return pl.ds(pl.multiple_of(t * g.size, g.size), g.size)


def early_span(g, part):
    spans = []
    for side in (0, 1):
        rows, pair = (range(g.rows), side) if part == "own" else (group_rows(g, 1 - side, part), 1 - side)
        lo = rows[0] - g.reach_low + g.pair * pair
        hi = rows[-1] - g.reach_low + g.pair * (pair + 1)
        met = [k for k, t in enumerate(g.inner_rows(side, "early")) if lo <= t < hi]
        spans.append((even_down(met[0]), met[-1] + 1))
    count = even_up(max(hi - lo for lo, hi in spans))
    total = len(g.inner_rows(0, "early"))
    return [min(lo, total - count) for lo, _ in spans], count


def far_span(g, part):
    spans = []
    for side in (0, 1):
        rows = group_rows(g, 1 - side, part)
        lo = rows[0] - g.reach_low + g.pair * (1 - side)
        hi = rows[-1] - g.reach_low + g.pair * (2 - side)
        met = [k for k, t in enumerate(g.inner_rows(side, "far")) if t is not None and lo <= t < hi]
        spans.append((even_down(met[0]), met[-1] + 1) if met else (0, 0))
    count = even_up(max(hi - lo for lo, hi in spans))
    return [min(lo, g.inner_count("far") - count) for lo, _ in spans], count


def cubic_left(g, side, part, rows, band, band_first, lefts):
    pair = side if part == "own" else 1 - side
    starts, count = early_span(g, part)
    lists = [g.inner_rows(side, "early")[starts[side] : starts[side] + count]]
    if part == "own":
        lists.append(g.inner_rows(side, "late"))
    else:
        starts, count = far_span(g, part)
        lists.append(g.inner_rows(side, "far")[starts[side] : starts[side] + count])
    for dst, inner_rows in zip(lefts, lists):
        left_rows(g, dst, inner_rows, rows, band, band_first, g.pair * pair, g.pair)


def cubic_right(g, side, part, inners):
    rights = []
    for inner, span in zip(inners, (early_span, far_span)):
        if span == far_span and part == "own":
            rights.append(inner)
            continue
        starts, count = span(g, part)
        start = pl.multiple_of(by_side(side, starts) * g.size, 2 * g.size)
        rights.append(inner.at[pl.ds(start, count * g.size), :])
    return rights


def left_scratch(g, part, count):
    sizes = [early_span(g, part)[1], g.inner_count("late") if part == "own" else far_span(g, part)[1]]
    return [pltpu.VMEM((count * g.size, n * g.size), jnp.bfloat16) for n in sizes]


def cubic_kernel(g, keep, *refs):
    squares, inners, (out, band, own, *lefts) = refs[:4], refs[4:6], refs[6:]
    layer = layer_index()
    side, core = layer // 2, layer % 2
    cols = g.slab * g.size
    for n, name in enumerate("AB"):
        rows = band_rows(g, side, name)
        own[rows, :] = squares[2 * n][...]
        for q in range(2):
            column = pl.ds(pl.multiple_of((core ^ q) * cols, cols), cols)
            band[rows, column] = squares[2 * n + q][...]
    rights = cubic_right(g, side, "own", inners)
    size = (g.rows + 1) // 2
    for n, first in enumerate(range(0, g.rows, size)):
        rows = range(first, min(first + size, g.rows))
        col = even_down(first)
        width = even_up(rows[-1] + g.slab) - col
        used = lefts[2 * n : 2 * n + 2]
        for value in (0, 1):
            pl.when(side == value)(functools.partial(cubic_left, g, value, "own", rows, band, first, used))
        product = sum(
            dot(left[: len(rows) * g.size, :], window_of(g, core, right, col, width))
            for left, right in zip(used, rights)
        )
        for k, t in enumerate(rows):
            at = (t - col) * g.size
            here = slice(t * g.size, (t + 1) * g.size)
            out[here, :] = 3.0 * own[here, :].astype(jnp.float32) - 2.0 * (
                product[k * g.size : (k + 1) * g.size, at : at + cols] * keep[t : t + 1, :]
            )


def other_part(g, layer, name, squares, inners, band, lefts):
    side, core = layer // 2, layer % 2
    cols = g.slab * g.size
    _, width = g.group(name)
    for q in range(2):
        band[:, pl.ds(pl.multiple_of((core ^ q) * cols, cols), cols)] = squares[q][...]
    for value in (0, 1):
        rows = group_rows(g, 1 - value, name)
        pl.when(side == value)(functools.partial(cubic_left, g, value, name, rows, band, 0, lefts))
    first = group_first(g, 1 - side, name)
    rights = cubic_right(g, side, name, inners)
    return first, sum(
        dot(left[...], window_of(g, core, right, first, width)) for left, right in zip(lefts, rights)
    )


def slab_early(g, slab):
    side = 1 - slab // 2
    rows = group_rows(g, 1 - side, "B")
    early = g.inner_rows(side, "early")
    lo, hi = rows[0] - g.reach_low + g.slab * slab, rows[-1] - g.reach_low + g.slab * (slab + 1)
    met = [k for k, t in enumerate(early) if lo <= t < hi]
    count = even_up(len(rows) + g.slab - 1)
    return min(even_down(met[0]), len(early) - count), count


def slab_rights(g, slab, early, far, out):
    side, core = layer_index() // 2, layer_index() % 2
    _, width = g.group("B")
    first = group_first(g, 1 - side, "B")
    start, count = jnp.int32(0), slab_early(g, 0)[1]
    for value in range(g.layers):
        start = jnp.where(slab == value, slab_early(g, value)[0], start)
    far_starts, far_count = far_span(g, "B")
    split = count * g.size
    at = lambda start, count: pl.ds(pl.multiple_of(start * g.size, 2 * g.size), count * g.size)
    out[:split, :] = window_of(g, core, early.at[at(start, count), :], first, width)
    out[split:, :] = window_of(g, core, far.at[at(by_side(side, far_starts), far_count), :], first, width)


def slab_left(g, slab, square, left):
    far_starts, far_count = far_span(g, "B")

    def gather(slab):
        here = 1 - slab // 2
        start, count = slab_early(g, slab)
        inner_rows = g.inner_rows(here, "early")[start : start + count]
        inner_rows = inner_rows + g.inner_rows(here, "far")[far_starts[here] : far_starts[here] + far_count]
        left_rows(g, left, inner_rows, group_rows(g, 1 - here, "B"), square, 0, g.slab * slab, g.slab)

    for value in range(g.layers):
        pl.when(slab == value)(functools.partial(gather, value))


def other_kernel(g, keep, *refs):
    squares, inners, (partial, out, straight, beside, band, *lefts) = refs[:2], refs[2:4], refs[4:]
    first, product = other_part(g, layer_index(), "A", squares, inners, band, lefts)
    for n in range(g.group("A")[0]):
        out[n * g.size : (n + 1) * g.size, :] = partial[block_rows(g, first + n), :] - 2.0 * (
            own_columns(g, product, n) * keep[pl.ds(first + n, 1), :]
        )
    for q, right in ((2, straight), (3, beside)):
        slab_rights(g, layer_index() ^ q, *inners, right)


def slab_kernel(g, keep, square, right, partial, out, left):
    slab_left(g, layer_index() ^ 2, square, left)
    first = group_first(g, 1 - layer_index() // 2, "B")
    product = dot(left[...], right[...])
    for n in range(g.group("B")[0]):
        out[n * g.size : (n + 1) * g.size, :] = partial[block_rows(g, first + n), :] - 2.0 * (
            own_columns(g, product, n) * keep[pl.ds(first + n, 1), :]
        )


def last_kernel(g, keep, square, right, partial, done, out, rows, sems, left):
    side = layer_index() // 2
    copies = [pltpu.make_async_copy(done, out.at[band_rows(g, 1 - side, "A"), :], sems.at[0])]
    copies[0].start()
    slab_left(g, layer_index() ^ 3, square, left)
    first, count = group_first(g, 1 - side, "B"), g.group("B")[0]
    step = count // 2
    for begin in range(0, count, step):
        here = slice(begin * g.size, (begin + step) * g.size)
        part = dot(left[here, :], right[...])
        for n in range(begin, begin + step):
            value = part[(n - begin) * g.size : (n - begin + 1) * g.size, n * g.size : (n + g.slab) * g.size]
            row = slice(n * g.size, (n + 1) * g.size)
            rows[row, :] = partial[row, :] - 2.0 * (value * keep[pl.ds(first + n, 1), :])
            to = pl.ds(pl.multiple_of((first + n) * g.size, g.size), g.size)
            copies.append(pltpu.make_async_copy(rows.at[row, :], out.at[to, :], sems.at[len(copies)]))
            copies[-1].start()
    for copy in copies:
        copy.wait()


def call(kernel, out_shape, scratch, *args, after=(), placed=(), place=VMEM):
    specs = [VMEM] * len(args) + [pl.BlockSpec(memory_space=pl.ANY)] * len(after) + [HBM] * len(placed)
    return pl.pallas_call(
        kernel,
        out_shape=out_shape,
        in_specs=specs,
        out_specs=jax.tree.map(lambda _: place, out_shape),
        scratch_shapes=scratch,
        compiler_params=pltpu.CompilerParams(vmem_limit_bytes=LIMIT),
        cost_estimate=pl.CostEstimate(flops=0, bytes_accessed=0, transcendentals=0),
    )(*args, *after, *placed)


def body(density, pattern):
    layers, ring = lax.axis_size("layer"), lax.axis_size("row")
    g = Geometry(*density.shape, *pattern.shape, layers)
    rows_dev, cols = density.shape
    bf16 = functools.partial(jax.ShapeDtypeStruct, dtype=jnp.bfloat16)
    scratch = lambda *shape: pltpu.VMEM(shape, jnp.bfloat16)

    def swap(value, bit):
        return lax.ppermute(value, "layer", [(s, s ^ bit) for s in range(layers)])

    def send(value, name, keep=lambda layer, row: True):
        pairs = []
        for l in range(layers):
            step = step_of(l // 2, name)
            pairs += [
                (l * ring + r, l * ring + (r - step) % ring) for r in range(ring) if keep(l, r)
            ]
        return lax.ppermute(value, ("layer", "row"), pairs)

    half_rows, slab = rows_dev // 2, (rows_dev, cols)
    cross_shape = (g.far * g.size, cols)

    def put_after(value, *after):
        return call(pass_kernel, bf16(value.shape), [], value, after=after)

    sources = [pltpu.with_memory_space_constraint(value, pltpu.HBM) for value in (density, pattern.T)]
    masked, keep, give = call(
        functools.partial(mask_kernel, g),
        [
            bf16(slab), jax.ShapeDtypeStruct(((g.rows + 7) // 8 * 8, cols), jnp.float32),
            bf16((half_rows, cols)),
        ],
        [scratch(*slab), pltpu.VMEM(pattern.T.shape, pattern.dtype), pltpu.SemaphoreType.DMA((2,))],
        placed=sources,
    )
    thin = send(masked, NEAR_THIN)
    other = swap(masked, 2)
    beside = swap(masked, 1)
    far_shape = message_shape(g, FAR_WIDE)
    head_shape = (far_shape[0] - cross_shape[0], cols)
    wide, far_wide = call(
        functools.partial(pack_kernel, g),
        [bf16(message_shape(g, NEAR_WIDE)), bf16(head_shape)], [scratch(half_rows, 2 * cols)],
        masked, swap(give, 1),
    )
    relayed = send(wide, FAR_WIDE, lambda layer, row: row % 2 != layer // 2)
    crossed = swap(thin, 2)
    wide, far_wide = call(
        functools.partial(relay_kernel, g),
        [bf16(wide.shape), bf16(far_shape)], [], wide, relayed, far_wide, other, after=(thin,),
    )
    wide = lax.ppermute(wide, "row", [(r, r ^ 1) for r in range(ring)])
    far_wide = send(far_wide, FAR_WIDE)

    early, late, far = (g.inner_count(part) * g.size for part in ("early", "late", "far"))
    (high_a, wide_a), (high_b, wide_b) = (tuple(n * g.size for n in g.group(name)) for name in "AB")
    span = g.span * g.size
    f32 = functools.partial(jax.ShapeDtypeStruct, dtype=jnp.float32)

    slabs = (masked, beside, other, swap(other, 1))
    inner_early, sum_a, late_a = call(
        functools.partial(early_kernel, g),
        [bf16((early, span)), f32((high_a, wide_a)), bf16((high_a, late))], [scratch(high_a, early)],
        *slabs, thin, swap(thin, 1),
    )
    far_beside = swap(far_wide, 1)
    far_thin = call(
        functools.partial(far_thin_kernel, g),
        bf16(message_shape(g, FAR_THIN)), [], far_wide, far_beside, after=(sum_a,),
    )
    far_thin = swap(far_thin, 2)
    pieces = [crossed, swap(crossed, 1), wide, swap(wide, 1), far_wide, far_beside]
    square_a, inner_late = call(
        functools.partial(late_kernel, g),
        [bf16((high_a, cols)), bf16((late, span))],
        [],
        keep, *pieces, sum_a, late_a,
    )
    across_a, beside_a = swap(square_a, 2), swap(square_a, 1)
    sum_b, far_b = call(
        functools.partial(sum_kernel, g),
        [f32((high_b, wide_b)), bf16((high_b, far))], [scratch(high_b, early), scratch(high_b, late)],
        *slabs, inner_early, inner_late,
    )
    square_b, inner_far = call(
        functools.partial(square_kernel, g),
        [bf16((high_b, cols)), bf16((far, span))], [],
        keep, far_thin, swap(far_thin, 1), sum_b, far_b,
    )
    across_b, beside_b = swap(square_b, 2), swap(square_b, 1)
    partial = call(
        functools.partial(cubic_kernel, g),
        f32(slab),
        [scratch(rows_dev, 2 * cols), scratch(*slab)] + 2 * left_scratch(g, "own", (g.rows + 1) // 2),
        keep, square_a, beside_a, square_b, beside_b, inner_early, inner_late,
    )
    meet = (slab_early(g, 0)[1] + far_span(g, "B")[1]) * g.size
    done, straight, next_to = call(
        functools.partial(other_kernel, g),
        [f32((high_a, cols)), bf16((meet, wide_b)), bf16((meet, wide_b))],
        [scratch(high_a, 2 * cols)] + left_scratch(g, "A", g.group("A")[0]),
        keep, across_a, swap(across_a, 1), inner_early, inner_far, partial,
    )
    across_b = put_after(across_b, done)
    left = scratch(high_b, meet)
    partial = call(
        functools.partial(slab_kernel, g), f32((high_b, cols)), [left], keep, across_b, straight, partial
    )
    return call(
        functools.partial(last_kernel, g),
        f32(slab),
        [pltpu.VMEM((high_b, cols), jnp.float32), pltpu.SemaphoreType.DMA((1 + g.group("B")[0],)), left],
        keep, swap(across_b, 1), next_to, partial, done,
        place=HBM,
    )


def solution(mesh):
    placed = (P("row", "layer"), P("row", "layer"))
    return jax.shard_map(
        body, mesh=mesh, in_specs=placed, out_specs=P("row", "layer"), check_vma=False
    )
```

```python
import functools

import jax
import jax.numpy as jnp
from jax import lax
from jax.experimental import pallas as pl
from jax.experimental.pallas import tpu as pltpu
from jax.sharding import PartitionSpec as P

VMEM = pl.BlockSpec(memory_space=pltpu.VMEM)
HBM = pl.BlockSpec(memory_space=pltpu.HBM)
LIMIT = 12 * 1024 * 1024


class Geometry:
    def __init__(self, rows_dev, slab_cols, block_rows, slab_offsets, layers):
        self.rows, self.slab = block_rows, slab_offsets
        self.size = rows_dev // block_rows
        self.layers = layers
        self.offsets = slab_offsets * layers
        self.half = self.offsets // 2
        self.pair = 2 * slab_offsets
        self.reach_low, self.reach_high = self.half, self.half - 1
        self.columns = self.pair + block_rows - 1
        self.span = even_up(self.columns)
        self.far = even_up(max(len(self.reached(step)) for step in (-2, 2)))

    def needed(self, t, side):
        lo, hi = self.pair * side - t, self.pair * side - t + self.columns
        if t < 0:
            lo = max(lo, -t)
        if t >= self.rows:
            hi = min(hi, self.offsets - (t - self.rows + 1))
        lo, hi = max(lo, 0), min(hi, self.offsets)
        return lo, max(lo, hi)

    def reached(self, step):
        first = step * self.rows
        return [
            t
            for t in range(first, first + self.rows)
            if -self.reach_low <= t < self.rows + self.reach_high
        ]

    def inner_rows(self, side, part):
        if part == "early":
            return sorted(list(range(self.rows)) + self.reached(step_of(side, NEAR_THIN)))
        rows = []
        for name in ([NEAR_WIDE, FAR_WIDE] if part == "late" else [FAR_THIN]):
            reached = self.reached(step_of(side, name))
            rows += reached + [None] * (0 if name[0] == "near" else self.far - len(reached))
        return rows

    def inner_count(self, part):
        return len(self.inner_rows(0, part))

    def group(self, name):
        first = even_up(2 * self.rows // 5)
        count = first if name == "A" else self.rows - first
        return count, even_up(count - 1 + self.slab)

    def first(self, side, name):
        return 0 if (side == 0) == (name == "A") else self.rows - self.group(name)[0]

    def layout(self, side, name):
        step = step_of(side, name)
        found = []
        for t in self.reached(step):
            lo, hi = self.needed(t, side)
            lo, hi = max(lo, self.pair * side), min(hi, self.pair * (side + 1))
            if hi > lo:
                if name[0] == "near":
                    lo, hi = even_down(lo), even_up(hi)
                found.append((hi - lo, t, lo, hi))
        found.sort(reverse=True)
        if name[0] == "far":
            places, used = {}, []
            for width, t, lo, hi in found:
                free = [n for n, taken in enumerate(used) if taken + width <= self.slab]
                slot = free[0] if free else len(used)
                used += [] if free else [0]
                places[t] = (slot, used[slot], lo, hi)
                used[slot] += width
            return places, len(used), max(used)
        slots = (len(found) + 1) // 2
        used = [0] * slots
        places = {}
        for n, (width, t, lo, hi) in enumerate(found):
            slot = n if n < slots else 2 * slots - 1 - n
            places[t] = (slot, used[slot], lo, hi)
            used[slot] += width
        return places, slots, max(used)


def even_down(n):
    return n // 2 * 2


def even_up(n):
    return (n + 1) // 2 * 2


def step_of(side, name):
    sign = 1 if (name[1] == "thin") == (side == 0) else -1
    return sign * (1 if name[0] == "near" else 2)


NEAR_WIDE, NEAR_THIN = ("near", "wide"), ("near", "thin")
FAR_WIDE, FAR_THIN = ("far", "wide"), ("far", "thin")


def message_shape(g, name):
    layouts = [g.layout(side, name) for side in (0, 1)]
    rows, cols = max(f[1] for f in layouts) * g.size // 2, max(f[2] for f in layouts) * g.size
    if name == FAR_WIDE:
        return rows + g.far * g.size, g.slab * g.size
    return rows, cols


def layer_index():
    return lax.axis_index("layer").astype(jnp.int32)


def mask_kernel(g, density_ref, pattern_ref, out_ref, keep, give, density, pattern, sems):
    copies = [
        pltpu.make_async_copy(source, target, sems.at[n])
        for n, (source, target) in enumerate(((pattern_ref, pattern), (density_ref, density)))
    ]
    for copy in copies:
        copy.start()
    copies[0].wait()
    offsets, cols = pattern.shape[0], keep.shape[1]
    block = lax.broadcasted_iota(jnp.int32, (offsets, cols), 1) // g.size
    row = lax.broadcasted_iota(jnp.int32, (offsets, cols), 0)
    spread = jnp.where(block == row, 1.0, 0.0).astype(jnp.float32)
    keep[: g.rows, :] = lax.dot_general(
        pattern[...].astype(jnp.float32), spread, (((0,), (0,)), ((), ())),
        preferred_element_type=jnp.float32,
    )
    keep[g.rows :, :] = jnp.zeros((keep.shape[0] - g.rows, cols), keep.dtype)
    copies[1].wait()
    half = g.size // 2
    for t in range(g.rows):
        rows = slice(t * g.size, (t + 1) * g.size)
        out_ref[rows, :] = density[rows, :] * keep[t : t + 1, :].astype(jnp.bfloat16)
        start = pl.multiple_of(t * g.size + half * (1 - layer_index() % 2), half)
        give[t * half : (t + 1) * half, :] = out_ref[pl.ds(start, half), :]


def cross_rows(g, side):
    rows = [t - step_of(side, FAR_WIDE) * g.rows for t in g.reached(step_of(side, FAR_WIDE))]
    count = g.far
    return min(rows[0], g.rows - count), count


def place_row(dst_ref, dst_row, dst_lo, src_ref, src_row, height, lo, hi, shift, size, limit):
    first, last = max(lo, shift), min(hi, limit + shift)
    base = dst_lo - lo
    rows = slice(dst_row, dst_row + height)
    if first >= last:
        dst_ref[rows, dst_lo * size : (hi + base) * size] = jnp.zeros(
            (height, (hi - lo) * size), dst_ref.dtype
        )
        return
    value = src_ref[src_row : src_row + height, (first - shift) * size : (last - shift) * size]
    parts = []
    if first > lo:
        parts.append(jnp.zeros((height, (first - lo) * size), dst_ref.dtype))
    parts.append(value)
    if hi > last:
        parts.append(jnp.zeros((height, (hi - last) * size), dst_ref.dtype))
    if len(parts) > 1:
        value = jnp.concatenate(parts, axis=1)
    dst_ref[rows, dst_lo * size : (hi + base) * size] = value


def pack(g, side, name, source, row_of, lead, height, out):
    places, slots, _ = g.layout(side, name)
    filled = [0] * slots
    for t, (slot, col, lo, hi) in places.items():
        out[slot * height : (slot + 1) * height, col * g.size : (col + hi - lo) * g.size] = source[
            pl.ds(row_of(t - step_of(side, name) * g.rows), height), (lo - lead) * g.size : (hi - lead) * g.size
        ]
        filled[slot] = max(filled[slot], col + hi - lo)
    for slot, count in enumerate(filled):
        if count * g.size < out.shape[1]:
            out[slot * height : (slot + 1) * height, count * g.size :] = jnp.zeros(
                (height, out.shape[1] - count * g.size), out.dtype
            )
    if slots * height < out.shape[0] and name != FAR_WIDE:
        out[slots * height :, :] = jnp.zeros((out.shape[0] - slots * height, out.shape[1]), out.dtype)


def fill_near(g, core, own, given, near):
    half, cols = g.size // 2, g.slab * g.size
    here, there = (pl.ds(pl.multiple_of(c * cols, cols), cols) for c in (core, 1 - core))
    for t in range(g.rows):
        src = pl.multiple_of(t * g.size + half * core, half)
        near[t * half : (t + 1) * half, here] = own[pl.ds(src, half), :]
    near[:, there] = given[...]


def pack_kernel(g, own_ref, given_ref, wide, far, near):
    side, core = layer_index() // 2, layer_index() % 2
    half = g.size // 2
    fill_near(g, core, own_ref, given_ref, near)

    def fill(side):
        for name, out in ((NEAR_WIDE, wide), (FAR_WIDE, far)):
            pack(g, side, name, near, lambda row: row * half, side * g.pair, half, out)

    for value in (0, 1):
        pl.when(side == value)(functools.partial(fill, value))


def far_kernel(g, far_ref, other_ref, after_ref, message):
    message[: far_ref.shape[0], :] = far_ref[...]

    def fill(side):
        first, count = cross_rows(g, side)
        message[far_ref.shape[0] :, :] = other_ref[first * g.size : (first + count) * g.size, :]

    for value in (0, 1):
        pl.when(layer_index() // 2 == value)(functools.partial(fill, value))


def relay_kernel(g, own_ref, relayed_ref, after_ref, out_ref):
    pick((lax.axis_index("row") % 2) == layer_index() // 2, own_ref, relayed_ref, out_ref)


def pass_kernel(in_ref, *refs):
    refs[-1][...] = in_ref[...]


def far_thin_kernel(g, far_own, far_beside, after_ref, message):
    side, core = layer_index() // 2, layer_index() % 2
    half = g.size // 2

    def fill(side, source):
        first, count = cross_rows(g, side)
        start = source.shape[0] - (count + first) * g.size
        row_of = lambda row: pl.multiple_of(start + row * g.size + half * core, half)
        pack(g, 1 - side, FAR_THIN, source, row_of, (1 - side) * (g.offsets - g.slab), half, message)

    for value in (0, 1):
        for held, source in ((True, far_own), (False, far_beside)):
            here = jnp.logical_and(side == value, (core == 1 - value) == held)
            pl.when(here)(functools.partial(fill, value, source))


def fill_pair(g, core, slabs, pair):
    cols = g.slab * g.size
    for q, slab in enumerate(slabs):
        pair[:, pl.ds(pl.multiple_of((core ^ q) * cols, cols), cols)] = slab[...]


def place_parts(g, dst, at, height, t, side, parts):
    shift = t - g.pair * side
    values, done = [], 0
    for lo, hi, load in parts:
        lo, hi = max(lo, done - shift), min(hi, g.span - shift)
        if lo >= hi:
            continue
        if lo + shift > done:
            values.append(jnp.zeros((height, (lo + shift - done) * g.size), dst.dtype))
        values.append(load(lo, hi))
        done = hi + shift
    if done < g.span:
        values.append(jnp.zeros((height, (g.span - done) * g.size), dst.dtype))
    dst[pl.ds(at, height), :] = jnp.concatenate(values, axis=1) if len(values) > 1 else values[0]


def left_rows(g, dst, inner_rows, rows, band, band_first, lead, limit):
    runs = []
    for k, t in enumerate(inner_rows):
        offset = None if t is None else t - k
        if runs and runs[-1][0] == offset:
            runs[-1][2] = k + 1
        else:
            runs.append([offset, k, k + 1])
    for n, i in enumerate(rows):
        for offset, lo, hi in runs:
            shift = hi if offset is None else i - g.reach_low - offset + lead
            place_row(
                dst, n * g.size, lo, band, (band_first + n) * g.size, g.size, lo, hi, shift, g.size, limit
            )


def window_of(g, core, inner, col, cols):
    start = pl.multiple_of((core * g.slab + col) * g.size, 2 * g.size)
    return inner[:, pl.ds(start, cols * g.size)]


def dot(left, right):
    return jnp.dot(left, right, preferred_element_type=jnp.float32)


def own_columns(g, product, n):
    return product[n * g.size : (n + 1) * g.size, n * g.size : (n + g.slab) * g.size]


def by_side(side, values):
    return jnp.where(side == 0, values[0], values[1])


def group_first(g, side, name):
    return by_side(side, [g.first(value, name) for value in (0, 1)])


def message_part(g, side, name, t, piece, height):
    places, _, _ = g.layout(side, name)
    if t not in places:
        return []
    slot, col, lo, hi = places[t]
    rows = slice(slot * height, (slot + 1) * height)
    return [(lo, hi, lambda a, b: piece[rows, (col + a - lo) * g.size : (col + b - lo) * g.size])]


def pair_part(g, pair_index, ref, row, height):
    base = g.pair * pair_index
    return (
        base,
        base + g.pair,
        lambda a, b: ref[pl.ds(row, height), (a - base) * g.size : (b - base) * g.size],
    )


def pick(condition, first, second, out):
    pl.when(condition)(lambda: out.__setitem__(..., first[...]))
    pl.when(jnp.logical_not(condition))(lambda: out.__setitem__(..., second[...]))


def group_rows(g, side, name):
    first = g.first(side, name)
    return range(first, first + g.group(name)[0])


class Slabs:
    def __init__(self, g, layer, slabs):
        self.width, self.slabs, self.layer = g.slab * g.size, slabs, layer

    def __getitem__(self, at):
        rows, cols = at
        found = []
        for place in range(len(self.slabs)):
            lo, hi = max(cols.start, place * self.width), min(cols.stop, (place + 1) * self.width)
            if lo < hi:
                here = slice(lo - place * self.width, hi - place * self.width)
                found.append(self.slabs[self.layer ^ place][rows, here])
        return found[0] if len(found) == 1 else jnp.concatenate(found, axis=1)


def early_kernel(g, *refs):
    owns, thins = refs[:4], refs[4:6]
    inner, sum_a, late_a, left_a = refs[6:]
    side, core = layer_index() // 2, layer_index() % 2

    def gather(layer):
        side, core = layer // 2, layer % 2
        band, pair = Slabs(g, layer, owns), Slabs(g, core, thins)
        near = g.reached(step_of(side, NEAR_THIN))
        early, late = (g.inner_rows(side, part) for part in ("early", "late"))
        for k, t in enumerate(early):
            if 0 <= t < g.rows:
                source, row, lead, limit = band, t, 0, g.offsets
            else:
                source, row, lead, limit = pair, t - near[0], g.pair * side, g.pair
            rows = slice(row * g.size, (row + 1) * g.size)
            part = (lead, lead + limit, lambda a, b, source=source, rows=rows, lead=lead: source[
                rows, (a - lead) * g.size : (b - lead) * g.size
            ])
            place_parts(g, inner, k * g.size, g.size, t, side, [part])
        rows = group_rows(g, side, "A")
        for left, inner_rows in ((left_a, early), (late_a, late)):
            left_rows(g, left, inner_rows, rows, band, rows[0], 0, g.offsets)

    for value in range(g.layers):
        pl.when(layer_index() == value)(functools.partial(gather, value))
    col, (_, cols) = group_first(g, side, "A"), g.group("A")
    sum_a[...] = dot(left_a[...], window_of(g, core, inner, col, cols))


def square_of(g, name, side, core, keep, lefts, inners, product=0.0):
    first, (_, cols) = group_first(g, side, name), g.group(name)
    for left, inner in zip(lefts, inners):
        product = product + dot(left[...], window_of(g, core, inner, first, cols))
    return lambda n: (own_columns(g, product, n) * keep[pl.ds(first + n, 1), :]).astype(jnp.bfloat16)


def late_kernel(g, keep, *refs):
    crossed, wides, wide_fars = (refs[2 * n : 2 * n + 2] for n in range(3))
    total, left, square, inner = refs[6:]
    layer = layer_index()
    side, core = layer // 2, layer % 2
    half = g.size // 2

    def slab_parts(side, core, slabs, row, height):
        base = g.pair * (1 - side)
        parts = []
        for c in (0, 1):
            lo, slab = base + c * g.slab, slabs[core ^ c]
            parts.append((lo, lo + g.slab, lambda a, b, lo=lo, slab=slab: slab[
                row : row + height, (a - lo) * g.size : (b - lo) * g.size
            ]))
        return parts

    def gather(layer):
        side, core = layer // 2, layer % 2
        near = g.reached(step_of(side, NEAR_WIDE))
        tail = wide_fars[0].shape[0] - g.far * g.size
        for k, t in enumerate(g.inner_rows(side, "late")):
            if t is None:
                inner[k * g.size : (k + 1) * g.size, :] = jnp.zeros((g.size, inner.shape[1]), inner.dtype)
                continue
            if t in near:
                name, pieces, slabs, row = NEAR_WIDE, wides, crossed, (t - near[0]) * g.size
            else:
                name, pieces, slabs = FAR_WIDE, wide_fars, wide_fars
                row = tail + (t - step_of(side, FAR_WIDE) * g.rows - cross_rows(g, side)[0]) * g.size
            for q, piece in enumerate(pieces):
                at = half * (core ^ q)
                parts = message_part(g, side, name, t, piece, half)
                parts += slab_parts(side, core, slabs, row + at, half)
                parts.sort(key=lambda part: part[0])
                place_parts(g, inner, k * g.size + at, half, t, side, parts)

    for value in range(g.layers):
        pl.when(layer == value)(functools.partial(gather, value))
    row_of = square_of(g, "A", side, core, keep, [left], [inner], total[...])
    for n in range(g.group("A")[0]):
        square[n * g.size : (n + 1) * g.size, :] = row_of(n)


def sum_kernel(g, *refs):
    owns, (early, late, out, far_left, early_left, late_left) = refs[:4], refs[4:]
    side, core = layer_index() // 2, layer_index() % 2

    def fill(layer):
        side = layer // 2
        rows = group_rows(g, side, "B")
        for left, part in ((early_left, "early"), (late_left, "late"), (far_left, "far")):
            inner_rows = g.inner_rows(side, part)
            left_rows(g, left, inner_rows, rows, Slabs(g, layer, owns), rows[0], 0, g.offsets)

    for value in range(g.layers):
        pl.when(layer_index() == value)(functools.partial(fill, value))
    first, (_, cols) = group_first(g, side, "B"), g.group("B")
    out[...] = dot(early_left[...], window_of(g, core, early, first, cols))
    out[...] += dot(late_left[...], window_of(g, core, late, first, cols))


def square_kernel(g, keep, far, far_beside, total, far_left, *refs):
    square, inner = refs
    side, core = layer_index() // 2, layer_index() % 2
    half = g.size // 2

    def gather(side):
        for k, t in enumerate(g.inner_rows(side, "far")):
            for q, piece in enumerate((far, far_beside)):
                at = pl.multiple_of(k * g.size + half * (core ^ q), half)
                parts = [] if t is None else message_part(g, side, FAR_THIN, t, piece, half)
                place_parts(g, inner, at, half, t or 0, side, parts)

    for value in (0, 1):
        pl.when(side == value)(functools.partial(gather, value))
    row_of = square_of(g, "B", side, core, keep, [far_left], [inner], total[...])
    for n in range(g.group("B")[0]):
        square[n * g.size : (n + 1) * g.size, :] = row_of(n)


def band_rows(g, side, name):
    return pl.ds(pl.multiple_of(group_first(g, side, name) * g.size, 2 * g.size), g.group(name)[0] * g.size)


def block_rows(g, t):
    return pl.ds(pl.multiple_of(t * g.size, g.size), g.size)


def early_span(g, part):
    spans = []
    for side in (0, 1):
        rows, pair = (range(g.rows), side) if part == "own" else (group_rows(g, 1 - side, part), 1 - side)
        lo = rows[0] - g.reach_low + g.pair * pair
        hi = rows[-1] - g.reach_low + g.pair * (pair + 1)
        met = [k for k, t in enumerate(g.inner_rows(side, "early")) if lo <= t < hi]
        spans.append((even_down(met[0]), met[-1] + 1))
    count = even_up(max(hi - lo for lo, hi in spans))
    total = len(g.inner_rows(0, "early"))
    return [min(lo, total - count) for lo, _ in spans], count


def far_span(g, part):
    spans = []
    for side in (0, 1):
        rows = group_rows(g, 1 - side, part)
        lo = rows[0] - g.reach_low + g.pair * (1 - side)
        hi = rows[-1] - g.reach_low + g.pair * (2 - side)
        met = [k for k, t in enumerate(g.inner_rows(side, "far")) if t is not None and lo <= t < hi]
        spans.append((even_down(met[0]), met[-1] + 1) if met else (0, 0))
    count = even_up(max(hi - lo for lo, hi in spans))
    return [min(lo, g.inner_count("far") - count) for lo, _ in spans], count


def cubic_left(g, side, part, rows, band, band_first, lefts):
    pair = side if part == "own" else 1 - side
    starts, count = early_span(g, part)
    lists = [g.inner_rows(side, "early")[starts[side] : starts[side] + count]]
    if part == "own":
        lists.append(g.inner_rows(side, "late"))
    else:
        starts, count = far_span(g, part)
        lists.append(g.inner_rows(side, "far")[starts[side] : starts[side] + count])
    for dst, inner_rows in zip(lefts, lists):
        left_rows(g, dst, inner_rows, rows, band, band_first, g.pair * pair, g.pair)


def cubic_right(g, side, part, inners):
    rights = []
    for inner, span in zip(inners, (early_span, far_span)):
        if span == far_span and part == "own":
            rights.append(inner)
            continue
        starts, count = span(g, part)
        start = pl.multiple_of(by_side(side, starts) * g.size, 2 * g.size)
        rights.append(inner.at[pl.ds(start, count * g.size), :])
    return rights


def left_scratch(g, part, count):
    sizes = [early_span(g, part)[1], g.inner_count("late") if part == "own" else far_span(g, part)[1]]
    return [pltpu.VMEM((count * g.size, n * g.size), jnp.bfloat16) for n in sizes]


def cubic_kernel(g, keep, *refs):
    squares, inners, (out, band, own, *lefts) = refs[:4], refs[4:6], refs[6:]
    layer = layer_index()
    side, core = layer // 2, layer % 2
    cols = g.slab * g.size
    for n, name in enumerate("AB"):
        rows = band_rows(g, side, name)
        own[rows, :] = squares[2 * n][...]
        for q in range(2):
            column = pl.ds(pl.multiple_of((core ^ q) * cols, cols), cols)
            band[rows, column] = squares[2 * n + q][...]
    rights = cubic_right(g, side, "own", inners)
    size = (g.rows + 1) // 2
    for n, first in enumerate(range(0, g.rows, size)):
        rows = range(first, min(first + size, g.rows))
        col = even_down(first)
        width = even_up(rows[-1] + g.slab) - col
        used = lefts[2 * n : 2 * n + 2]
        for value in (0, 1):
            pl.when(side == value)(functools.partial(cubic_left, g, value, "own", rows, band, first, used))
        product = sum(
            dot(left[: len(rows) * g.size, :], window_of(g, core, right, col, width))
            for left, right in zip(used, rights)
        )
        for k, t in enumerate(rows):
            at = (t - col) * g.size
            here = slice(t * g.size, (t + 1) * g.size)
            out[here, :] = 3.0 * own[here, :].astype(jnp.float32) - 2.0 * (
                product[k * g.size : (k + 1) * g.size, at : at + cols] * keep[t : t + 1, :]
            )


def other_part(g, layer, name, squares, inners, band, lefts):
    side, core = layer // 2, layer % 2
    cols = g.slab * g.size
    _, width = g.group(name)
    for q in range(2):
        band[:, pl.ds(pl.multiple_of((core ^ q) * cols, cols), cols)] = squares[q][...]
    for value in (0, 1):
        rows = group_rows(g, 1 - value, name)
        pl.when(side == value)(functools.partial(cubic_left, g, value, name, rows, band, 0, lefts))
    first = group_first(g, 1 - side, name)
    rights = cubic_right(g, side, name, inners)
    return first, sum(
        dot(left[...], window_of(g, core, right, first, width)) for left, right in zip(lefts, rights)
    )


def slab_early(g, slab):
    side = 1 - slab // 2
    rows = group_rows(g, 1 - side, "B")
    early = g.inner_rows(side, "early")
    lo, hi = rows[0] - g.reach_low + g.slab * slab, rows[-1] - g.reach_low + g.slab * (slab + 1)
    met = [k for k, t in enumerate(early) if lo <= t < hi]
    count = even_up(len(rows) + g.slab - 1)
    return min(even_down(met[0]), len(early) - count), count


def slab_rights(g, slab, early, far, out):
    side, core = layer_index() // 2, layer_index() % 2
    _, width = g.group("B")
    first = group_first(g, 1 - side, "B")
    start, count = jnp.int32(0), slab_early(g, 0)[1]
    for value in range(g.layers):
        start = jnp.where(slab == value, slab_early(g, value)[0], start)
    far_starts, far_count = far_span(g, "B")
    split = count * g.size
    at = lambda start, count: pl.ds(pl.multiple_of(start * g.size, 2 * g.size), count * g.size)
    out[:split, :] = window_of(g, core, early.at[at(start, count), :], first, width)
    out[split:, :] = window_of(g, core, far.at[at(by_side(side, far_starts), far_count), :], first, width)


def slab_left(g, slab, square, left):
    far_starts, far_count = far_span(g, "B")

    def gather(slab):
        here = 1 - slab // 2
        start, count = slab_early(g, slab)
        inner_rows = g.inner_rows(here, "early")[start : start + count]
        inner_rows = inner_rows + g.inner_rows(here, "far")[far_starts[here] : far_starts[here] + far_count]
        left_rows(g, left, inner_rows, group_rows(g, 1 - here, "B"), square, 0, g.slab * slab, g.slab)

    for value in range(g.layers):
        pl.when(slab == value)(functools.partial(gather, value))


def other_kernel(g, keep, *refs):
    squares, inners, (partial, out, straight, beside, band, *lefts) = refs[:2], refs[2:4], refs[4:]
    first, product = other_part(g, layer_index(), "A", squares, inners, band, lefts)
    for n in range(g.group("A")[0]):
        out[n * g.size : (n + 1) * g.size, :] = partial[block_rows(g, first + n), :] - 2.0 * (
            own_columns(g, product, n) * keep[pl.ds(first + n, 1), :]
        )
    for q, right in ((2, straight), (3, beside)):
        slab_rights(g, layer_index() ^ q, *inners, right)


def slab_kernel(g, keep, square, right, partial, out, left):
    slab_left(g, layer_index() ^ 2, square, left)
    first = group_first(g, 1 - layer_index() // 2, "B")
    product = dot(left[...], right[...])
    for n in range(g.group("B")[0]):
        out[n * g.size : (n + 1) * g.size, :] = partial[block_rows(g, first + n), :] - 2.0 * (
            own_columns(g, product, n) * keep[pl.ds(first + n, 1), :]
        )


def last_kernel(g, keep, square, right, partial, done, out, rows, sems, left):
    side = layer_index() // 2
    copies = [pltpu.make_async_copy(done, out.at[band_rows(g, 1 - side, "A"), :], sems.at[0])]
    copies[0].start()
    slab_left(g, layer_index() ^ 3, square, left)
    first, count = group_first(g, 1 - side, "B"), g.group("B")[0]
    step = count // 2
    for begin in range(0, count, step):
        here = slice(begin * g.size, (begin + step) * g.size)
        part = dot(left[here, :], right[...])
        for n in range(begin, begin + step):
            value = part[(n - begin) * g.size : (n - begin + 1) * g.size, n * g.size : (n + g.slab) * g.size]
            row = slice(n * g.size, (n + 1) * g.size)
            rows[row, :] = partial[row, :] - 2.0 * (value * keep[pl.ds(first + n, 1), :])
            to = pl.ds(pl.multiple_of((first + n) * g.size, g.size), g.size)
            copies.append(pltpu.make_async_copy(rows.at[row, :], out.at[to, :], sems.at[len(copies)]))
            copies[-1].start()
    for copy in copies:
        copy.wait()


def call(kernel, out_shape, scratch, *args, after=(), placed=(), place=VMEM):
    specs = [VMEM] * len(args) + [pl.BlockSpec(memory_space=pl.ANY)] * len(after) + [HBM] * len(placed)
    return pl.pallas_call(
        kernel,
        out_shape=out_shape,
        in_specs=specs,
        out_specs=jax.tree.map(lambda _: place, out_shape),
        scratch_shapes=scratch,
        compiler_params=pltpu.CompilerParams(vmem_limit_bytes=LIMIT),
        cost_estimate=pl.CostEstimate(flops=0, bytes_accessed=0, transcendentals=0),
    )(*args, *after, *placed)


def body(density, pattern):
    layers, ring = lax.axis_size("layer"), lax.axis_size("row")
    g = Geometry(*density.shape, *pattern.shape, layers)
    rows_dev, cols = density.shape
    bf16 = functools.partial(jax.ShapeDtypeStruct, dtype=jnp.bfloat16)
    scratch = lambda *shape: pltpu.VMEM(shape, jnp.bfloat16)

    def swap(value, bit):
        return lax.ppermute(value, "layer", [(s, s ^ bit) for s in range(layers)])

    def send(value, name, keep=lambda layer, row: True):
        pairs = []
        for l in range(layers):
            step = step_of(l // 2, name)
            pairs += [
                (l * ring + r, l * ring + (r - step) % ring) for r in range(ring) if keep(l, r)
            ]
        return lax.ppermute(value, ("layer", "row"), pairs)

    half_rows, slab = rows_dev // 2, (rows_dev, cols)
    cross_shape = (g.far * g.size, cols)

    def put_after(value, *after):
        return call(pass_kernel, bf16(value.shape), [], value, after=after)

    sources = [pltpu.with_memory_space_constraint(value, pltpu.HBM) for value in (density, pattern.T)]
    masked, keep, give = call(
        functools.partial(mask_kernel, g),
        [
            bf16(slab), jax.ShapeDtypeStruct(((g.rows + 7) // 8 * 8, cols), jnp.float32),
            bf16((half_rows, cols)),
        ],
        [scratch(*slab), pltpu.VMEM(pattern.T.shape, pattern.dtype), pltpu.SemaphoreType.DMA((2,))],
        placed=sources,
    )
    thin = send(masked, NEAR_THIN)
    other = swap(masked, 2)
    beside = swap(masked, 1)
    far_shape = message_shape(g, FAR_WIDE)
    head_shape = (far_shape[0] - cross_shape[0], cols)
    wide, far_wide = call(
        functools.partial(pack_kernel, g),
        [bf16(message_shape(g, NEAR_WIDE)), bf16(head_shape)], [scratch(half_rows, 2 * cols)],
        masked, swap(give, 1),
    )
    relayed = send(wide, FAR_WIDE, lambda layer, row: row % 2 != layer // 2)
    crossed = swap(thin, 2)
    message = call(functools.partial(far_kernel, g), bf16(far_shape), [], far_wide, other, after=(thin,))
    far_wide = send(message, FAR_WIDE)
    wide = call(functools.partial(relay_kernel, g), bf16(wide.shape), [], wide, relayed, after=(message,))
    wide = lax.ppermute(wide, "row", [(r, r ^ 1) for r in range(ring)])

    early, late, far = (g.inner_count(part) * g.size for part in ("early", "late", "far"))
    (high_a, wide_a), (high_b, wide_b) = (tuple(n * g.size for n in g.group(name)) for name in "AB")
    span = g.span * g.size
    f32 = functools.partial(jax.ShapeDtypeStruct, dtype=jnp.float32)

    slabs = (masked, beside, other, swap(other, 1))
    inner_early, sum_a, late_a = call(
        functools.partial(early_kernel, g),
        [bf16((early, span)), f32((high_a, wide_a)), bf16((high_a, late))], [scratch(high_a, early)],
        *slabs, thin, swap(thin, 1),
    )
    far_beside = swap(far_wide, 1)
    far_thin = call(
        functools.partial(far_thin_kernel, g),
        bf16(message_shape(g, FAR_THIN)), [], far_wide, far_beside, after=(sum_a,),
    )
    far_thin = swap(far_thin, 2)
    pieces = [crossed, swap(crossed, 1), wide, swap(wide, 1), far_wide, far_beside]
    square_a, inner_late = call(
        functools.partial(late_kernel, g),
        [bf16((high_a, cols)), bf16((late, span))],
        [],
        keep, *pieces, sum_a, late_a,
    )
    across_a, beside_a = swap(square_a, 2), swap(square_a, 1)
    sum_b, far_b = call(
        functools.partial(sum_kernel, g),
        [f32((high_b, wide_b)), bf16((high_b, far))], [scratch(high_b, early), scratch(high_b, late)],
        *slabs, inner_early, inner_late,
    )
    square_b, inner_far = call(
        functools.partial(square_kernel, g),
        [bf16((high_b, cols)), bf16((far, span))], [],
        keep, far_thin, swap(far_thin, 1), sum_b, far_b,
    )
    across_b, beside_b = swap(square_b, 2), swap(square_b, 1)
    partial = call(
        functools.partial(cubic_kernel, g),
        f32(slab),
        [scratch(rows_dev, 2 * cols), scratch(*slab)] + 2 * left_scratch(g, "own", (g.rows + 1) // 2),
        keep, square_a, beside_a, square_b, beside_b, inner_early, inner_late,
    )
    meet = (slab_early(g, 0)[1] + far_span(g, "B")[1]) * g.size
    done, straight, next_to = call(
        functools.partial(other_kernel, g),
        [f32((high_a, cols)), bf16((meet, wide_b)), bf16((meet, wide_b))],
        [scratch(high_a, 2 * cols)] + left_scratch(g, "A", g.group("A")[0]),
        keep, across_a, swap(across_a, 1), inner_early, inner_far, partial,
    )
    across_b = put_after(across_b, done)
    left = scratch(high_b, meet)
    partial = call(
        functools.partial(slab_kernel, g), f32((high_b, cols)), [left], keep, across_b, straight, partial
    )
    return call(
        functools.partial(last_kernel, g),
        f32(slab),
        [pltpu.VMEM((high_b, cols), jnp.float32), pltpu.SemaphoreType.DMA((1 + g.group("B")[0],)), left],
        keep, swap(across_b, 1), next_to, partial, done,
        place=HBM,
    )


def solution(mesh):
    placed = (P("row", "layer"), P("row", "layer"))
    return jax.shard_map(
        body, mesh=mesh, in_specs=placed, out_specs=P("row", "layer"), check_vma=False
    )
```

```python
import functools

import jax
import jax.numpy as jnp
from jax import lax
from jax.experimental import pallas as pl
from jax.experimental.pallas import tpu as pltpu
from jax.sharding import PartitionSpec as P

VMEM = pl.BlockSpec(memory_space=pltpu.VMEM)
HBM = pl.BlockSpec(memory_space=pltpu.HBM)
LIMIT = 12 * 1024 * 1024


class Geometry:
    def __init__(self, rows_dev, slab_cols, block_rows, slab_offsets, layers):
        self.rows, self.slab = block_rows, slab_offsets
        self.size = rows_dev // block_rows
        self.layers = layers
        self.offsets = slab_offsets * layers
        self.half = self.offsets // 2
        self.pair = 2 * slab_offsets
        self.reach_low, self.reach_high = self.half, self.half - 1
        self.columns = self.pair + block_rows - 1
        self.span = even_up(self.columns)
        self.far = even_up(max(len(self.reached(step)) for step in (-2, 2)))

    def needed(self, t, side):
        lo, hi = self.pair * side - t, self.pair * side - t + self.columns
        if t < 0:
            lo = max(lo, -t)
        if t >= self.rows:
            hi = min(hi, self.offsets - (t - self.rows + 1))
        lo, hi = max(lo, 0), min(hi, self.offsets)
        return lo, max(lo, hi)

    def reached(self, step):
        first = step * self.rows
        return [
            t
            for t in range(first, first + self.rows)
            if -self.reach_low <= t < self.rows + self.reach_high
        ]

    def inner_rows(self, side, part):
        if part == "early":
            return sorted(list(range(self.rows)) + self.reached(step_of(side, NEAR_THIN)))
        rows = []
        for name in ([NEAR_WIDE, FAR_WIDE] if part == "late" else [FAR_THIN]):
            reached = self.reached(step_of(side, name))
            rows += reached + [None] * (0 if name[0] == "near" else self.far - len(reached))
        return rows

    def inner_count(self, part):
        return len(self.inner_rows(0, part))

    def group(self, name):
        first = even_up(2 * self.rows // 5)
        count = first if name == "A" else self.rows - first
        return count, even_up(count - 1 + self.slab)

    def first(self, side, name):
        return 0 if (side == 0) == (name == "A") else self.rows - self.group(name)[0]

    def layout(self, side, name):
        step = step_of(side, name)
        found = []
        for t in self.reached(step):
            lo, hi = self.needed(t, side)
            lo, hi = max(lo, self.pair * side), min(hi, self.pair * (side + 1))
            if hi > lo:
                if name[0] == "near":
                    lo, hi = even_down(lo), even_up(hi)
                found.append((hi - lo, t, lo, hi))
        found.sort(reverse=True)
        if name[0] == "far":
            places, used = {}, []
            for width, t, lo, hi in found:
                free = [n for n, taken in enumerate(used) if taken + width <= self.slab]
                slot = free[0] if free else len(used)
                used += [] if free else [0]
                places[t] = (slot, used[slot], lo, hi)
                used[slot] += width
            return places, len(used), max(used)
        slots = (len(found) + 1) // 2
        used = [0] * slots
        places = {}
        for n, (width, t, lo, hi) in enumerate(found):
            slot = n if n < slots else 2 * slots - 1 - n
            places[t] = (slot, used[slot], lo, hi)
            used[slot] += width
        return places, slots, max(used)


def even_down(n):
    return n // 2 * 2


def even_up(n):
    return (n + 1) // 2 * 2


def step_of(side, name):
    sign = 1 if (name[1] == "thin") == (side == 0) else -1
    return sign * (1 if name[0] == "near" else 2)


NEAR_WIDE, NEAR_THIN = ("near", "wide"), ("near", "thin")
FAR_WIDE, FAR_THIN = ("far", "wide"), ("far", "thin")


def message_shape(g, name):
    layouts = [g.layout(side, name) for side in (0, 1)]
    rows, cols = max(f[1] for f in layouts) * g.size // 2, max(f[2] for f in layouts) * g.size
    if name == FAR_WIDE:
        return rows + g.far * g.size, g.slab * g.size
    return rows, cols


def layer_index():
    return lax.axis_index("layer").astype(jnp.int32)


def mask_kernel(g, density_ref, pattern_ref, out_ref, keep, give, density, pattern, sems):
    copies = [
        pltpu.make_async_copy(source, target, sems.at[n])
        for n, (source, target) in enumerate(((pattern_ref, pattern), (density_ref, density)))
    ]
    for copy in copies:
        copy.start()
    copies[0].wait()
    offsets, cols = pattern.shape[0], keep.shape[1]
    block = lax.broadcasted_iota(jnp.int32, (offsets, cols), 1) // g.size
    row = lax.broadcasted_iota(jnp.int32, (offsets, cols), 0)
    spread = jnp.where(block == row, 1.0, 0.0).astype(jnp.float32)
    keep[: g.rows, :] = lax.dot_general(
        pattern[...].astype(jnp.float32), spread, (((0,), (0,)), ((), ())),
        preferred_element_type=jnp.float32,
    )
    keep[g.rows :, :] = jnp.zeros((keep.shape[0] - g.rows, cols), keep.dtype)
    copies[1].wait()
    half = g.size // 2
    for t in range(g.rows):
        rows = slice(t * g.size, (t + 1) * g.size)
        out_ref[rows, :] = density[rows, :] * keep[t : t + 1, :].astype(jnp.bfloat16)
        start = pl.multiple_of(t * g.size + half * (1 - layer_index() % 2), half)
        give[t * half : (t + 1) * half, :] = out_ref[pl.ds(start, half), :]


def cross_rows(g, side):
    rows = [t - step_of(side, FAR_WIDE) * g.rows for t in g.reached(step_of(side, FAR_WIDE))]
    count = g.far
    return min(rows[0], g.rows - count), count


def place_row(dst_ref, dst_row, dst_lo, src_ref, src_row, height, lo, hi, shift, size, limit):
    first, last = max(lo, shift), min(hi, limit + shift)
    base = dst_lo - lo
    rows = slice(dst_row, dst_row + height)
    if first >= last:
        dst_ref[rows, dst_lo * size : (hi + base) * size] = jnp.zeros(
            (height, (hi - lo) * size), dst_ref.dtype
        )
        return
    value = src_ref[src_row : src_row + height, (first - shift) * size : (last - shift) * size]
    parts = []
    if first > lo:
        parts.append(jnp.zeros((height, (first - lo) * size), dst_ref.dtype))
    parts.append(value)
    if hi > last:
        parts.append(jnp.zeros((height, (hi - last) * size), dst_ref.dtype))
    if len(parts) > 1:
        value = jnp.concatenate(parts, axis=1)
    dst_ref[rows, dst_lo * size : (hi + base) * size] = value


def pack(g, side, name, source, row_of, lead, height, out):
    places, slots, _ = g.layout(side, name)
    filled = [0] * slots
    for t, (slot, col, lo, hi) in places.items():
        out[slot * height : (slot + 1) * height, col * g.size : (col + hi - lo) * g.size] = source[
            pl.ds(row_of(t - step_of(side, name) * g.rows), height), (lo - lead) * g.size : (hi - lead) * g.size
        ]
        filled[slot] = max(filled[slot], col + hi - lo)
    for slot, count in enumerate(filled):
        if count * g.size < out.shape[1]:
            out[slot * height : (slot + 1) * height, count * g.size :] = jnp.zeros(
                (height, out.shape[1] - count * g.size), out.dtype
            )
    if slots * height < out.shape[0] and name != FAR_WIDE:
        out[slots * height :, :] = jnp.zeros((out.shape[0] - slots * height, out.shape[1]), out.dtype)


def fill_near(g, core, own, given, near):
    half, cols = g.size // 2, g.slab * g.size
    here, there = (pl.ds(pl.multiple_of(c * cols, cols), cols) for c in (core, 1 - core))
    for t in range(g.rows):
        src = pl.multiple_of(t * g.size + half * core, half)
        near[t * half : (t + 1) * half, here] = own[pl.ds(src, half), :]
    near[:, there] = given[...]


def pack_kernel(g, own_ref, given_ref, wide, far, near):
    side, core = layer_index() // 2, layer_index() % 2
    half = g.size // 2
    fill_near(g, core, own_ref, given_ref, near)

    def fill(side):
        for name, out in ((NEAR_WIDE, wide), (FAR_WIDE, far)):
            pack(g, side, name, near, lambda row: row * half, side * g.pair, half, out)

    for value in (0, 1):
        pl.when(side == value)(functools.partial(fill, value))


def relay_kernel(g, own_ref, relayed_ref, far_ref, other_ref, after_ref, out_ref, message):
    side, row = layer_index() // 2, lax.axis_index("row")
    pick((row % 2) == side, own_ref, relayed_ref, out_ref)
    message[: far_ref.shape[0], :] = far_ref[...]

    def fill(side):
        first, count = cross_rows(g, side)
        message[far_ref.shape[0] :, :] = other_ref[first * g.size : (first + count) * g.size, :]

    for value in (0, 1):
        pl.when(side == value)(functools.partial(fill, value))


def pass_kernel(in_ref, *refs):
    refs[-1][...] = in_ref[...]


def far_thin_kernel(g, far_own, far_beside, after_ref, message):
    side, core = layer_index() // 2, layer_index() % 2
    half = g.size // 2

    def fill(side, source):
        first, count = cross_rows(g, side)
        start = source.shape[0] - (count + first) * g.size
        row_of = lambda row: pl.multiple_of(start + row * g.size + half * core, half)
        pack(g, 1 - side, FAR_THIN, source, row_of, (1 - side) * (g.offsets - g.slab), half, message)

    for value in (0, 1):
        for held, source in ((True, far_own), (False, far_beside)):
            here = jnp.logical_and(side == value, (core == 1 - value) == held)
            pl.when(here)(functools.partial(fill, value, source))


def fill_pair(g, core, slabs, pair):
    cols = g.slab * g.size
    for q, slab in enumerate(slabs):
        pair[:, pl.ds(pl.multiple_of((core ^ q) * cols, cols), cols)] = slab[...]


def place_parts(g, dst, at, height, t, side, parts):
    shift = t - g.pair * side
    values, done = [], 0
    for lo, hi, load in parts:
        lo, hi = max(lo, done - shift), min(hi, g.span - shift)
        if lo >= hi:
            continue
        if lo + shift > done:
            values.append(jnp.zeros((height, (lo + shift - done) * g.size), dst.dtype))
        values.append(load(lo, hi))
        done = hi + shift
    if done < g.span:
        values.append(jnp.zeros((height, (g.span - done) * g.size), dst.dtype))
    dst[pl.ds(at, height), :] = jnp.concatenate(values, axis=1) if len(values) > 1 else values[0]


def left_rows(g, dst, inner_rows, rows, band, band_first, lead, limit):
    runs = []
    for k, t in enumerate(inner_rows):
        offset = None if t is None else t - k
        if runs and runs[-1][0] == offset:
            runs[-1][2] = k + 1
        else:
            runs.append([offset, k, k + 1])
    for n, i in enumerate(rows):
        for offset, lo, hi in runs:
            shift = hi if offset is None else i - g.reach_low - offset + lead
            place_row(
                dst, n * g.size, lo, band, (band_first + n) * g.size, g.size, lo, hi, shift, g.size, limit
            )


def window_of(g, core, inner, col, cols):
    start = pl.multiple_of((core * g.slab + col) * g.size, 2 * g.size)
    return inner[:, pl.ds(start, cols * g.size)]


def dot(left, right):
    return jnp.dot(left, right, preferred_element_type=jnp.float32)


def own_columns(g, product, n):
    return product[n * g.size : (n + 1) * g.size, n * g.size : (n + g.slab) * g.size]


def by_side(side, values):
    return jnp.where(side == 0, values[0], values[1])


def group_first(g, side, name):
    return by_side(side, [g.first(value, name) for value in (0, 1)])


def message_part(g, side, name, t, piece, height):
    places, _, _ = g.layout(side, name)
    if t not in places:
        return []
    slot, col, lo, hi = places[t]
    rows = slice(slot * height, (slot + 1) * height)
    return [(lo, hi, lambda a, b: piece[rows, (col + a - lo) * g.size : (col + b - lo) * g.size])]


def pair_part(g, pair_index, ref, row, height):
    base = g.pair * pair_index
    return (
        base,
        base + g.pair,
        lambda a, b: ref[pl.ds(row, height), (a - base) * g.size : (b - base) * g.size],
    )


def pick(condition, first, second, out):
    pl.when(condition)(lambda: out.__setitem__(..., first[...]))
    pl.when(jnp.logical_not(condition))(lambda: out.__setitem__(..., second[...]))


def group_rows(g, side, name):
    first = g.first(side, name)
    return range(first, first + g.group(name)[0])


class Slabs:
    def __init__(self, g, layer, slabs):
        self.width, self.slabs, self.layer = g.slab * g.size, slabs, layer

    def __getitem__(self, at):
        rows, cols = at
        found = []
        for place in range(len(self.slabs)):
            lo, hi = max(cols.start, place * self.width), min(cols.stop, (place + 1) * self.width)
            if lo < hi:
                here = slice(lo - place * self.width, hi - place * self.width)
                found.append(self.slabs[self.layer ^ place][rows, here])
        return found[0] if len(found) == 1 else jnp.concatenate(found, axis=1)


def early_kernel(g, *refs):
    owns, thins = refs[:4], refs[4:6]
    inner, sum_a, late_a, left_a = refs[6:]
    side, core = layer_index() // 2, layer_index() % 2

    def gather(layer):
        side, core = layer // 2, layer % 2
        band, pair = Slabs(g, layer, owns), Slabs(g, core, thins)
        near = g.reached(step_of(side, NEAR_THIN))
        early, late = (g.inner_rows(side, part) for part in ("early", "late"))
        for k, t in enumerate(early):
            if 0 <= t < g.rows:
                source, row, lead, limit = band, t, 0, g.offsets
            else:
                source, row, lead, limit = pair, t - near[0], g.pair * side, g.pair
            rows = slice(row * g.size, (row + 1) * g.size)
            part = (lead, lead + limit, lambda a, b, source=source, rows=rows, lead=lead: source[
                rows, (a - lead) * g.size : (b - lead) * g.size
            ])
            place_parts(g, inner, k * g.size, g.size, t, side, [part])
        rows = group_rows(g, side, "A")
        for left, inner_rows in ((left_a, early), (late_a, late)):
            left_rows(g, left, inner_rows, rows, band, rows[0], 0, g.offsets)

    for value in range(g.layers):
        pl.when(layer_index() == value)(functools.partial(gather, value))
    col, (_, cols) = group_first(g, side, "A"), g.group("A")
    sum_a[...] = dot(left_a[...], window_of(g, core, inner, col, cols))


def square_of(g, name, side, core, keep, lefts, inners, product=0.0):
    first, (_, cols) = group_first(g, side, name), g.group(name)
    for left, inner in zip(lefts, inners):
        product = product + dot(left[...], window_of(g, core, inner, first, cols))
    return lambda n: (own_columns(g, product, n) * keep[pl.ds(first + n, 1), :]).astype(jnp.bfloat16)


def late_kernel(g, keep, *refs):
    crossed, wides, wide_fars = (refs[2 * n : 2 * n + 2] for n in range(3))
    total, left, square, inner = refs[6:]
    layer = layer_index()
    side, core = layer // 2, layer % 2
    half = g.size // 2

    def slab_parts(side, core, slabs, row, height):
        base = g.pair * (1 - side)
        parts = []
        for c in (0, 1):
            lo, slab = base + c * g.slab, slabs[core ^ c]
            parts.append((lo, lo + g.slab, lambda a, b, lo=lo, slab=slab: slab[
                row : row + height, (a - lo) * g.size : (b - lo) * g.size
            ]))
        return parts

    def gather(layer):
        side, core = layer // 2, layer % 2
        near = g.reached(step_of(side, NEAR_WIDE))
        tail = wide_fars[0].shape[0] - g.far * g.size
        for k, t in enumerate(g.inner_rows(side, "late")):
            if t is None:
                inner[k * g.size : (k + 1) * g.size, :] = jnp.zeros((g.size, inner.shape[1]), inner.dtype)
                continue
            if t in near:
                name, pieces, slabs, row = NEAR_WIDE, wides, crossed, (t - near[0]) * g.size
            else:
                name, pieces, slabs = FAR_WIDE, wide_fars, wide_fars
                row = tail + (t - step_of(side, FAR_WIDE) * g.rows - cross_rows(g, side)[0]) * g.size
            for q, piece in enumerate(pieces):
                at = half * (core ^ q)
                parts = message_part(g, side, name, t, piece, half)
                parts += slab_parts(side, core, slabs, row + at, half)
                parts.sort(key=lambda part: part[0])
                place_parts(g, inner, k * g.size + at, half, t, side, parts)

    for value in range(g.layers):
        pl.when(layer == value)(functools.partial(gather, value))
    row_of = square_of(g, "A", side, core, keep, [left], [inner], total[...])
    for n in range(g.group("A")[0]):
        square[n * g.size : (n + 1) * g.size, :] = row_of(n)


def sum_kernel(g, *refs):
    owns, (early, late, out, far_left, early_left, late_left) = refs[:4], refs[4:]
    side, core = layer_index() // 2, layer_index() % 2

    def fill(layer):
        side = layer // 2
        rows = group_rows(g, side, "B")
        for left, part in ((early_left, "early"), (late_left, "late"), (far_left, "far")):
            inner_rows = g.inner_rows(side, part)
            left_rows(g, left, inner_rows, rows, Slabs(g, layer, owns), rows[0], 0, g.offsets)

    for value in range(g.layers):
        pl.when(layer_index() == value)(functools.partial(fill, value))
    first, (_, cols) = group_first(g, side, "B"), g.group("B")
    out[...] = dot(early_left[...], window_of(g, core, early, first, cols))
    out[...] += dot(late_left[...], window_of(g, core, late, first, cols))


def square_kernel(g, keep, far, far_beside, total, far_left, *refs):
    square, inner = refs
    side, core = layer_index() // 2, layer_index() % 2
    half = g.size // 2

    def gather(side):
        for k, t in enumerate(g.inner_rows(side, "far")):
            for q, piece in enumerate((far, far_beside)):
                at = pl.multiple_of(k * g.size + half * (core ^ q), half)
                parts = [] if t is None else message_part(g, side, FAR_THIN, t, piece, half)
                place_parts(g, inner, at, half, t or 0, side, parts)

    for value in (0, 1):
        pl.when(side == value)(functools.partial(gather, value))
    row_of = square_of(g, "B", side, core, keep, [far_left], [inner], total[...])
    for n in range(g.group("B")[0]):
        square[n * g.size : (n + 1) * g.size, :] = row_of(n)


def band_rows(g, side, name):
    return pl.ds(pl.multiple_of(group_first(g, side, name) * g.size, 2 * g.size), g.group(name)[0] * g.size)


def block_rows(g, t):
    return pl.ds(pl.multiple_of(t * g.size, g.size), g.size)


def early_span(g, part):
    spans = []
    for side in (0, 1):
        rows, pair = (range(g.rows), side) if part == "own" else (group_rows(g, 1 - side, part), 1 - side)
        lo = rows[0] - g.reach_low + g.pair * pair
        hi = rows[-1] - g.reach_low + g.pair * (pair + 1)
        met = [k for k, t in enumerate(g.inner_rows(side, "early")) if lo <= t < hi]
        spans.append((even_down(met[0]), met[-1] + 1))
    count = even_up(max(hi - lo for lo, hi in spans))
    total = len(g.inner_rows(0, "early"))
    return [min(lo, total - count) for lo, _ in spans], count


def far_span(g, part):
    spans = []
    for side in (0, 1):
        rows = group_rows(g, 1 - side, part)
        lo = rows[0] - g.reach_low + g.pair * (1 - side)
        hi = rows[-1] - g.reach_low + g.pair * (2 - side)
        met = [k for k, t in enumerate(g.inner_rows(side, "far")) if t is not None and lo <= t < hi]
        spans.append((even_down(met[0]), met[-1] + 1) if met else (0, 0))
    count = even_up(max(hi - lo for lo, hi in spans))
    return [min(lo, g.inner_count("far") - count) for lo, _ in spans], count


def cubic_left(g, side, part, rows, band, band_first, lefts):
    pair = side if part == "own" else 1 - side
    starts, count = early_span(g, part)
    lists = [g.inner_rows(side, "early")[starts[side] : starts[side] + count]]
    if part == "own":
        lists.append(g.inner_rows(side, "late"))
    else:
        starts, count = far_span(g, part)
        lists.append(g.inner_rows(side, "far")[starts[side] : starts[side] + count])
    for dst, inner_rows in zip(lefts, lists):
        left_rows(g, dst, inner_rows, rows, band, band_first, g.pair * pair, g.pair)


def cubic_right(g, side, part, inners):
    rights = []
    for inner, span in zip(inners, (early_span, far_span)):
        if span == far_span and part == "own":
            rights.append(inner)
            continue
        starts, count = span(g, part)
        start = pl.multiple_of(by_side(side, starts) * g.size, 2 * g.size)
        rights.append(inner.at[pl.ds(start, count * g.size), :])
    return rights


def left_scratch(g, part, count):
    sizes = [early_span(g, part)[1], g.inner_count("late") if part == "own" else far_span(g, part)[1]]
    return [pltpu.VMEM((count * g.size, n * g.size), jnp.bfloat16) for n in sizes]


def cubic_kernel(g, keep, *refs):
    squares, inners, (out, band, own, *lefts) = refs[:4], refs[4:6], refs[6:]
    layer = layer_index()
    side, core = layer // 2, layer % 2
    cols = g.slab * g.size
    for n, name in enumerate("AB"):
        rows = band_rows(g, side, name)
        own[rows, :] = squares[2 * n][...]
        for q in range(2):
            column = pl.ds(pl.multiple_of((core ^ q) * cols, cols), cols)
            band[rows, column] = squares[2 * n + q][...]
    rights = cubic_right(g, side, "own", inners)
    size = (g.rows + 1) // 2
    for n, first in enumerate(range(0, g.rows, size)):
        rows = range(first, min(first + size, g.rows))
        col = even_down(first)
        width = even_up(rows[-1] + g.slab) - col
        used = lefts[2 * n : 2 * n + 2]
        for value in (0, 1):
            pl.when(side == value)(functools.partial(cubic_left, g, value, "own", rows, band, first, used))
        product = sum(
            dot(left[: len(rows) * g.size, :], window_of(g, core, right, col, width))
            for left, right in zip(used, rights)
        )
        for k, t in enumerate(rows):
            at = (t - col) * g.size
            here = slice(t * g.size, (t + 1) * g.size)
            out[here, :] = 3.0 * own[here, :].astype(jnp.float32) - 2.0 * (
                product[k * g.size : (k + 1) * g.size, at : at + cols] * keep[t : t + 1, :]
            )


def other_part(g, layer, name, squares, inners, band, lefts):
    side, core = layer // 2, layer % 2
    cols = g.slab * g.size
    _, width = g.group(name)
    for q in range(2):
        band[:, pl.ds(pl.multiple_of((core ^ q) * cols, cols), cols)] = squares[q][...]
    for value in (0, 1):
        rows = group_rows(g, 1 - value, name)
        pl.when(side == value)(functools.partial(cubic_left, g, value, name, rows, band, 0, lefts))
    first = group_first(g, 1 - side, name)
    rights = cubic_right(g, side, name, inners)
    return first, sum(
        dot(left[...], window_of(g, core, right, first, width)) for left, right in zip(lefts, rights)
    )


def slab_early(g, slab):
    side = 1 - slab // 2
    rows = group_rows(g, 1 - side, "B")
    early = g.inner_rows(side, "early")
    lo, hi = rows[0] - g.reach_low + g.slab * slab, rows[-1] - g.reach_low + g.slab * (slab + 1)
    met = [k for k, t in enumerate(early) if lo <= t < hi]
    count = even_up(len(rows) + g.slab - 1)
    return min(even_down(met[0]), len(early) - count), count


def slab_rights(g, slab, early, far, out):
    side, core = layer_index() // 2, layer_index() % 2
    _, width = g.group("B")
    first = group_first(g, 1 - side, "B")
    start, count = jnp.int32(0), slab_early(g, 0)[1]
    for value in range(g.layers):
        start = jnp.where(slab == value, slab_early(g, value)[0], start)
    far_starts, far_count = far_span(g, "B")
    split = count * g.size
    at = lambda start, count: pl.ds(pl.multiple_of(start * g.size, 2 * g.size), count * g.size)
    out[:split, :] = window_of(g, core, early.at[at(start, count), :], first, width)
    out[split:, :] = window_of(g, core, far.at[at(by_side(side, far_starts), far_count), :], first, width)


def slab_left(g, slab, square, left):
    far_starts, far_count = far_span(g, "B")

    def gather(slab):
        here = 1 - slab // 2
        start, count = slab_early(g, slab)
        inner_rows = g.inner_rows(here, "early")[start : start + count]
        inner_rows = inner_rows + g.inner_rows(here, "far")[far_starts[here] : far_starts[here] + far_count]
        left_rows(g, left, inner_rows, group_rows(g, 1 - here, "B"), square, 0, g.slab * slab, g.slab)

    for value in range(g.layers):
        pl.when(slab == value)(functools.partial(gather, value))


def other_kernel(g, keep, *refs):
    squares, inners, (partial, out, straight, beside, band, *lefts) = refs[:2], refs[2:4], refs[4:]
    first, product = other_part(g, layer_index(), "A", squares, inners, band, lefts)
    for n in range(g.group("A")[0]):
        out[n * g.size : (n + 1) * g.size, :] = partial[block_rows(g, first + n), :] - 2.0 * (
            own_columns(g, product, n) * keep[pl.ds(first + n, 1), :]
        )
    for q, right in ((2, straight), (3, beside)):
        slab_rights(g, layer_index() ^ q, *inners, right)


def slab_kernel(g, keep, square, right, partial, out, left):
    slab_left(g, layer_index() ^ 2, square, left)
    first = group_first(g, 1 - layer_index() // 2, "B")
    product = dot(left[...], right[...])
    for n in range(g.group("B")[0]):
        out[n * g.size : (n + 1) * g.size, :] = partial[block_rows(g, first + n), :] - 2.0 * (
            own_columns(g, product, n) * keep[pl.ds(first + n, 1), :]
        )


def last_kernel(g, keep, square, right, partial, done, out, rows, sems, left):
    side = layer_index() // 2
    copies = [pltpu.make_async_copy(done, out.at[band_rows(g, 1 - side, "A"), :], sems.at[0])]
    copies[0].start()
    slab_left(g, layer_index() ^ 3, square, left)
    first, count = group_first(g, 1 - side, "B"), g.group("B")[0]
    step = count // 2
    for begin in range(0, count, step):
        here = slice(begin * g.size, (begin + step) * g.size)
        part = dot(left[here, :], right[...])
        for n in range(begin, begin + step):
            value = part[(n - begin) * g.size : (n - begin + 1) * g.size, n * g.size : (n + g.slab) * g.size]
            row = slice(n * g.size, (n + 1) * g.size)
            rows[row, :] = partial[row, :] - 2.0 * (value * keep[pl.ds(first + n, 1), :])
            to = pl.ds(pl.multiple_of((first + n) * g.size, g.size), g.size)
            copies.append(pltpu.make_async_copy(rows.at[row, :], out.at[to, :], sems.at[len(copies)]))
            copies[-1].start()
    for copy in copies:
        copy.wait()


def call(kernel, out_shape, scratch, *args, after=(), placed=(), place=VMEM):
    specs = [VMEM] * len(args) + [pl.BlockSpec(memory_space=pl.ANY)] * len(after) + [HBM] * len(placed)
    return pl.pallas_call(
        kernel,
        out_shape=out_shape,
        in_specs=specs,
        out_specs=jax.tree.map(lambda _: place, out_shape),
        scratch_shapes=scratch,
        compiler_params=pltpu.CompilerParams(vmem_limit_bytes=LIMIT),
        cost_estimate=pl.CostEstimate(flops=0, bytes_accessed=0, transcendentals=0),
    )(*args, *after, *placed)


def body(density, pattern):
    layers, ring = lax.axis_size("layer"), lax.axis_size("row")
    g = Geometry(*density.shape, *pattern.shape, layers)
    rows_dev, cols = density.shape
    bf16 = functools.partial(jax.ShapeDtypeStruct, dtype=jnp.bfloat16)
    scratch = lambda *shape: pltpu.VMEM(shape, jnp.bfloat16)

    def swap(value, bit):
        return lax.ppermute(value, "layer", [(s, s ^ bit) for s in range(layers)])

    def send(value, name, keep=lambda layer, row: True):
        pairs = []
        for l in range(layers):
            step = step_of(l // 2, name)
            pairs += [
                (l * ring + r, l * ring + (r - step) % ring) for r in range(ring) if keep(l, r)
            ]
        return lax.ppermute(value, ("layer", "row"), pairs)

    half_rows, slab = rows_dev // 2, (rows_dev, cols)
    cross_shape = (g.far * g.size, cols)

    def put_after(value, *after):
        return call(pass_kernel, bf16(value.shape), [], value, after=after)

    sources = [pltpu.with_memory_space_constraint(value, pltpu.HBM) for value in (density, pattern.T)]
    masked, keep, give = call(
        functools.partial(mask_kernel, g),
        [
            bf16(slab), jax.ShapeDtypeStruct(((g.rows + 7) // 8 * 8, cols), jnp.float32),
            bf16((half_rows, cols)),
        ],
        [scratch(*slab), pltpu.VMEM(pattern.T.shape, pattern.dtype), pltpu.SemaphoreType.DMA((2,))],
        placed=sources,
    )
    thin = send(masked, NEAR_THIN)
    other = swap(masked, 2)
    beside = swap(masked, 1)
    far_shape = message_shape(g, FAR_WIDE)
    head_shape = (far_shape[0] - cross_shape[0], cols)
    wide, far_wide = call(
        functools.partial(pack_kernel, g),
        [bf16(message_shape(g, NEAR_WIDE)), bf16(head_shape)], [scratch(half_rows, 2 * cols)],
        masked, swap(give, 1),
    )
    relayed = send(wide, FAR_WIDE, lambda layer, row: row % 2 != layer // 2)
    crossed = swap(thin, 2)
    wide, far_wide = call(
        functools.partial(relay_kernel, g),
        [bf16(wide.shape), bf16(far_shape)], [], wide, relayed, far_wide, other, after=(relayed,),
    )
    wide = lax.ppermute(wide, "row", [(r, r ^ 1) for r in range(ring)])
    far_wide = send(far_wide, FAR_WIDE)

    early, late, far = (g.inner_count(part) * g.size for part in ("early", "late", "far"))
    (high_a, wide_a), (high_b, wide_b) = (tuple(n * g.size for n in g.group(name)) for name in "AB")
    span = g.span * g.size
    f32 = functools.partial(jax.ShapeDtypeStruct, dtype=jnp.float32)

    slabs = (masked, beside, other, swap(other, 1))
    inner_early, sum_a, late_a = call(
        functools.partial(early_kernel, g),
        [bf16((early, span)), f32((high_a, wide_a)), bf16((high_a, late))], [scratch(high_a, early)],
        *slabs, thin, swap(thin, 1),
    )
    far_beside = swap(far_wide, 1)
    far_thin = call(
        functools.partial(far_thin_kernel, g),
        bf16(message_shape(g, FAR_THIN)), [], far_wide, far_beside, after=(sum_a,),
    )
    far_thin = swap(far_thin, 2)
    pieces = [crossed, swap(crossed, 1), wide, swap(wide, 1), far_wide, far_beside]
    square_a, inner_late = call(
        functools.partial(late_kernel, g),
        [bf16((high_a, cols)), bf16((late, span))],
        [],
        keep, *pieces, sum_a, late_a,
    )
    across_a, beside_a = swap(square_a, 2), swap(square_a, 1)
    sum_b, far_b = call(
        functools.partial(sum_kernel, g),
        [f32((high_b, wide_b)), bf16((high_b, far))], [scratch(high_b, early), scratch(high_b, late)],
        *slabs, inner_early, inner_late,
    )
    square_b, inner_far = call(
        functools.partial(square_kernel, g),
        [bf16((high_b, cols)), bf16((far, span))], [],
        keep, far_thin, swap(far_thin, 1), sum_b, far_b,
    )
    across_b, beside_b = swap(square_b, 2), swap(square_b, 1)
    partial = call(
        functools.partial(cubic_kernel, g),
        f32(slab),
        [scratch(rows_dev, 2 * cols), scratch(*slab)] + 2 * left_scratch(g, "own", (g.rows + 1) // 2),
        keep, square_a, beside_a, square_b, beside_b, inner_early, inner_late,
    )
    meet = (slab_early(g, 0)[1] + far_span(g, "B")[1]) * g.size
    done, straight, next_to = call(
        functools.partial(other_kernel, g),
        [f32((high_a, cols)), bf16((meet, wide_b)), bf16((meet, wide_b))],
        [scratch(high_a, 2 * cols)] + left_scratch(g, "A", g.group("A")[0]),
        keep, across_a, swap(across_a, 1), inner_early, inner_far, partial,
    )
    across_b = put_after(across_b, done)
    left = scratch(high_b, meet)
    partial = call(
        functools.partial(slab_kernel, g), f32((high_b, cols)), [left], keep, across_b, straight, partial
    )
    return call(
        functools.partial(last_kernel, g),
        f32(slab),
        [pltpu.VMEM((high_b, cols), jnp.float32), pltpu.SemaphoreType.DMA((1 + g.group("B")[0],)), left],
        keep, swap(across_b, 1), next_to, partial, done,
        place=HBM,
    )


def solution(mesh):
    placed = (P("row", "layer"), P("row", "layer"))
    return jax.shard_map(
        body, mesh=mesh, in_specs=placed, out_specs=P("row", "layer"), check_vma=False
    )
```
